32 devices in a mesh: section: 2 (over core), ctx: 16 (over z, y, x).
Axes of the slice: x: 2, y: 2, z: 4, core: 2. Of those that a mesh axis runs over, the one named last changes fastest.
Arguments:
- queries: bfloat16 [2, 2048, 2560], P('section', 'ctx'), may hold values from -6 to 6
- keys: bfloat16 [2048, 512], P('ctx'), may hold values from -6 to 6
- values: bfloat16 [2048, 512], P('ctx'), may hold values from -6 to 6
- cotangent: bfloat16 [2, 2048, 2560], P('section', 'ctx'), may hold values from -6 to 6
- segment_ids: int32 [2048], P('ctx'), may hold values from 0 to 23, never falling along the last dimension, each value on 1 to 256 neighbouring positions
Outputs:
- grad_queries: bfloat16 [2, 2048, 2560], P('section', 'ctx')
- grad_keys: float32 [2048, 512], P('ctx', 'section')
- grad_values: float32 [2048, 512], P('ctx', 'section')
The draws below stay inside these ranges and needn't reach their ends.
Inputs may be any that keep to these rules, and one draw needn't show every extreme that they name: `segment_ids`: ids never fall; each document covers 1 to 256 tokens, one exactly 256.
All inputs are finite; a program needn't handle non-finite values.
Results may differ from the reference program's by a relative error of at most 0.007.
Values may be sent and summed in bfloat16 or wider, within the bound.
A program may use at most 64 MiB of HBM per device.

```python
import math
import jax
import jax.numpy as jnp
import numpy as np
from jax import lax

H = 20
G = 4
DH = 128
TOK_DEV = 128
DOC_SHARDS = 2
LAYERS = 2
TOKENS = 2048
DOC_MOST = 256
DOCS = 24


def draw_queries(key, part):
    key = jax.random.fold_in(key, 1)
    shape = (LAYERS, TOKENS, H * DH)
    base = jnp.clip(jax.random.normal(key, shape, jnp.float32), -6.0, 6.0)
    return base.astype(jnp.bfloat16)


def draw_keys(key, part):
    key = jax.random.fold_in(key, 2)
    shape = (TOKENS, G * DH)
    base = jnp.clip(jax.random.normal(key, shape, jnp.float32), -6.0, 6.0)
    return base.astype(jnp.bfloat16)


def levels(key, shape, pieces, low, largest):
    gain, own = 1.0, jax.random.fold_in(key, 6)
    for position, shards_of in pieces:
        steps = jnp.exp(jax.random.uniform(jax.random.fold_in(own, position), (shards_of,), jnp.float32, low / len(pieces), largest / len(pieces)))
        gain = gain * jnp.repeat(steps, shape[position] // shards_of).reshape([-1 if axis == position else 1 for axis in range(len(shape))])
    return gain


def profile(count, total, bound, slope):
    portions = [(1 << 20) // math.isqrt(rank ** slope) + 1 for rank in range(2, count + 1)]
    rest, holding = total - bound - (count - 1), [1] * (count - 1)
    while rest > 0:
        free = [i for i in range(count - 1) if holding[i] < bound]
        pool, left = sum([portions[i] for i in free]), rest
        for i in free:
            extra = min(bound - holding[i], max(1, left * portions[i] // pool), rest)
            holding[i] = holding[i] + extra
            rest = rest - extra
    return np.array([bound] + holding)


def uneven(stream_key, count, total, limit, slope):
    if count == 2:
        one = jax.random.randint(stream_key, (), max(1, total - limit), min(limit, total - 1) + 1)
        return jnp.stack([one, total - one])
    sizes = jnp.asarray(profile(count, total, limit, slope), jnp.int32)
    twos = (count - 1) // 2
    source_of, taker = sizes[1:1 + 2 * twos:2], sizes[2:2 + 2 * twos:2]
    room = jnp.minimum(source_of - 1, limit - taker)
    passed = jax.random.randint(jax.random.fold_in(stream_key, 1), (twos,), 0, 1 << 20) % (room + 1)
    sizes = sizes.at[1:1 + 2 * twos:2].set(source_of - passed).at[2:2 + 2 * twos:2].set(taker + passed)
    return sizes[jax.random.permutation(jax.random.fold_in(stream_key, 2), count)]


def bell_draw(key, shape, scale, bound, pieces=(), kind=jnp.bfloat16):
    result = jax.random.normal(key, shape, jnp.float32) * scale
    if len(pieces) > 0:
        result = levels(key, shape, pieces, -0.22, 0.18) * result
    return jnp.clip(result, min=-bound, max=bound).astype(kind)


def setup_inputs(seed: int = 0) -> dict:
    arg_keys = jax.random.split(jax.random.key(seed), 6)
    queries = draw_queries(jax.random.fold_in(arg_keys[5], 71), 0)
    keys = draw_keys(jax.random.fold_in(arg_keys[5], 71), 0)
    values = bell_draw(arg_keys[2], (TOKENS, G * DH), 1.0, 6.0, ((0, 16),))
    cotangent = bell_draw(arg_keys[3], (LAYERS, TOKENS, H * DH), 1.0, 6.0, ((0, 2), (1, 16)))
    segment_ids = jnp.searchsorted(jnp.cumsum(uneven(arg_keys[4], DOCS, TOKENS, DOC_MOST, 2)), jnp.arange(TOKENS), side="right").astype(jnp.int32)
    return {"queries": queries, "keys": keys, "values": values, "cotangent": cotangent, "segment_ids": segment_ids}


def by_group(rows, groups):
    count, width = rows.shape
    head_ratio = width // (groups * DH)
    return rows.reshape(count, groups, head_ratio, DH).transpose(1, 2, 0, 3).reshape(groups, head_ratio * count, DH)


def reference(queries, keys, values, cotangent, segment_ids):
    score_scale = DH ** -0.5
    head_ratio = H // G
    pad_rows = DOC_SHARDS * TOK_DEV
    window = (DOC_SHARDS + 1) * TOK_DEV
    key_pad = jnp.concatenate([jnp.zeros((pad_rows, G * DH), keys.dtype), keys], 0)
    value_pad = jnp.concatenate([jnp.zeros((pad_rows, G * DH), values.dtype), values], 0)
    seg_pad = jnp.concatenate([jnp.full((pad_rows,), -1, jnp.int32), segment_ids.astype(jnp.int32)], 0)
    zero_index = jnp.zeros((), jnp.int32)

    def layer_pass(carry, layer_data):
        query_layer, grad_layer = layer_data

        def block_pass(inner, block_index):
            key_acc, value_acc = inner
            row_start = (block_index * TOK_DEV).astype(jnp.int32)
            query_rows = by_group(lax.dynamic_slice_in_dim(query_layer, row_start, TOK_DEV, 0), G).astype(jnp.float32)
            grad_rows = by_group(lax.dynamic_slice_in_dim(grad_layer, row_start, TOK_DEV, 0), G).astype(jnp.float32)
            key_block = lax.dynamic_slice_in_dim(key_pad, row_start, window, 0)
            value_block = lax.dynamic_slice_in_dim(value_pad, row_start, window, 0)
            key_seg = lax.dynamic_slice_in_dim(seg_pad, row_start, window, 0)
            key_rows = key_block.reshape(window, G, DH).transpose(1, 0, 2).astype(jnp.float32)
            value_rows = value_block.reshape(window, G, DH).transpose(1, 0, 2).astype(jnp.float32)
            scores = jnp.einsum("grd,gkd->grk", query_rows, key_rows) * score_scale
            row_pos = row_start + jnp.tile(jnp.arange(TOK_DEV, dtype=jnp.int32), head_ratio)
            row_seg = jnp.tile(lax.dynamic_slice_in_dim(segment_ids, row_start, TOK_DEV, 0), head_ratio)
            key_pos = row_start - pad_rows + jnp.arange(window, dtype=jnp.int32)
            allowed = (row_seg[:, None] == key_seg[None, :]) & (key_pos[None, :] <= row_pos[:, None])
            row_max = jnp.max(jnp.where(allowed, scores, -jnp.inf), -1, keepdims=True)
            row_sum = jnp.sum(jnp.where(allowed, jnp.exp(scores - row_max), 0.0), -1, keepdims=True)
            log_total = row_max + jnp.log(row_sum)
            probs = jnp.where(allowed, jnp.exp(scores - log_total), 0.0)
            probs_low = lax.optimization_barrier(probs.astype(jnp.bfloat16)).astype(jnp.float32)
            output_rows = jnp.einsum("grk,gkd->grd", probs_low, value_rows)
            row_dot = jnp.sum(grad_rows * output_rows, -1, keepdims=True)
            grad_probs = jnp.einsum("grd,gkd->grk", grad_rows, value_rows)
            grad_scores = probs * (grad_probs - row_dot)
            scaled_low = lax.optimization_barrier((grad_scores * score_scale).astype(jnp.bfloat16)).astype(jnp.float32)
            grad_query = jnp.einsum("grk,gkd->grd", scaled_low, key_rows)
            grad_key = jnp.einsum("grk,grd->gkd", scaled_low, query_rows).transpose(1, 0, 2).reshape(window, G * DH)
            grad_value = jnp.einsum("grk,grd->gkd", probs_low, grad_rows).transpose(1, 0, 2).reshape(window, G * DH)
            key_acc = lax.dynamic_update_slice(key_acc, lax.dynamic_slice_in_dim(key_acc, row_start, window, 0) + grad_key, (row_start, zero_index))
            value_acc = lax.dynamic_update_slice(value_acc, lax.dynamic_slice_in_dim(value_acc, row_start, window, 0) + grad_value, (row_start, zero_index))
            query_out = grad_query.reshape(G, head_ratio, TOK_DEV, DH).transpose(2, 0, 1, 3).reshape(TOK_DEV, H * DH)
            return (key_acc, value_acc), query_out.astype(jnp.bfloat16)

        carry, query_blocks = lax.scan(block_pass, carry, jnp.arange(TOKENS // TOK_DEV, dtype=jnp.int32))
        return carry, query_blocks.reshape(TOKENS, H * DH)

    start_acc = jnp.zeros((TOKENS + pad_rows, G * DH), jnp.float32)
    (key_acc, value_acc), grad_queries = lax.scan(layer_pass, (start_acc, start_acc), (queries, cotangent))
    return grad_queries, key_acc[pad_rows:], value_acc[pad_rows:]
```

```python
import functools

import jax
import jax.numpy as jnp
from jax import lax
from jax.experimental import pallas as pl
from jax.experimental.pallas import tpu as pltpu
from jax.sharding import PartitionSpec as P

DH = 128
DOC_SHARDS = 2
LOG2E = 1.4426950408889634
MESH = pl.DeviceIdType.MESH


def shifted(shard, axis, by):
    size = lax.axis_size(axis)
    pairs = [(i, i + by) for i in range(size) if 0 <= i + by < size]
    return lax.ppermute(shard, axis, pairs)


def as_sent(shard):

    def short(part):
        return part.astype(jnp.bfloat16) if part.dtype == jnp.float32 else part

    return jax.tree.map(short, shard)


def by_group(rows, groups):
    count, width = rows.shape
    head_ratio = width // (groups * DH)
    return (
        rows.reshape(count, groups, head_ratio, DH)
        .transpose(1, 2, 0, 3)
        .reshape(groups, head_ratio * count, DH)
    )


def add_pair(first, second):
    return (first[0] + second[0], first[1] + second[1])


def on_device(queries, keys, values, cotangent, segment_ids):
    tok_rows = keys.shape[0]
    groups = keys.shape[1] // DH
    heads = queries.shape[2] // DH
    head_ratio = heads // groups
    score_scale = DH ** (-0.5)
    cycle_size = lax.axis_size("ctx")
    my_index = lax.axis_index("ctx")
    query_rows = by_group(queries[0], groups)
    grad_rows = by_group(cotangent[0], groups)
    row_pos = my_index * tok_rows + jnp.tile(jnp.arange(tok_rows, dtype=jnp.int32), head_ratio)
    row_seg = jnp.tile(segment_ids, head_ratio)
    blocks = []
    current = (keys, values, segment_ids)
    for shard_step in range(DOC_SHARDS + 1):
        if shard_step > 0:
            current = shifted((current[0], current[1], current[2]), "ctx", 1)
        key_block, value_block, key_seg = current
        key_rows = key_block.reshape(tok_rows, groups, DH).transpose(1, 0, 2)
        value_rows = value_block.reshape(tok_rows, groups, DH).transpose(1, 0, 2)
        key_pos = (my_index - shard_step) % cycle_size * tok_rows + jnp.arange(
            tok_rows, dtype=jnp.int32
        )
        allowed = (row_seg[:, None] == key_seg[None, :]) & (key_pos[None, :] <= row_pos[:, None])
        if shard_step == 0:
            is_live = jnp.array(True)
        else:
            is_live = (my_index >= shard_step) & (key_seg[-1] >= segment_ids[0])
        blocks.append((key_rows, value_rows, allowed, is_live))
    row_count = head_ratio * tok_rows
    row_max = jnp.full((groups, row_count, 1), -1e30, jnp.float32)
    row_sum = jnp.zeros((groups, row_count, 1), jnp.float32)
    kept_scores = []
    for key_rows, value_rows, allowed, is_live in blocks:

        def running_stats(key_rows=key_rows, allowed=allowed, row_max=row_max, row_sum=row_sum):
            scores = (
                jnp.einsum("grd,gkd->grk", query_rows, key_rows, preferred_element_type=jnp.float32)
                * score_scale
            )
            block_max = jnp.max(jnp.where(allowed, scores, -1e30), -1, keepdims=True)
            new_max = jnp.maximum(row_max, block_max)
            added = jnp.sum(jnp.where(allowed, jnp.exp(scores - new_max), 0.0), -1, keepdims=True)
            return (new_max, row_sum * jnp.exp(row_max - new_max) + added, scores)

        row_max, row_sum, scores = running_stats()
        kept_scores.append(scores)
    log_total = row_max + jnp.log(row_sum)

    def block_probs(scores, allowed):
        return jnp.where(allowed, jnp.exp(scores - log_total), 0.0)

    output_rows = jnp.zeros((groups, row_count, DH), jnp.float32)
    for (key_rows, value_rows, allowed, is_live), scores in zip(blocks, kept_scores):

        def output_part(scores=scores, value_rows=value_rows, allowed=allowed):
            probs_low = block_probs(scores, allowed).astype(jnp.bfloat16)
            return jnp.einsum(
                "grk,gkd->grd", probs_low, value_rows, preferred_element_type=jnp.float32
            )

        output_rows = output_rows + output_part()
    row_dot = jnp.sum(grad_rows.astype(jnp.float32) * output_rows, -1, keepdims=True)
    grad_query = jnp.zeros((groups, row_count, DH), jnp.float32)
    partials = []
    for (key_rows, value_rows, allowed, is_live), scores in zip(blocks, kept_scores):

        def backward_part(scores=scores, key_rows=key_rows, value_rows=value_rows, allowed=allowed):
            probs = block_probs(scores, allowed)
            probs_low = probs.astype(jnp.bfloat16)
            grad_probs = jnp.einsum(
                "grd,gkd->grk", grad_rows, value_rows, preferred_element_type=jnp.float32
            )
            scaled_low = (probs * (grad_probs - row_dot) * score_scale).astype(jnp.bfloat16)
            query_part = jnp.einsum(
                "grk,gkd->grd", scaled_low, key_rows, preferred_element_type=jnp.float32
            )
            key_part = jnp.einsum(
                "grk,grd->gkd", scaled_low, query_rows, preferred_element_type=jnp.float32
            )
            value_part = jnp.einsum(
                "grk,grd->gkd", probs_low, grad_rows, preferred_element_type=jnp.float32
            )
            key_flat = key_part.transpose(1, 0, 2).reshape(tok_rows, groups * DH)
            value_flat = value_part.transpose(1, 0, 2).reshape(tok_rows, groups * DH)
            return (query_part, key_flat, value_flat)

        query_part, key_flat, value_flat = backward_part()
        grad_query = grad_query + query_part
        partials.append((key_flat, value_flat))
    summed = partials[0]
    for shard_step in range(1, DOC_SHARDS + 1):
        arrived = shifted(as_sent(partials[shard_step]), "ctx", -shard_step)
        summed = add_pair(summed, arrived)
    summed = lax.psum_scatter(summed, "section", scatter_dimension=1, tiled=True)
    query_out = (
        grad_query.reshape(groups, head_ratio, tok_rows, DH)
        .transpose(2, 0, 1, 3)
        .reshape(1, tok_rows, heads * DH)
    )
    return (query_out.astype(jnp.bfloat16), summed[0], summed[1])


def dot(first, second, first_dim, second_dim):
    return lax.dot_general(
        first,
        second,
        (((first_dim,), (second_dim,)), ((), ())),
        preferred_element_type=jnp.float32,
    )


def kernel(
    cycle_size,
    q_hbm,
    k_hbm,
    v_hbm,
    g_hbm,
    seg_hbm,
    dq_hbm,
    dk_ref,
    dv_ref,
    q_buf,
    g_buf,
    k_buf,
    v_buf,
    seg_buf,
    bias,
    s_buf,
    gp_buf,
    p_buf,
    ds_buf,
    dq_buf,
    part,
    got,
    local_sem,
    pair_send,
    pair_recv,
    near_send,
    near_recv,
    part_send,
    part_recv,
):
    tok = k_hbm.shape[0]
    half = q_buf.shape[2]
    width = k_buf.shape[1]
    groups = width // DH
    ratio = half // width
    rows = ratio * tok
    shards = DOC_SHARDS + 1
    scale = DH ** (-0.5)
    me = lax.axis_index("ctx")
    core = lax.axis_index("section")
    other = 1 - core
    my_cols = pl.ds(pl.multiple_of(core * half, DH), half)
    other_cols = pl.ds(pl.multiple_of(other * half, DH), half)
    my_heads = pl.ds(pl.multiple_of(core * width, DH), width)
    steps = range(1, shards)

    def block(step):
        return slice((shards - 1 - step) * tok, (shards - step) * tok)

    def block_ds(step):
        return pl.ds((shards - 1 - step) * tok, tok)

    barrier = pltpu.get_barrier_semaphore()
    pl.semaphore_signal(barrier, inc=1, device_id={"section": other}, device_id_type=MESH)
    greeted = 1
    for step in steps:
        has_next = me + step < cycle_size
        has_prev = me >= step

        @pl.when(has_next)
        def _(step=step):
            pl.semaphore_signal(barrier, inc=1, device_id={"ctx": me + step}, device_id_type=MESH)

        @pl.when(has_prev)
        def _(step=step):
            pl.semaphore_signal(barrier, inc=1, device_id={"ctx": me - step}, device_id_type=MESH)

        greeted = greeted + has_next.astype(jnp.int32) + has_prev.astype(jnp.int32)

    local = [
        pltpu.make_async_copy(source, target, local_sem.at[i])
        for i, (source, target) in enumerate(
            (
                (k_hbm.at[:, my_heads], k_buf.at[block_ds(0), :]),
                (q_hbm.at[0, :, my_cols], q_buf.at[0]),
                (v_hbm.at[:, my_heads], v_buf.at[block_ds(0), :]),
                (g_hbm.at[0, :, my_cols], g_buf.at[0]),
                (seg_hbm, seg_buf.at[0]),
            )
        )
    ]
    for copy in local:
        copy.start()
    for step in steps:

        @pl.when(me < step)
        def _(step=step):
            k_buf[block(step), :] = jnp.zeros((tok, width), jnp.bfloat16)
            v_buf[block(step), :] = jnp.zeros((tok, width), jnp.bfloat16)
            seg_buf[step] = jnp.full((1, tok), -1, jnp.int32)

    pl.semaphore_wait(barrier, greeted)

    def near_copies(step):
        at = step - 1
        pairs = (
            (seg_hbm, seg_buf.at[step]),
            (k_hbm.at[:, my_heads], k_buf.at[block_ds(step), :]),
            (v_hbm.at[:, my_heads], v_buf.at[block_ds(step), :]),
        )
        return [
            pltpu.make_async_remote_copy(
                src_ref=source,
                dst_ref=target,
                send_sem=near_send.at[at, i],
                recv_sem=near_recv.at[at, i],
                device_id={"ctx": me + step},
                device_id_type=MESH,
            )
            for i, (source, target) in enumerate(pairs)
        ]

    near = {step: near_copies(step) for step in steps}
    for step in reversed(steps):

        @pl.when(me + step < cycle_size)
        def _(step=step):
            for copy in near[step]:
                copy.start()

    def pair_copy(source, target, at):
        return pltpu.make_async_remote_copy(
            src_ref=source,
            dst_ref=target,
            send_sem=pair_send.at[at],
            recv_sem=pair_recv.at[at],
            device_id={"section": other},
            device_id_type=MESH,
        )

    pair = [
        pair_copy(q_hbm.at[0, :, other_cols], q_buf.at[1], 0),
        pair_copy(g_hbm.at[0, :, other_cols], g_buf.at[1], 1),
    ]
    for copy in pair:
        copy.start()

    def head_cols(group, head):
        start = (group * ratio + head) * DH
        return slice(start, start + DH)

    def stacked(buf, slot, group):
        return jnp.concatenate([buf[slot, :, head_cols(group, h)] for h in range(ratio)], 0)

    def products(step, slot):
        for group in range(groups):
            cols = slice(group * DH, (group + 1) * DH)
            s_buf[group, slot, block(step), :] = dot(
                k_buf[block(step), cols], stacked(q_buf, slot, group), 1, 1
            )
            gp_buf[group, slot, block(step), :] = dot(
                v_buf[block(step), cols], stacked(g_buf, slot, group), 1, 1
            )

    def mask(step):
        key_seg = jnp.broadcast_to(seg_buf[step].astype(jnp.float32), (tok, tok)).T
        row_seg = seg_buf[0].astype(jnp.float32)
        allowed = key_seg == row_seg
        if step == 0:
            key_at = lax.broadcasted_iota(jnp.int32, (tok, tok), 0)
            row_at = lax.broadcasted_iota(jnp.int32, (tok, tok), 1)
            allowed = allowed & (key_at <= row_at)
        bias[block(step), :] = jnp.where(allowed, 0.0, -1e30)

    for copy in local:
        copy.wait()
    mask(0)
    products(0, 0)
    for copy in pair:
        copy.wait_recv()
    products(0, 1)
    for step in steps:

        @pl.when(me >= step)
        def _(step=step):
            for copy in near[step]:
                copy.wait_recv()

        mask(step)
        products(step, 0)
        products(step, 1)

    for group in range(groups):
        for slot in range(2):
            for head in range(ratio):
                cols = slice(head * tok, (head + 1) * tok)
                scores = s_buf[group, slot, :, cols] * (scale * LOG2E) + bias[...]
                exps = jnp.exp2(scores - jnp.max(scores, 0, keepdims=True))
                grad_probs = gp_buf[group, slot, :, cols]
                inverse = 1.0 / jnp.sum(exps, 0, keepdims=True)
                probs = exps * inverse
                row_dot = jnp.sum(probs * grad_probs, 0, keepdims=True)
                scaled = probs * (grad_probs - row_dot) * scale
                at = slice(slot * rows + head * tok, slot * rows + (head + 1) * tok)
                p_buf[group, :, at] = probs.astype(jnp.bfloat16)
                ds_buf[group, :, at] = scaled.astype(jnp.bfloat16)

    def all_rows(buf, group):
        return jnp.concatenate([stacked(buf, 0, group), stacked(buf, 1, group)], 0)

    def key_value_grads(step, group):
        return (
            dot(ds_buf[group, block(step), :], all_rows(q_buf, group), 1, 0),
            dot(p_buf[group, block(step), :], all_rows(g_buf, group), 1, 0),
        )

    parts = {
        step: pltpu.make_async_remote_copy(
            src_ref=part.at[step - 1],
            dst_ref=got.at[step - 1],
            send_sem=part_send.at[step - 1],
            recv_sem=part_recv.at[step - 1],
            device_id={"ctx": me - step},
            device_id_type=MESH,
        )
        for step in steps
    }
    for step in reversed(steps):
        for group in range(groups):
            cols = slice(group * DH, (group + 1) * DH)
            grad_key, grad_value = key_value_grads(step, group)
            part[step - 1, 0, :, cols] = grad_key.astype(jnp.bfloat16)
            part[step - 1, 1, :, cols] = grad_value.astype(jnp.bfloat16)

        @pl.when(me >= step)
        def _(step=step):
            parts[step].start()

    def query_grads(slot):
        for group in range(groups):
            cols = slice(group * DH, (group + 1) * DH)
            flipped = dot(
                k_buf[:, cols], ds_buf[group, :, slot * rows : (slot + 1) * rows], 0, 0
            )
            for head in range(ratio):
                dq_buf[slot, :, head_cols(group, head)] = flipped[
                    :, head * tok : (head + 1) * tok
                ].T.astype(jnp.bfloat16)

    query_grads(1)
    query_send = pair_copy(dq_buf.at[1], dq_hbm.at[0, :, my_cols], 2)
    query_send.start()
    query_grads(0)
    query_keep = pltpu.make_async_copy(dq_buf.at[0], dq_hbm.at[0, :, my_cols], local_sem.at[0])
    query_keep.start()
    for group in range(groups):
        cols = slice(group * DH, (group + 1) * DH)
        grad_key, grad_value = key_value_grads(0, group)
        dk_ref[:, cols] = grad_key
        dv_ref[:, cols] = grad_value
    for step in steps:

        @pl.when(me + step < cycle_size)
        def _(step=step):
            parts[step].wait_recv()
            dk_ref[...] += got[step - 1, 0].astype(jnp.float32)
            dv_ref[...] += got[step - 1, 1].astype(jnp.float32)

    query_keep.wait()
    query_send.wait()
    for copy in pair:
        copy.wait_send()
    for step in steps:

        @pl.when(me + step < cycle_size)
        def _(step=step):
            for copy in near[step]:
                copy.wait_send()

        @pl.when(me >= step)
        def _(step=step):
            parts[step].wait_send()


def by_heads(cycle_size, queries, keys, values, cotangent, segment_ids):
    tok = keys.shape[0]
    half = queries.shape[2] // 2
    width = keys.shape[1] // 2
    groups = width // DH
    rows = half // groups
    rows = rows // DH * tok
    window = (DOC_SHARDS + 1) * tok
    bf16, f32 = jnp.bfloat16, jnp.float32
    anywhere = pl.BlockSpec(memory_space=pl.ANY)
    in_vmem = pl.BlockSpec(memory_space=pltpu.VMEM)
    dma = pltpu.SemaphoreType.DMA
    return pl.pallas_call(
        functools.partial(kernel, cycle_size),
        out_shape=(
            jax.ShapeDtypeStruct(queries.shape, bf16),
            jax.ShapeDtypeStruct((tok, width), f32),
            jax.ShapeDtypeStruct((tok, width), f32),
        ),
        in_specs=[anywhere] * 5,
        out_specs=(anywhere, in_vmem, in_vmem),
        scratch_shapes=[
            pltpu.VMEM((2, tok, half), bf16),
            pltpu.VMEM((2, tok, half), bf16),
            pltpu.VMEM((window, width), bf16),
            pltpu.VMEM((window, width), bf16),
            pltpu.VMEM((DOC_SHARDS + 1, 1, tok), jnp.int32),
            pltpu.VMEM((window, tok), f32),
            pltpu.VMEM((groups, 2, window, rows), f32),
            pltpu.VMEM((groups, 2, window, rows), f32),
            pltpu.VMEM((groups, window, 2 * rows), bf16),
            pltpu.VMEM((groups, window, 2 * rows), bf16),
            pltpu.VMEM((2, tok, half), bf16),
            pltpu.VMEM((DOC_SHARDS, 2, tok, width), bf16),
            pltpu.VMEM((DOC_SHARDS, 2, tok, width), bf16),
            dma((5,)),
            dma((3,)),
            dma((3,)),
            dma((DOC_SHARDS, 3)),
            dma((DOC_SHARDS, 3)),
            dma((DOC_SHARDS,)),
            dma((DOC_SHARDS,)),
        ],
        compiler_params=pltpu.CompilerParams(
            collective_id=0, has_side_effects=True, vmem_limit_bytes=48 << 20
        ),
    )(queries, keys, values, cotangent, segment_ids.reshape(1, tok))


def solution(mesh):
    placed = (
        P("section", "ctx", None),
        P("ctx", None),
        P("ctx", None),
        P("section", "ctx", None),
        P("ctx"),
    )
    cycle_size = mesh.shape["ctx"]
    pairs = mesh.shape["section"] == 2

    def step(queries, keys, values, cotangent, segment_ids):
        tok, width = keys.shape
        halves = pairs and queries.shape[0] == 1 and tok % DH == 0 and width % (2 * DH) == 0
        if halves:
            return by_heads(cycle_size, queries, keys, values, cotangent, segment_ids)
        return on_device(queries, keys, values, cotangent, segment_ids)

    return jax.shard_map(
        step,
        mesh=mesh,
        in_specs=placed,
        out_specs=(P("section", "ctx", None), P("ctx", "section"), P("ctx", "section")),
        check_vma=False,
    )
```

```python
import functools

import jax
import jax.numpy as jnp
from jax import lax
from jax.experimental import pallas as pl
from jax.experimental.pallas import tpu as pltpu
from jax.sharding import PartitionSpec as P

DH = 128
DOC_SHARDS = 2
LOG2E = 1.4426950408889634
MESH = pl.DeviceIdType.MESH
VMEM_BYTES = 63 << 20
PIECES = 4


def shifted(shard, axis, by):
    size = lax.axis_size(axis)
    pairs = [(i, i + by) for i in range(size) if 0 <= i + by < size]
    return lax.ppermute(shard, axis, pairs)


def as_sent(shard):

    def short(part):
        return part.astype(jnp.bfloat16) if part.dtype == jnp.float32 else part

    return jax.tree.map(short, shard)


def by_group(rows, groups):
    count, width = rows.shape
    head_ratio = width // (groups * DH)
    return (
        rows.reshape(count, groups, head_ratio, DH)
        .transpose(1, 2, 0, 3)
        .reshape(groups, head_ratio * count, DH)
    )


def add_pair(first, second):
    return (first[0] + second[0], first[1] + second[1])


def on_device(queries, keys, values, cotangent, segment_ids):
    tok_rows = keys.shape[0]
    groups = keys.shape[1] // DH
    heads = queries.shape[2] // DH
    head_ratio = heads // groups
    score_scale = DH ** (-0.5)
    cycle_size = lax.axis_size("ctx")
    my_index = lax.axis_index("ctx")
    query_rows = by_group(queries[0], groups)
    grad_rows = by_group(cotangent[0], groups)
    row_pos = my_index * tok_rows + jnp.tile(jnp.arange(tok_rows, dtype=jnp.int32), head_ratio)
    row_seg = jnp.tile(segment_ids, head_ratio)
    blocks = []
    current = (keys, values, segment_ids)
    for shard_step in range(DOC_SHARDS + 1):
        if shard_step > 0:
            current = shifted((current[0], current[1], current[2]), "ctx", 1)
        key_block, value_block, key_seg = current
        key_rows = key_block.reshape(tok_rows, groups, DH).transpose(1, 0, 2)
        value_rows = value_block.reshape(tok_rows, groups, DH).transpose(1, 0, 2)
        key_pos = (my_index - shard_step) % cycle_size * tok_rows + jnp.arange(
            tok_rows, dtype=jnp.int32
        )
        allowed = (row_seg[:, None] == key_seg[None, :]) & (key_pos[None, :] <= row_pos[:, None])
        if shard_step == 0:
            is_live = jnp.array(True)
        else:
            is_live = (my_index >= shard_step) & (key_seg[-1] >= segment_ids[0])
        blocks.append((key_rows, value_rows, allowed, is_live))
    row_count = head_ratio * tok_rows
    row_max = jnp.full((groups, row_count, 1), -1e30, jnp.float32)
    row_sum = jnp.zeros((groups, row_count, 1), jnp.float32)
    kept_scores = []
    for key_rows, value_rows, allowed, is_live in blocks:

        def running_stats(key_rows=key_rows, allowed=allowed, row_max=row_max, row_sum=row_sum):
            scores = (
                jnp.einsum("grd,gkd->grk", query_rows, key_rows, preferred_element_type=jnp.float32)
                * score_scale
            )
            block_max = jnp.max(jnp.where(allowed, scores, -1e30), -1, keepdims=True)
            new_max = jnp.maximum(row_max, block_max)
            added = jnp.sum(jnp.where(allowed, jnp.exp(scores - new_max), 0.0), -1, keepdims=True)
            return (new_max, row_sum * jnp.exp(row_max - new_max) + added, scores)

        row_max, row_sum, scores = running_stats()
        kept_scores.append(scores)
    log_total = row_max + jnp.log(row_sum)

    def block_probs(scores, allowed):
        return jnp.where(allowed, jnp.exp(scores - log_total), 0.0)

    output_rows = jnp.zeros((groups, row_count, DH), jnp.float32)
    for (key_rows, value_rows, allowed, is_live), scores in zip(blocks, kept_scores):

        def output_part(scores=scores, value_rows=value_rows, allowed=allowed):
            probs_low = block_probs(scores, allowed).astype(jnp.bfloat16)
            return jnp.einsum(
                "grk,gkd->grd", probs_low, value_rows, preferred_element_type=jnp.float32
            )

        output_rows = output_rows + output_part()
    row_dot = jnp.sum(grad_rows.astype(jnp.float32) * output_rows, -1, keepdims=True)
    grad_query = jnp.zeros((groups, row_count, DH), jnp.float32)
    partials = []
    for (key_rows, value_rows, allowed, is_live), scores in zip(blocks, kept_scores):

        def backward_part(scores=scores, key_rows=key_rows, value_rows=value_rows, allowed=allowed):
            probs = block_probs(scores, allowed)
            probs_low = probs.astype(jnp.bfloat16)
            grad_probs = jnp.einsum(
                "grd,gkd->grk", grad_rows, value_rows, preferred_element_type=jnp.float32
            )
            scaled_low = (probs * (grad_probs - row_dot) * score_scale).astype(jnp.bfloat16)
            query_part = jnp.einsum(
                "grk,gkd->grd", scaled_low, key_rows, preferred_element_type=jnp.float32
            )
            key_part = jnp.einsum(
                "grk,grd->gkd", scaled_low, query_rows, preferred_element_type=jnp.float32
            )
            value_part = jnp.einsum(
                "grk,grd->gkd", probs_low, grad_rows, preferred_element_type=jnp.float32
            )
            key_flat = key_part.transpose(1, 0, 2).reshape(tok_rows, groups * DH)
            value_flat = value_part.transpose(1, 0, 2).reshape(tok_rows, groups * DH)
            return (query_part, key_flat, value_flat)

        query_part, key_flat, value_flat = backward_part()
        grad_query = grad_query + query_part
        partials.append((key_flat, value_flat))
    summed = partials[0]
    for shard_step in range(1, DOC_SHARDS + 1):
        arrived = shifted(as_sent(partials[shard_step]), "ctx", -shard_step)
        summed = add_pair(summed, arrived)
    summed = lax.psum_scatter(summed, "section", scatter_dimension=1, tiled=True)
    query_out = (
        grad_query.reshape(groups, head_ratio, tok_rows, DH)
        .transpose(2, 0, 1, 3)
        .reshape(1, tok_rows, heads * DH)
    )
    return (query_out.astype(jnp.bfloat16), summed[0], summed[1])


def dot(first, second, first_dim, second_dim):
    return lax.dot_general(
        first,
        second,
        (((first_dim,), (second_dim,)), ((), ())),
        preferred_element_type=jnp.float32,
    )


def kernel(
    cycle_size,
    q_hbm,
    k_hbm,
    v_hbm,
    g_hbm,
    seg_hbm,
    dq_hbm,
    dk_ref,
    dv_ref,
    q_buf,
    g_buf,
    k_buf,
    v_buf,
    seg_buf,
    bias,
    s_buf,
    gp_buf,
    p_buf,
    ds_buf,
    dq_buf,
    part,
    got,
    local_sem,
    pair_send,
    pair_recv,
    seg_send,
    seg_recv,
    near_send,
    near_recv,
    part_send,
    part_recv,
):
    tok = k_hbm.shape[0]
    groups = k_buf.shape[0]
    share = q_buf.shape[3]
    ratio = share // DH
    rows = ratio * tok
    shards = DOC_SHARDS + 1
    scale = DH ** (-0.5)
    me = lax.axis_index("ctx")
    core = lax.axis_index("section")
    other = 1 - core
    steps = range(1, shards)

    def query_cols(owner, group):
        return pl.ds(pl.multiple_of((owner * groups + group) * share, DH), share)

    def key_cols(group):
        return pl.ds(pl.multiple_of((core * groups + group) * DH, DH), DH)

    def block(step):
        return slice((shards - 1 - step) * tok, (shards - step) * tok)

    def block_ds(step):
        return pl.ds((shards - 1 - step) * tok, tok)

    barrier = pltpu.get_barrier_semaphore()
    pl.semaphore_signal(barrier, inc=1, device_id={"section": other}, device_id_type=MESH)
    greeted = 1
    for step in steps:
        has_next = me + step < cycle_size
        has_prev = me >= step

        @pl.when(has_next)
        def _(step=step):
            pl.semaphore_signal(barrier, inc=1, device_id={"ctx": me + step}, device_id_type=MESH)

        @pl.when(has_prev)
        def _(step=step):
            pl.semaphore_signal(barrier, inc=1, device_id={"ctx": me - step}, device_id_type=MESH)

        greeted = greeted + has_next.astype(jnp.int32) + has_prev.astype(jnp.int32)

    def own_copies(group):
        pairs = (
            (k_hbm.at[:, key_cols(group)], k_buf.at[group, block_ds(0), :]),
            (q_hbm.at[0, :, query_cols(core, group)], q_buf.at[0, group]),
            (v_hbm.at[:, key_cols(group)], v_buf.at[group, block_ds(0), :]),
            (g_hbm.at[0, :, query_cols(core, group)], g_buf.at[0, group]),
        )
        return [
            pltpu.make_async_copy(source, target, local_sem.at[group, i])
            for i, (source, target) in enumerate(pairs)
        ]

    own = [own_copies(group) for group in range(groups)]
    own_seg = pltpu.make_async_copy(seg_hbm, seg_buf.at[0], local_sem.at[groups, 0])
    own_seg.start()
    for copies in own:
        for copy in copies:
            copy.start()
    for step in steps:

        @pl.when(me < step)
        def _(step=step):
            for group in range(groups):
                k_buf[group, block(step), :] = jnp.zeros((tok, DH), jnp.bfloat16)
                v_buf[group, block(step), :] = jnp.zeros((tok, DH), jnp.bfloat16)
            seg_buf[step] = jnp.full((1, tok), -1, jnp.int32)

    pl.semaphore_wait(barrier, greeted)

    def to_next(source, target, step, send, recv):
        return pltpu.make_async_remote_copy(
            src_ref=source,
            dst_ref=target,
            send_sem=send,
            recv_sem=recv,
            device_id={"ctx": me + step},
            device_id_type=MESH,
        )

    def near_copies(step, group):
        at = step - 1
        pairs = (
            (k_hbm.at[:, key_cols(group)], k_buf.at[group, block_ds(step), :]),
            (v_hbm.at[:, key_cols(group)], v_buf.at[group, block_ds(step), :]),
        )
        return [
            to_next(source, target, step, near_send.at[at, group, i], near_recv.at[at, group, i])
            for i, (source, target) in enumerate(pairs)
        ]

    near = {step: [near_copies(step, group) for group in range(groups)] for step in steps}
    near_seg = {
        step: to_next(
            seg_hbm, seg_buf.at[step], step, seg_send.at[step - 1], seg_recv.at[step - 1]
        )
        for step in steps
    }

    def pair_copy(source, target, group, at):
        return pltpu.make_async_remote_copy(
            src_ref=source,
            dst_ref=target,
            send_sem=pair_send.at[group, at],
            recv_sem=pair_recv.at[group, at],
            device_id={"section": other},
            device_id_type=MESH,
        )

    pair = [
        [
            pair_copy(q_hbm.at[0, :, query_cols(other, group)], q_buf.at[1, group], group, 0),
            pair_copy(g_hbm.at[0, :, query_cols(other, group)], g_buf.at[1, group], group, 1),
        ]
        for group in range(groups)
    ]
    for group in range(groups):
        for step in reversed(steps):

            @pl.when(me + step < cycle_size)
            def _(step=step, group=group):
                if group == 0:
                    near_seg[step].start()
                for copy in near[step][group]:
                    copy.start()

        for copy in pair[group]:
            copy.start()

    def head_cols(head):
        return slice(head * DH, (head + 1) * DH)

    def stacked(buf, slot, group):
        return jnp.concatenate([buf[slot, group, :, head_cols(h)] for h in range(ratio)], 0)

    def products(step, slot, group):
        s_buf[group, slot, block(step), :] = dot(
            k_buf[group, block(step), :], stacked(q_buf, slot, group), 1, 1
        )
        gp_buf[group, slot, block(step), :] = dot(
            v_buf[group, block(step), :], stacked(g_buf, slot, group), 1, 1
        )

    def mask(step):
        key_seg = jnp.broadcast_to(seg_buf[step].astype(jnp.float32), (tok, tok)).T
        row_seg = seg_buf[0].astype(jnp.float32)
        allowed = key_seg == row_seg
        if step == 0:
            key_at = lax.broadcasted_iota(jnp.int32, (tok, tok), 0)
            row_at = lax.broadcasted_iota(jnp.int32, (tok, tok), 1)
            allowed = allowed & (key_at <= row_at)
        bias[block(step), :] = jnp.where(allowed, 0.0, -1e30)

    def probabilities(group, slot):
        for head in range(ratio):
            cols = slice(head * tok, (head + 1) * tok)
            scores = s_buf[group, slot, :, cols] * (scale * LOG2E) + bias[...]
            exps = jnp.exp2(scores - jnp.max(scores, 0, keepdims=True))
            grad_probs = gp_buf[group, slot, :, cols]
            inverse = 1.0 / jnp.sum(exps, 0, keepdims=True)
            probs = exps * inverse
            row_dot = jnp.sum(probs * grad_probs, 0, keepdims=True)
            scaled = probs * (grad_probs - row_dot) * scale
            at = slice(slot * rows + head * tok, slot * rows + (head + 1) * tok)
            p_buf[group, :, at] = probs.astype(jnp.bfloat16)
            ds_buf[group, :, at] = scaled.astype(jnp.bfloat16)

    def all_rows(buf, group):
        return jnp.concatenate([stacked(buf, 0, group), stacked(buf, 1, group)], 0)

    def key_value_grads(step, group):
        return (
            dot(ds_buf[group, block(step), :], all_rows(q_buf, group), 1, 0),
            dot(p_buf[group, block(step), :], all_rows(g_buf, group), 1, 0),
        )

    def query_grads(group, slot):
        flipped = dot(k_buf[group], ds_buf[group, :, slot * rows : (slot + 1) * rows], 0, 0)
        for head in range(ratio):
            dq_buf[slot, group, :, head_cols(head)] = flipped[
                :, head * tok : (head + 1) * tok
            ].T.astype(jnp.bfloat16)

    def part_copy(step, group):
        return pltpu.make_async_remote_copy(
            src_ref=part.at[group, step - 1],
            dst_ref=got.at[group, step - 1],
            send_sem=part_send.at[group, step - 1],
            recv_sem=part_recv.at[group, step - 1],
            device_id={"ctx": me - step},
            device_id_type=MESH,
        )

    parts = [{step: part_copy(step, group) for step in steps} for group in range(groups)]
    query_send = [
        pair_copy(dq_buf.at[1, group], dq_hbm.at[0, :, query_cols(core, group)], group, 2)
        for group in range(groups)
    ]
    query_keep = [
        pltpu.make_async_copy(
            dq_buf.at[0, group], dq_hbm.at[0, :, query_cols(core, group)], local_sem.at[group, 4]
        )
        for group in range(groups)
    ]

    own_seg.wait()
    mask(0)
    for group in range(groups):
        for copy in own[group]:
            copy.wait()
        products(0, 0, group)
    for group in range(groups):
        for copy in pair[group]:
            copy.wait_recv()
        products(0, 1, group)
    for group in range(groups):
        for step in steps:

            @pl.when(me >= step)
            def _(step=step, group=group):
                if group == 0:
                    near_seg[step].wait_recv()
                for copy in near[step][group]:
                    copy.wait_recv()

            if group == 0:
                mask(step)
            products(step, 0, group)
            products(step, 1, group)
        probabilities(group, 0)
        probabilities(group, 1)
        for step in reversed(steps):
            grad_key, grad_value = key_value_grads(step, group)
            part[group, step - 1, 0] = grad_key.astype(jnp.bfloat16)
            part[group, step - 1, 1] = grad_value.astype(jnp.bfloat16)

            @pl.when(me >= step)
            def _(step=step, group=group):
                parts[group][step].start()

        query_grads(group, 1)
        query_send[group].start()
        query_grads(group, 0)
        query_keep[group].start()
        grad_key, grad_value = key_value_grads(0, group)
        dk_ref[:, head_cols(group)] = grad_key
        dv_ref[:, head_cols(group)] = grad_value
    for group in range(groups):
        for step in steps:

            @pl.when(me + step < cycle_size)
            def _(step=step, group=group):
                parts[group][step].wait_recv()
                dk_ref[:, head_cols(group)] += got[group, step - 1, 0].astype(jnp.float32)
                dv_ref[:, head_cols(group)] += got[group, step - 1, 1].astype(jnp.float32)

    for group in range(groups):
        query_keep[group].wait()
        query_send[group].wait()
        for copy in pair[group]:
            copy.wait_send()
        for step in steps:

            @pl.when(me + step < cycle_size)
            def _(step=step, group=group):
                if group == 0:
                    near_seg[step].wait_send()
                for copy in near[step][group]:
                    copy.wait_send()

            @pl.when(me >= step)
            def _(step=step, group=group):
                parts[group][step].wait_send()


def hand_over(dq_in, dk_in, dv_in, dq_out, dk_out, dv_out, sem):
    piece = dq_in.shape[1] // PIECES
    cuts = [pl.ds(i * piece, piece) for i in range(PIECES)]
    pairs = [(dq_in.at[:, cut], dq_out.at[:, cut]) for cut in cuts]
    pairs += [(dk_in, dk_out), (dv_in, dv_out)]
    copies = [pltpu.make_async_copy(*pair, sem.at[i]) for i, pair in enumerate(pairs)]
    for copy in copies:
        copy.start()
    for copy in copies:
        copy.wait()


def by_heads(cycle_size, queries, keys, values, cotangent, segment_ids):
    tok = keys.shape[0]
    half = queries.shape[2] // 2
    width = keys.shape[1] // 2
    groups = width // DH
    rows = half // groups
    rows = rows // DH * tok
    window = (DOC_SHARDS + 1) * tok
    bf16, f32 = jnp.bfloat16, jnp.float32
    anywhere = pl.BlockSpec(memory_space=pl.ANY)
    in_hbm = pl.BlockSpec(memory_space=pltpu.HBM)
    in_vmem = pl.BlockSpec(memory_space=pltpu.VMEM)
    dma = pltpu.SemaphoreType.DMA
    shapes = (
        jax.ShapeDtypeStruct(queries.shape, bf16),
        jax.ShapeDtypeStruct((tok, width), f32),
        jax.ShapeDtypeStruct((tok, width), f32),
    )
    grads = pl.pallas_call(
        functools.partial(kernel, cycle_size),
        out_shape=shapes,
        in_specs=[in_hbm] * 5,
        out_specs=(anywhere, in_vmem, in_vmem),
        scratch_shapes=[
            pltpu.VMEM((2, groups, tok, half // groups), bf16),
            pltpu.VMEM((2, groups, tok, half // groups), bf16),
            pltpu.VMEM((groups, window, DH), bf16),
            pltpu.VMEM((groups, window, DH), bf16),
            pltpu.VMEM((DOC_SHARDS + 1, 1, tok), jnp.int32),
            pltpu.VMEM((window, tok), f32),
            pltpu.VMEM((groups, 2, window, rows), f32),
            pltpu.VMEM((groups, 2, window, rows), f32),
            pltpu.VMEM((groups, window, 2 * rows), bf16),
            pltpu.VMEM((groups, window, 2 * rows), bf16),
            pltpu.VMEM((2, groups, tok, half // groups), bf16),
            pltpu.VMEM((groups, DOC_SHARDS, 2, tok, DH), bf16),
            pltpu.VMEM((groups, DOC_SHARDS, 2, tok, DH), bf16),
            dma((groups + 1, 5)),
            dma((groups, 3)),
            dma((groups, 3)),
            dma((DOC_SHARDS,)),
            dma((DOC_SHARDS,)),
            dma((DOC_SHARDS, groups, 2)),
            dma((DOC_SHARDS, groups, 2)),
            dma((groups, DOC_SHARDS)),
            dma((groups, DOC_SHARDS)),
        ],
        compiler_params=pltpu.CompilerParams(
            collective_id=0, has_side_effects=True, vmem_limit_bytes=VMEM_BYTES
        ),
    )(queries, keys, values, cotangent, segment_ids.reshape(1, tok))
    return pl.pallas_call(
        hand_over,
        out_shape=shapes,
        in_specs=[anywhere] * 3,
        out_specs=(in_hbm,) * 3,
        scratch_shapes=[dma((PIECES + 2,))],
        compiler_params=pltpu.CompilerParams(vmem_limit_bytes=VMEM_BYTES),
    )(*grads)


def solution(mesh):
    placed = (
        P("section", "ctx", None),
        P("ctx", None),
        P("ctx", None),
        P("section", "ctx", None),
        P("ctx"),
    )
    cycle_size = mesh.shape["ctx"]
    pairs = mesh.shape["section"] == 2

    def step(queries, keys, values, cotangent, segment_ids):
        tok, width = keys.shape
        halves = pairs and queries.shape[0] == 1 and tok % DH == 0 and width % (2 * DH) == 0
        if halves:
            return by_heads(cycle_size, queries, keys, values, cotangent, segment_ids)
        return on_device(queries, keys, values, cotangent, segment_ids)

    return jax.shard_map(
        step,
        mesh=mesh,
        in_specs=placed,
        out_specs=(P("section", "ctx", None), P("ctx", "section"), P("ctx", "section")),
        check_vma=False,
    )
```

```python
import functools

import jax
import jax.numpy as jnp
from jax import lax
from jax.experimental import pallas as pl
from jax.experimental.pallas import tpu as pltpu
from jax.sharding import PartitionSpec as P

DH = 128
DOC_SHARDS = 2
LOG2E = 1.4426950408889634
MESH = pl.DeviceIdType.MESH
VMEM_BYTES = 63 << 20
PIECES = 4


def shifted(shard, axis, by):
    size = lax.axis_size(axis)
    pairs = [(i, i + by) for i in range(size) if 0 <= i + by < size]
    return lax.ppermute(shard, axis, pairs)


def as_sent(shard):

    def short(part):
        return part.astype(jnp.bfloat16) if part.dtype == jnp.float32 else part

    return jax.tree.map(short, shard)


def by_group(rows, groups):
    count, width = rows.shape
    head_ratio = width // (groups * DH)
    return (
        rows.reshape(count, groups, head_ratio, DH)
        .transpose(1, 2, 0, 3)
        .reshape(groups, head_ratio * count, DH)
    )


def add_pair(first, second):
    return (first[0] + second[0], first[1] + second[1])


def on_device(queries, keys, values, cotangent, segment_ids):
    tok_rows = keys.shape[0]
    groups = keys.shape[1] // DH
    heads = queries.shape[2] // DH
    head_ratio = heads // groups
    score_scale = DH ** (-0.5)
    cycle_size = lax.axis_size("ctx")
    my_index = lax.axis_index("ctx")
    query_rows = by_group(queries[0], groups)
    grad_rows = by_group(cotangent[0], groups)
    row_pos = my_index * tok_rows + jnp.tile(jnp.arange(tok_rows, dtype=jnp.int32), head_ratio)
    row_seg = jnp.tile(segment_ids, head_ratio)
    blocks = []
    current = (keys, values, segment_ids)
    for shard_step in range(DOC_SHARDS + 1):
        if shard_step > 0:
            current = shifted((current[0], current[1], current[2]), "ctx", 1)
        key_block, value_block, key_seg = current
        key_rows = key_block.reshape(tok_rows, groups, DH).transpose(1, 0, 2)
        value_rows = value_block.reshape(tok_rows, groups, DH).transpose(1, 0, 2)
        key_pos = (my_index - shard_step) % cycle_size * tok_rows + jnp.arange(
            tok_rows, dtype=jnp.int32
        )
        allowed = (row_seg[:, None] == key_seg[None, :]) & (key_pos[None, :] <= row_pos[:, None])
        if shard_step == 0:
            is_live = jnp.array(True)
        else:
            is_live = (my_index >= shard_step) & (key_seg[-1] >= segment_ids[0])
        blocks.append((key_rows, value_rows, allowed, is_live))
    row_count = head_ratio * tok_rows
    row_max = jnp.full((groups, row_count, 1), -1e30, jnp.float32)
    row_sum = jnp.zeros((groups, row_count, 1), jnp.float32)
    kept_scores = []
    for key_rows, value_rows, allowed, is_live in blocks:

        def running_stats(key_rows=key_rows, allowed=allowed, row_max=row_max, row_sum=row_sum):
            scores = (
                jnp.einsum("grd,gkd->grk", query_rows, key_rows, preferred_element_type=jnp.float32)
                * score_scale
            )
            block_max = jnp.max(jnp.where(allowed, scores, -1e30), -1, keepdims=True)
            new_max = jnp.maximum(row_max, block_max)
            added = jnp.sum(jnp.where(allowed, jnp.exp(scores - new_max), 0.0), -1, keepdims=True)
            return (new_max, row_sum * jnp.exp(row_max - new_max) + added, scores)

        row_max, row_sum, scores = running_stats()
        kept_scores.append(scores)
    log_total = row_max + jnp.log(row_sum)

    def block_probs(scores, allowed):
        return jnp.where(allowed, jnp.exp(scores - log_total), 0.0)

    output_rows = jnp.zeros((groups, row_count, DH), jnp.float32)
    for (key_rows, value_rows, allowed, is_live), scores in zip(blocks, kept_scores):

        def output_part(scores=scores, value_rows=value_rows, allowed=allowed):
            probs_low = block_probs(scores, allowed).astype(jnp.bfloat16)
            return jnp.einsum(
                "grk,gkd->grd", probs_low, value_rows, preferred_element_type=jnp.float32
            )

        output_rows = output_rows + output_part()
    row_dot = jnp.sum(grad_rows.astype(jnp.float32) * output_rows, -1, keepdims=True)
    grad_query = jnp.zeros((groups, row_count, DH), jnp.float32)
    partials = []
    for (key_rows, value_rows, allowed, is_live), scores in zip(blocks, kept_scores):

        def backward_part(scores=scores, key_rows=key_rows, value_rows=value_rows, allowed=allowed):
            probs = block_probs(scores, allowed)
            probs_low = probs.astype(jnp.bfloat16)
            grad_probs = jnp.einsum(
                "grd,gkd->grk", grad_rows, value_rows, preferred_element_type=jnp.float32
            )
            scaled_low = (probs * (grad_probs - row_dot) * score_scale).astype(jnp.bfloat16)
            query_part = jnp.einsum(
                "grk,gkd->grd", scaled_low, key_rows, preferred_element_type=jnp.float32
            )
            key_part = jnp.einsum(
                "grk,grd->gkd", scaled_low, query_rows, preferred_element_type=jnp.float32
            )
            value_part = jnp.einsum(
                "grk,grd->gkd", probs_low, grad_rows, preferred_element_type=jnp.float32
            )
            key_flat = key_part.transpose(1, 0, 2).reshape(tok_rows, groups * DH)
            value_flat = value_part.transpose(1, 0, 2).reshape(tok_rows, groups * DH)
            return (query_part, key_flat, value_flat)

        query_part, key_flat, value_flat = backward_part()
        grad_query = grad_query + query_part
        partials.append((key_flat, value_flat))
    summed = partials[0]
    for shard_step in range(1, DOC_SHARDS + 1):
        arrived = shifted(as_sent(partials[shard_step]), "ctx", -shard_step)
        summed = add_pair(summed, arrived)
    summed = lax.psum_scatter(summed, "section", scatter_dimension=1, tiled=True)
    query_out = (
        grad_query.reshape(groups, head_ratio, tok_rows, DH)
        .transpose(2, 0, 1, 3)
        .reshape(1, tok_rows, heads * DH)
    )
    return (query_out.astype(jnp.bfloat16), summed[0], summed[1])


def dot(first, second, first_dim, second_dim):
    return lax.dot_general(
        first,
        second,
        (((first_dim,), (second_dim,)), ((), ())),
        preferred_element_type=jnp.float32,
    )


def kernel(
    cycle_size,
    q_hbm,
    k_hbm,
    v_hbm,
    g_hbm,
    seg_hbm,
    dq_hbm,
    dk_ref,
    dv_ref,
    q_buf,
    g_buf,
    k_buf,
    v_buf,
    seg_buf,
    bias,
    s_buf,
    gp_buf,
    p_buf,
    ds_buf,
    dq_buf,
    part,
    got,
    local_sem,
    pair_send,
    pair_recv,
    seg_send,
    seg_recv,
    near_send,
    near_recv,
    part_send,
    part_recv,
):
    tok = k_hbm.shape[0]
    groups = k_buf.shape[0]
    share = q_buf.shape[3]
    ratio = share // DH
    rows = ratio * tok
    shards = DOC_SHARDS + 1
    scale = DH ** (-0.5)
    me = lax.axis_index("ctx")
    core = lax.axis_index("section")
    other = 1 - core
    steps = range(1, shards)

    def query_cols(owner, group):
        return pl.ds(pl.multiple_of((owner * groups + group) * share, DH), share)

    def key_cols(group):
        return pl.ds(pl.multiple_of((core * groups + group) * DH, DH), DH)

    def block(step):
        return slice((shards - 1 - step) * tok, (shards - step) * tok)

    def block_ds(step):
        return pl.ds((shards - 1 - step) * tok, tok)

    barrier = pltpu.get_barrier_semaphore()
    pl.semaphore_signal(barrier, inc=1, device_id={"section": other}, device_id_type=MESH)
    greeted = 1
    for step in steps:
        has_next = me + step < cycle_size
        has_prev = me >= step

        @pl.when(has_next)
        def _(step=step):
            pl.semaphore_signal(barrier, inc=1, device_id={"ctx": me + step}, device_id_type=MESH)

        @pl.when(has_prev)
        def _(step=step):
            pl.semaphore_signal(barrier, inc=1, device_id={"ctx": me - step}, device_id_type=MESH)

        greeted = greeted + has_next.astype(jnp.int32) + has_prev.astype(jnp.int32)

    def own_copies(group):
        pairs = (
            (k_hbm.at[:, key_cols(group)], k_buf.at[group, block_ds(0), :]),
            (q_hbm.at[0, :, query_cols(core, group)], q_buf.at[0, group]),
            (v_hbm.at[:, key_cols(group)], v_buf.at[group, block_ds(0), :]),
            (g_hbm.at[0, :, query_cols(core, group)], g_buf.at[0, group]),
        )
        return [
            pltpu.make_async_copy(source, target, local_sem.at[group, i])
            for i, (source, target) in enumerate(pairs)
        ]

    own = [own_copies(group) for group in range(groups)]
    own_seg = pltpu.make_async_copy(seg_hbm, seg_buf.at[0], local_sem.at[groups, 0])
    own_seg.start()
    for copies in own:
        for copy in copies:
            copy.start()
    for step in steps:

        @pl.when(me < step)
        def _(step=step):
            for group in range(groups):
                k_buf[group, block(step), :] = jnp.zeros((tok, DH), jnp.bfloat16)
                v_buf[group, block(step), :] = jnp.zeros((tok, DH), jnp.bfloat16)
            seg_buf[step] = jnp.full((1, tok), -1, jnp.int32)

    pl.semaphore_wait(barrier, greeted)

    def to_next(source, target, step, send, recv):
        return pltpu.make_async_remote_copy(
            src_ref=source,
            dst_ref=target,
            send_sem=send,
            recv_sem=recv,
            device_id={"ctx": me + step},
            device_id_type=MESH,
        )

    def near_copies(step, group):
        at = step - 1
        pairs = (
            (k_hbm.at[:, key_cols(group)], k_buf.at[group, block_ds(step), :]),
            (v_hbm.at[:, key_cols(group)], v_buf.at[group, block_ds(step), :]),
        )
        return [
            to_next(source, target, step, near_send.at[at, group, i], near_recv.at[at, group, i])
            for i, (source, target) in enumerate(pairs)
        ]

    near = {step: [near_copies(step, group) for group in range(groups)] for step in steps}
    near_seg = {
        step: to_next(
            seg_hbm, seg_buf.at[step], step, seg_send.at[step - 1], seg_recv.at[step - 1]
        )
        for step in steps
    }

    def pair_copy(source, target, group, at):
        return pltpu.make_async_remote_copy(
            src_ref=source,
            dst_ref=target,
            send_sem=pair_send.at[group, at],
            recv_sem=pair_recv.at[group, at],
            device_id={"section": other},
            device_id_type=MESH,
        )

    pair = [
        [
            pair_copy(q_hbm.at[0, :, query_cols(other, group)], q_buf.at[1, group], group, 0),
            pair_copy(g_hbm.at[0, :, query_cols(other, group)], g_buf.at[1, group], group, 1),
        ]
        for group in range(groups)
    ]
    for group in range(groups):
        for step in reversed(steps):

            @pl.when(me + step < cycle_size)
            def _(step=step, group=group):
                if group == 0:
                    near_seg[step].start()
                for copy in near[step][group]:
                    copy.start()

        for copy in pair[group]:
            copy.start()

    def head_cols(head):
        return slice(head * DH, (head + 1) * DH)

    def stacked(buf, slot, group):
        return jnp.concatenate([buf[slot, group, :, head_cols(h)] for h in range(ratio)], 0)

    def products(step, slot, group):
        s_buf[group, slot, block(step), :] = dot(
            k_buf[group, block(step), :], stacked(q_buf, slot, group), 1, 1
        )
        gp_buf[group, slot, block(step), :] = dot(
            v_buf[group, block(step), :], stacked(g_buf, slot, group), 1, 1
        )

    def mask(step):
        key_seg = jnp.broadcast_to(seg_buf[step].astype(jnp.float32), (tok, tok)).T
        row_seg = seg_buf[0].astype(jnp.float32)
        allowed = key_seg == row_seg
        if step == 0:
            key_at = lax.broadcasted_iota(jnp.int32, (tok, tok), 0)
            row_at = lax.broadcasted_iota(jnp.int32, (tok, tok), 1)
            allowed = allowed & (key_at <= row_at)
        bias[block(step), :] = jnp.where(allowed, 0.0, -1e30)

    def probabilities(group, slot):
        for head in range(ratio):
            cols = slice(head * tok, (head + 1) * tok)
            scores = s_buf[group, slot, :, cols] * (scale * LOG2E) + bias[...]
            exps = jnp.exp2(scores - jnp.max(scores, 0, keepdims=True))
            grad_probs = gp_buf[group, slot, :, cols]
            inverse = 1.0 / jnp.sum(exps, 0, keepdims=True)
            probs = exps * inverse
            row_dot = jnp.sum(probs * grad_probs, 0, keepdims=True)
            scaled = probs * (grad_probs - row_dot) * scale
            at = slice(slot * rows + head * tok, slot * rows + (head + 1) * tok)
            p_buf[group, :, at] = probs.astype(jnp.bfloat16)
            ds_buf[group, :, at] = scaled.astype(jnp.bfloat16)

    def all_rows(buf, group):
        return jnp.concatenate([stacked(buf, 0, group), stacked(buf, 1, group)], 0)

    def key_value_grads(step, group):
        return (
            dot(ds_buf[group, block(step), :], all_rows(q_buf, group), 1, 0),
            dot(p_buf[group, block(step), :], all_rows(g_buf, group), 1, 0),
        )

    def query_grads(group, slot):
        flipped = dot(k_buf[group], ds_buf[group, :, slot * rows : (slot + 1) * rows], 0, 0)
        for head in range(ratio):
            dq_buf[slot, group, :, head_cols(head)] = flipped[
                :, head * tok : (head + 1) * tok
            ].T.astype(jnp.bfloat16)

    def part_copy(step, group):
        return pltpu.make_async_remote_copy(
            src_ref=part.at[group, step - 1],
            dst_ref=got.at[group, step - 1],
            send_sem=part_send.at[group, step - 1],
            recv_sem=part_recv.at[group, step - 1],
            device_id={"ctx": me - step},
            device_id_type=MESH,
        )

    parts = [{step: part_copy(step, group) for step in steps} for group in range(groups)]
    query_send = [
        pair_copy(dq_buf.at[1, group], dq_hbm.at[0, :, query_cols(core, group)], group, 2)
        for group in range(groups)
    ]
    query_keep = [
        pltpu.make_async_copy(
            dq_buf.at[0, group], dq_hbm.at[0, :, query_cols(core, group)], local_sem.at[group, 4]
        )
        for group in range(groups)
    ]

    own_seg.wait()
    mask(0)
    for group in range(groups):
        for copy in own[group]:
            copy.wait()
        products(0, 0, group)
    for group in range(groups):
        for copy in pair[group]:
            copy.wait_recv()
        products(0, 1, group)
    for group in range(groups):
        for step in steps:

            @pl.when(me >= step)
            def _(step=step, group=group):
                if group == 0:
                    near_seg[step].wait_recv()
                for copy in near[step][group]:
                    copy.wait_recv()

            if group == 0:
                mask(step)
            products(step, 0, group)
            products(step, 1, group)
        probabilities(group, 0)
        probabilities(group, 1)
        for step in reversed(steps):
            grad_key, grad_value = key_value_grads(step, group)
            part[group, step - 1, 0] = grad_key.astype(jnp.bfloat16)
            part[group, step - 1, 1] = grad_value.astype(jnp.bfloat16)

            @pl.when(me >= step)
            def _(step=step, group=group):
                parts[group][step].start()

        query_grads(group, 1)
        query_send[group].start()
        query_grads(group, 0)
        query_keep[group].start()
        grad_key, grad_value = key_value_grads(0, group)
        dk_ref[:, head_cols(group)] = grad_key
        dv_ref[:, head_cols(group)] = grad_value
    for group in range(groups):
        for step in steps:

            @pl.when(me + step < cycle_size)
            def _(step=step, group=group):
                parts[group][step].wait_recv()
                dk_ref[:, head_cols(group)] += got[group, step - 1, 0].astype(jnp.float32)
                dv_ref[:, head_cols(group)] += got[group, step - 1, 1].astype(jnp.float32)

    for group in range(groups):
        query_keep[group].wait()
        query_send[group].wait()
        for copy in pair[group]:
            copy.wait_send()
        for step in steps:

            @pl.when(me + step < cycle_size)
            def _(step=step, group=group):
                if group == 0:
                    near_seg[step].wait_send()
                for copy in near[step][group]:
                    copy.wait_send()

            @pl.when(me >= step)
            def _(step=step, group=group):
                parts[group][step].wait_send()


def hand_over(dq_in, dk_in, dv_in, dq_out, dk_out, dv_out, dq_buf, dk_buf, dv_buf, sem):
    piece = dq_in.shape[1] // PIECES
    cuts = [pl.ds(i * piece, piece) for i in range(PIECES)]
    ways = [(dq_in.at[:, cut], dq_buf.at[:, cut], dq_out.at[:, cut]) for cut in cuts]
    ways += [(dk_in, dk_buf, dk_out), (dv_in, dv_buf, dv_out)]
    copies = [
        (
            pltpu.make_async_copy(source, held, sem.at[0, i]),
            pltpu.make_async_copy(held, target, sem.at[1, i]),
        )
        for i, (source, held, target) in enumerate(ways)
    ]
    for first, _ in copies:
        first.start()
    for first, second in copies:
        first.wait()
        second.start()
    for _, second in copies:
        second.wait()


def by_heads(cycle_size, queries, keys, values, cotangent, segment_ids):
    tok = keys.shape[0]
    half = queries.shape[2] // 2
    width = keys.shape[1] // 2
    groups = width // DH
    rows = half // groups
    rows = rows // DH * tok
    window = (DOC_SHARDS + 1) * tok
    bf16, f32 = jnp.bfloat16, jnp.float32
    anywhere = pl.BlockSpec(memory_space=pl.ANY)
    in_hbm = pl.BlockSpec(memory_space=pltpu.HBM)
    in_vmem = pl.BlockSpec(memory_space=pltpu.VMEM)
    dma = pltpu.SemaphoreType.DMA
    shapes = (
        jax.ShapeDtypeStruct(queries.shape, bf16),
        jax.ShapeDtypeStruct((tok, width), f32),
        jax.ShapeDtypeStruct((tok, width), f32),
    )
    grads = pl.pallas_call(
        functools.partial(kernel, cycle_size),
        out_shape=shapes,
        in_specs=[in_hbm] * 5,
        out_specs=(anywhere, in_vmem, in_vmem),
        scratch_shapes=[
            pltpu.VMEM((2, groups, tok, half // groups), bf16),
            pltpu.VMEM((2, groups, tok, half // groups), bf16),
            pltpu.VMEM((groups, window, DH), bf16),
            pltpu.VMEM((groups, window, DH), bf16),
            pltpu.VMEM((DOC_SHARDS + 1, 1, tok), jnp.int32),
            pltpu.VMEM((window, tok), f32),
            pltpu.VMEM((groups, 2, window, rows), f32),
            pltpu.VMEM((groups, 2, window, rows), f32),
            pltpu.VMEM((groups, window, 2 * rows), bf16),
            pltpu.VMEM((groups, window, 2 * rows), bf16),
            pltpu.VMEM((2, groups, tok, half // groups), bf16),
            pltpu.VMEM((groups, DOC_SHARDS, 2, tok, DH), bf16),
            pltpu.VMEM((groups, DOC_SHARDS, 2, tok, DH), bf16),
            dma((groups + 1, 5)),
            dma((groups, 3)),
            dma((groups, 3)),
            dma((DOC_SHARDS,)),
            dma((DOC_SHARDS,)),
            dma((DOC_SHARDS, groups, 2)),
            dma((DOC_SHARDS, groups, 2)),
            dma((groups, DOC_SHARDS)),
            dma((groups, DOC_SHARDS)),
        ],
        compiler_params=pltpu.CompilerParams(
            collective_id=0, has_side_effects=True, vmem_limit_bytes=VMEM_BYTES
        ),
    )(queries, keys, values, cotangent, segment_ids.reshape(1, tok))
    return pl.pallas_call(
        hand_over,
        out_shape=shapes,
        in_specs=[in_hbm] * 3,
        out_specs=(in_hbm,) * 3,
        scratch_shapes=[pltpu.VMEM(shape.shape, shape.dtype) for shape in shapes]
        + [dma((2, PIECES + 2))],
        compiler_params=pltpu.CompilerParams(vmem_limit_bytes=VMEM_BYTES),
    )(*grads)


def solution(mesh):
    placed = (
        P("section", "ctx", None),
        P("ctx", None),
        P("ctx", None),
        P("section", "ctx", None),
        P("ctx"),
    )
    cycle_size = mesh.shape["ctx"]
    pairs = mesh.shape["section"] == 2

    def step(queries, keys, values, cotangent, segment_ids):
        tok, width = keys.shape
        halves = pairs and queries.shape[0] == 1 and tok % DH == 0 and width % (2 * DH) == 0
        if halves:
            return by_heads(cycle_size, queries, keys, values, cotangent, segment_ids)
        return on_device(queries, keys, values, cotangent, segment_ids)

    return jax.shard_map(
        step,
        mesh=mesh,
        in_specs=placed,
        out_specs=(P("section", "ctx", None), P("ctx", "section"), P("ctx", "section")),
        check_vma=False,
    )
```

```python
import functools

import jax
import jax.numpy as jnp
from jax import lax
from jax.experimental import pallas as pl
from jax.experimental.pallas import tpu as pltpu
from jax.sharding import PartitionSpec as P

DH = 128
DOC_SHARDS = 2
LOG2E = 1.4426950408889634
MESH = pl.DeviceIdType.MESH
VMEM_BYTES = 63 << 20
PIECES = 4


def shifted(shard, axis, by):
    size = lax.axis_size(axis)
    pairs = [(i, i + by) for i in range(size) if 0 <= i + by < size]
    return lax.ppermute(shard, axis, pairs)


def as_sent(shard):

    def short(part):
        return part.astype(jnp.bfloat16) if part.dtype == jnp.float32 else part

    return jax.tree.map(short, shard)


def by_group(rows, groups):
    count, width = rows.shape
    head_ratio = width // (groups * DH)
    return (
        rows.reshape(count, groups, head_ratio, DH)
        .transpose(1, 2, 0, 3)
        .reshape(groups, head_ratio * count, DH)
    )


def add_pair(first, second):
    return (first[0] + second[0], first[1] + second[1])


def on_device(queries, keys, values, cotangent, segment_ids):
    tok_rows = keys.shape[0]
    groups = keys.shape[1] // DH
    heads = queries.shape[2] // DH
    head_ratio = heads // groups
    score_scale = DH ** (-0.5)
    cycle_size = lax.axis_size("ctx")
    my_index = lax.axis_index("ctx")
    query_rows = by_group(queries[0], groups)
    grad_rows = by_group(cotangent[0], groups)
    row_pos = my_index * tok_rows + jnp.tile(jnp.arange(tok_rows, dtype=jnp.int32), head_ratio)
    row_seg = jnp.tile(segment_ids, head_ratio)
    blocks = []
    current = (keys, values, segment_ids)
    for shard_step in range(DOC_SHARDS + 1):
        if shard_step > 0:
            current = shifted((current[0], current[1], current[2]), "ctx", 1)
        key_block, value_block, key_seg = current
        key_rows = key_block.reshape(tok_rows, groups, DH).transpose(1, 0, 2)
        value_rows = value_block.reshape(tok_rows, groups, DH).transpose(1, 0, 2)
        key_pos = (my_index - shard_step) % cycle_size * tok_rows + jnp.arange(
            tok_rows, dtype=jnp.int32
        )
        allowed = (row_seg[:, None] == key_seg[None, :]) & (key_pos[None, :] <= row_pos[:, None])
        if shard_step == 0:
            is_live = jnp.array(True)
        else:
            is_live = (my_index >= shard_step) & (key_seg[-1] >= segment_ids[0])
        blocks.append((key_rows, value_rows, allowed, is_live))
    row_count = head_ratio * tok_rows
    row_max = jnp.full((groups, row_count, 1), -1e30, jnp.float32)
    row_sum = jnp.zeros((groups, row_count, 1), jnp.float32)
    kept_scores = []
    for key_rows, value_rows, allowed, is_live in blocks:

        def running_stats(key_rows=key_rows, allowed=allowed, row_max=row_max, row_sum=row_sum):
            scores = (
                jnp.einsum("grd,gkd->grk", query_rows, key_rows, preferred_element_type=jnp.float32)
                * score_scale
            )
            block_max = jnp.max(jnp.where(allowed, scores, -1e30), -1, keepdims=True)
            new_max = jnp.maximum(row_max, block_max)
            added = jnp.sum(jnp.where(allowed, jnp.exp(scores - new_max), 0.0), -1, keepdims=True)
            return (new_max, row_sum * jnp.exp(row_max - new_max) + added, scores)

        row_max, row_sum, scores = running_stats()
        kept_scores.append(scores)
    log_total = row_max + jnp.log(row_sum)

    def block_probs(scores, allowed):
        return jnp.where(allowed, jnp.exp(scores - log_total), 0.0)

    output_rows = jnp.zeros((groups, row_count, DH), jnp.float32)
    for (key_rows, value_rows, allowed, is_live), scores in zip(blocks, kept_scores):

        def output_part(scores=scores, value_rows=value_rows, allowed=allowed):
            probs_low = block_probs(scores, allowed).astype(jnp.bfloat16)
            return jnp.einsum(
                "grk,gkd->grd", probs_low, value_rows, preferred_element_type=jnp.float32
            )

        output_rows = output_rows + output_part()
    row_dot = jnp.sum(grad_rows.astype(jnp.float32) * output_rows, -1, keepdims=True)
    grad_query = jnp.zeros((groups, row_count, DH), jnp.float32)
    partials = []
    for (key_rows, value_rows, allowed, is_live), scores in zip(blocks, kept_scores):

        def backward_part(scores=scores, key_rows=key_rows, value_rows=value_rows, allowed=allowed):
            probs = block_probs(scores, allowed)
            probs_low = probs.astype(jnp.bfloat16)
            grad_probs = jnp.einsum(
                "grd,gkd->grk", grad_rows, value_rows, preferred_element_type=jnp.float32
            )
            scaled_low = (probs * (grad_probs - row_dot) * score_scale).astype(jnp.bfloat16)
            query_part = jnp.einsum(
                "grk,gkd->grd", scaled_low, key_rows, preferred_element_type=jnp.float32
            )
            key_part = jnp.einsum(
                "grk,grd->gkd", scaled_low, query_rows, preferred_element_type=jnp.float32
            )
            value_part = jnp.einsum(
                "grk,grd->gkd", probs_low, grad_rows, preferred_element_type=jnp.float32
            )
            key_flat = key_part.transpose(1, 0, 2).reshape(tok_rows, groups * DH)
            value_flat = value_part.transpose(1, 0, 2).reshape(tok_rows, groups * DH)
            return (query_part, key_flat, value_flat)

        query_part, key_flat, value_flat = backward_part()
        grad_query = grad_query + query_part
        partials.append((key_flat, value_flat))
    summed = partials[0]
    for shard_step in range(1, DOC_SHARDS + 1):
        arrived = shifted(as_sent(partials[shard_step]), "ctx", -shard_step)
        summed = add_pair(summed, arrived)
    summed = lax.psum_scatter(summed, "section", scatter_dimension=1, tiled=True)
    query_out = (
        grad_query.reshape(groups, head_ratio, tok_rows, DH)
        .transpose(2, 0, 1, 3)
        .reshape(1, tok_rows, heads * DH)
    )
    return (query_out.astype(jnp.bfloat16), summed[0], summed[1])


def dot(first, second, first_dim, second_dim):
    return lax.dot_general(
        first,
        second,
        (((first_dim,), (second_dim,)), ((), ())),
        preferred_element_type=jnp.float32,
    )


def kernel(
    cycle_size,
    q_hbm,
    k_hbm,
    v_hbm,
    g_hbm,
    seg_hbm,
    dq_hbm,
    dk_ref,
    dv_ref,
    q_buf,
    g_buf,
    k_buf,
    v_buf,
    seg_buf,
    bias,
    s_own,
    gp_own,
    s_buf,
    gp_buf,
    p_buf,
    ds_buf,
    dq_buf,
    part,
    got,
    local_sem,
    pair_send,
    pair_recv,
    seg_send,
    seg_recv,
    near_send,
    near_recv,
    part_send,
    part_recv,
):
    tok = k_hbm.shape[0]
    groups = k_buf.shape[0]
    share = q_buf.shape[3]
    ratio = share // DH
    rows = ratio * tok
    shards = DOC_SHARDS + 1
    scale = DH ** (-0.5)
    me = lax.axis_index("ctx")
    core = lax.axis_index("section")
    other = 1 - core
    steps = range(1, shards)

    def query_cols(owner, group):
        return pl.ds(pl.multiple_of((owner * groups + group) * share, DH), share)

    def key_cols(group):
        return pl.ds(pl.multiple_of((core * groups + group) * DH, DH), DH)

    def block(step):
        return slice((shards - 1 - step) * tok, (shards - step) * tok)

    def block_ds(step):
        return pl.ds((shards - 1 - step) * tok, tok)

    barrier = pltpu.get_barrier_semaphore()
    pl.semaphore_signal(barrier, inc=1, device_id={"section": other}, device_id_type=MESH)
    greeted = 1
    for step in steps:
        has_next = me + step < cycle_size
        has_prev = me >= step

        @pl.when(has_next)
        def _(step=step):
            pl.semaphore_signal(barrier, inc=1, device_id={"ctx": me + step}, device_id_type=MESH)

        @pl.when(has_prev)
        def _(step=step):
            pl.semaphore_signal(barrier, inc=1, device_id={"ctx": me - step}, device_id_type=MESH)

        greeted = greeted + has_next.astype(jnp.int32) + has_prev.astype(jnp.int32)

    def own_copies(group):
        pairs = (
            (k_hbm.at[:, key_cols(group)], k_buf.at[group, block_ds(0), :]),
            (q_hbm.at[0, :, query_cols(core, group)], q_buf.at[0, group]),
            (v_hbm.at[:, key_cols(group)], v_buf.at[group, block_ds(0), :]),
            (g_hbm.at[0, :, query_cols(core, group)], g_buf.at[0, group]),
        )
        return [
            pltpu.make_async_copy(source, target, local_sem.at[group, i])
            for i, (source, target) in enumerate(pairs)
        ]

    own = [own_copies(group) for group in range(groups)]
    own_seg = pltpu.make_async_copy(seg_hbm, seg_buf.at[0], local_sem.at[groups, 0])
    own_seg.start()
    for copies in own:
        for copy in copies:
            copy.start()
    for step in steps:

        @pl.when(me < step)
        def _(step=step):
            for group in range(groups):
                k_buf[group, block(step), :] = jnp.zeros((tok, DH), jnp.bfloat16)
                v_buf[group, block(step), :] = jnp.zeros((tok, DH), jnp.bfloat16)
            seg_buf[step] = jnp.full((1, tok), -1, jnp.int32)

    pl.semaphore_wait(barrier, greeted)

    def to_next(source, target, step, send, recv):
        return pltpu.make_async_remote_copy(
            src_ref=source,
            dst_ref=target,
            send_sem=send,
            recv_sem=recv,
            device_id={"ctx": me + step},
            device_id_type=MESH,
        )

    def near_copies(step, group):
        at = step - 1
        pairs = (
            (k_hbm.at[:, key_cols(group)], k_buf.at[group, block_ds(step), :]),
            (v_hbm.at[:, key_cols(group)], v_buf.at[group, block_ds(step), :]),
        )
        return [
            to_next(source, target, step, near_send.at[at, group, i], near_recv.at[at, group, i])
            for i, (source, target) in enumerate(pairs)
        ]

    near = {step: [near_copies(step, group) for group in range(groups)] for step in steps}
    near_seg = {
        step: to_next(
            seg_hbm, seg_buf.at[step], step, seg_send.at[step - 1], seg_recv.at[step - 1]
        )
        for step in steps
    }

    def pair_copy(source, target, group, at):
        return pltpu.make_async_remote_copy(
            src_ref=source,
            dst_ref=target,
            send_sem=pair_send.at[group, at],
            recv_sem=pair_recv.at[group, at],
            device_id={"section": other},
            device_id_type=MESH,
        )

    pair = [
        [
            pair_copy(q_hbm.at[0, :, query_cols(other, group)], q_buf.at[1, group], group, 0),
            pair_copy(g_hbm.at[0, :, query_cols(other, group)], g_buf.at[1, group], group, 1),
        ]
        for group in range(groups)
    ]
    for group in range(groups):
        for step in reversed(steps):

            @pl.when(me + step < cycle_size)
            def _(step=step, group=group):
                if group == 0:
                    near_seg[step].start()
                for copy in near[step][group]:
                    copy.start()

        for copy in pair[group]:
            copy.start()

    def head_cols(head):
        return slice(head * DH, (head + 1) * DH)

    def stacked(buf, slot, group):
        return jnp.concatenate([buf[slot, group, :, head_cols(h)] for h in range(ratio)], 0)

    def all_rows(buf, group):
        return jnp.concatenate([stacked(buf, 0, group), stacked(buf, 1, group)], 0)

    def own_products(slot, group):
        at = slice(slot * rows, (slot + 1) * rows)
        s_own[group, :, at] = dot(k_buf[group, block(0), :], stacked(q_buf, slot, group), 1, 1)
        gp_own[group, :, at] = dot(v_buf[group, block(0), :], stacked(g_buf, slot, group), 1, 1)

    key_at = lax.broadcasted_iota(jnp.int32, (tok, tok), 0)
    row_at = lax.broadcasted_iota(jnp.int32, (tok, tok), 1)
    is_own = key_at <= row_at

    def key_segments(step):
        return jnp.broadcast_to(seg_buf[step].astype(jnp.float32), (tok, tok)).T

    def fill_bias():
        last = shards - 1
        row_seg = seg_buf[0].astype(jnp.float32)
        edge = jnp.where(is_own, key_segments(0), key_segments(last))
        bias[last * tok :, :] = jnp.where(edge == row_seg, 0.0, -1e30)
        for step in range(1, last):
            bias[block(step), :] = jnp.where(key_segments(step) == row_seg, 0.0, -1e30)

    inner = slice(tok, None)

    def probabilities(group):
        span = 2 * rows
        for start in range(0, span, tok):
            cols = slice(start, start + tok)
            edge_s = jnp.where(is_own, s_own[group, :, cols], s_buf[group, :tok, cols])
            edge_gp = jnp.where(is_own, gp_own[group, :, cols], gp_buf[group, :tok, cols])
            grad_probs = jnp.concatenate([gp_buf[group, inner, cols], edge_gp], 0)
            scores = jnp.concatenate([s_buf[group, inner, cols], edge_s], 0)
            scores = scores * (scale * LOG2E) + bias[inner, :]
            exps = jnp.exp2(scores - jnp.max(scores, 0, keepdims=True))
            total = jnp.sum(exps, 0, keepdims=True)
            row_dot = jnp.sum(exps * grad_probs, 0, keepdims=True) / total
            probs = exps * (1.0 / total)
            scaled = probs * (grad_probs - row_dot)
            for target, value in ((p_buf, probs), (ds_buf, scaled)):
                edge = value[-tok:]
                target[group, inner, cols] = jnp.concatenate(
                    [value[:-tok], jnp.where(is_own, edge, 0.0)], 0
                ).astype(jnp.bfloat16)
                target[group, :tok, cols] = jnp.where(is_own, 0.0, edge).astype(jnp.bfloat16)

    def key_value_grads(at, group):
        return (
            dot(ds_buf[group, at, :], all_rows(q_buf, group), 1, 0) * scale,
            dot(p_buf[group, at, :], all_rows(g_buf, group), 1, 0),
        )

    def query_grads(group, slot):
        flipped = dot(k_buf[group], ds_buf[group, :, slot * rows : (slot + 1) * rows], 0, 0)
        for head in range(ratio):
            dq_buf[slot, group, :, head_cols(head)] = (
                flipped[:, head * tok : (head + 1) * tok].T * scale
            ).astype(jnp.bfloat16)

    def part_copy(step, group):
        return pltpu.make_async_remote_copy(
            src_ref=part.at[group, step - 1],
            dst_ref=got.at[group, step - 1],
            send_sem=part_send.at[group, step - 1],
            recv_sem=part_recv.at[group, step - 1],
            device_id={"ctx": me - step},
            device_id_type=MESH,
        )

    parts = [{step: part_copy(step, group) for step in steps} for group in range(groups)]
    query_send = [
        pair_copy(dq_buf.at[1, group], dq_hbm.at[0, :, query_cols(core, group)], group, 2)
        for group in range(groups)
    ]
    query_keep = [
        pltpu.make_async_copy(
            dq_buf.at[0, group], dq_hbm.at[0, :, query_cols(core, group)], local_sem.at[group, 4]
        )
        for group in range(groups)
    ]

    own_seg.wait()
    for group in range(groups):
        for copy in own[group]:
            copy.wait()
        own_products(0, group)
    for group in range(groups):
        for copy in pair[group]:
            copy.wait_recv()
        own_products(1, group)
    far = slice(0, DOC_SHARDS * tok)
    for group in range(groups):
        for step in steps:

            @pl.when(me >= step)
            def _(step=step, group=group):
                if group == 0:
                    near_seg[step].wait_recv()
                for copy in near[step][group]:
                    copy.wait_recv()

        if group == 0:
            fill_bias()
        s_buf[group] = dot(k_buf[group, far, :], all_rows(q_buf, group), 1, 1)
        gp_buf[group] = dot(v_buf[group, far, :], all_rows(g_buf, group), 1, 1)
        probabilities(group)
        grad_key, grad_value = key_value_grads(far, group)
        for step in steps:
            part[group, step - 1, 0] = grad_key[block(step)].astype(jnp.bfloat16)
            part[group, step - 1, 1] = grad_value[block(step)].astype(jnp.bfloat16)
        for step in reversed(steps):

            @pl.when(me >= step)
            def _(step=step, group=group):
                parts[group][step].start()

    for group in range(groups):
        query_grads(group, 1)
        query_send[group].start()
    for group in range(groups):
        query_grads(group, 0)
        query_keep[group].start()
    for group in range(groups):
        grad_key, grad_value = key_value_grads(block(0), group)
        dk_ref[:, head_cols(group)] = grad_key
        dv_ref[:, head_cols(group)] = grad_value
    for group in range(groups):
        for step in steps:

            @pl.when(me + step < cycle_size)
            def _(step=step, group=group):
                parts[group][step].wait_recv()
                dk_ref[:, head_cols(group)] += got[group, step - 1, 0].astype(jnp.float32)
                dv_ref[:, head_cols(group)] += got[group, step - 1, 1].astype(jnp.float32)

    for group in range(groups):
        query_keep[group].wait()
        query_send[group].wait()
        for copy in pair[group]:
            copy.wait_send()
        for step in steps:

            @pl.when(me + step < cycle_size)
            def _(step=step, group=group):
                if group == 0:
                    near_seg[step].wait_send()
                for copy in near[step][group]:
                    copy.wait_send()

            @pl.when(me >= step)
            def _(step=step, group=group):
                parts[group][step].wait_send()


def hand_over(dq_in, dk_in, dv_in, dq_out, dk_out, dv_out, dq_buf, dk_buf, dv_buf, sem):
    piece = dq_in.shape[1] // PIECES
    cuts = [pl.ds(i * piece, piece) for i in range(PIECES)]
    ways = [(dq_in.at[:, cut], dq_buf.at[:, cut], dq_out.at[:, cut]) for cut in cuts]
    ways += [(dk_in, dk_buf, dk_out), (dv_in, dv_buf, dv_out)]
    copies = [
        (
            pltpu.make_async_copy(source, held, sem.at[0, i]),
            pltpu.make_async_copy(held, target, sem.at[1, i]),
        )
        for i, (source, held, target) in enumerate(ways)
    ]
    for first, _ in copies:
        first.start()
    for first, second in copies:
        first.wait()
        second.start()
    for _, second in copies:
        second.wait()


def by_heads(cycle_size, queries, keys, values, cotangent, segment_ids):
    tok = keys.shape[0]
    half = queries.shape[2] // 2
    width = keys.shape[1] // 2
    groups = width // DH
    rows = half // groups
    rows = rows // DH * tok
    window = (DOC_SHARDS + 1) * tok
    bf16, f32 = jnp.bfloat16, jnp.float32
    anywhere = pl.BlockSpec(memory_space=pl.ANY)
    in_hbm = pl.BlockSpec(memory_space=pltpu.HBM)
    in_vmem = pl.BlockSpec(memory_space=pltpu.VMEM)
    dma = pltpu.SemaphoreType.DMA
    shapes = (
        jax.ShapeDtypeStruct(queries.shape, bf16),
        jax.ShapeDtypeStruct((tok, width), f32),
        jax.ShapeDtypeStruct((tok, width), f32),
    )
    grads = pl.pallas_call(
        functools.partial(kernel, cycle_size),
        out_shape=shapes,
        in_specs=[in_hbm] * 5,
        out_specs=(anywhere, in_vmem, in_vmem),
        scratch_shapes=[
            pltpu.VMEM((2, groups, tok, half // groups), bf16),
            pltpu.VMEM((2, groups, tok, half // groups), bf16),
            pltpu.VMEM((groups, window, DH), bf16),
            pltpu.VMEM((groups, window, DH), bf16),
            pltpu.VMEM((DOC_SHARDS + 1, 1, tok), jnp.int32),
            pltpu.VMEM((window, tok), f32),
            pltpu.VMEM((groups, tok, 2 * rows), f32),
            pltpu.VMEM((groups, tok, 2 * rows), f32),
            pltpu.VMEM((groups, window - tok, 2 * rows), f32),
            pltpu.VMEM((groups, window - tok, 2 * rows), f32),
            pltpu.VMEM((groups, window, 2 * rows), bf16),
            pltpu.VMEM((groups, window, 2 * rows), bf16),
            pltpu.VMEM((2, groups, tok, half // groups), bf16),
            pltpu.VMEM((groups, DOC_SHARDS, 2, tok, DH), bf16),
            pltpu.VMEM((groups, DOC_SHARDS, 2, tok, DH), bf16),
            dma((groups + 1, 5)),
            dma((groups, 3)),
            dma((groups, 3)),
            dma((DOC_SHARDS,)),
            dma((DOC_SHARDS,)),
            dma((DOC_SHARDS, groups, 2)),
            dma((DOC_SHARDS, groups, 2)),
            dma((groups, DOC_SHARDS)),
            dma((groups, DOC_SHARDS)),
        ],
        compiler_params=pltpu.CompilerParams(
            collective_id=0, has_side_effects=True, vmem_limit_bytes=VMEM_BYTES
        ),
    )(queries, keys, values, cotangent, segment_ids.reshape(1, tok))
    return pl.pallas_call(
        hand_over,
        out_shape=shapes,
        in_specs=[in_hbm] * 3,
        out_specs=(in_hbm,) * 3,
        scratch_shapes=[pltpu.VMEM(shape.shape, shape.dtype) for shape in shapes]
        + [dma((2, PIECES + 2))],
        compiler_params=pltpu.CompilerParams(vmem_limit_bytes=VMEM_BYTES),
    )(*grads)


def solution(mesh):
    placed = (
        P("section", "ctx", None),
        P("ctx", None),
        P("ctx", None),
        P("section", "ctx", None),
        P("ctx"),
    )
    cycle_size = mesh.shape["ctx"]
    pairs = mesh.shape["section"] == 2

    def step(queries, keys, values, cotangent, segment_ids):
        tok, width = keys.shape
        halves = pairs and queries.shape[0] == 1 and tok % DH == 0 and width % (2 * DH) == 0
        if halves:
            return by_heads(cycle_size, queries, keys, values, cotangent, segment_ids)
        return on_device(queries, keys, values, cotangent, segment_ids)

    return jax.shard_map(
        step,
        mesh=mesh,
        in_specs=placed,
        out_specs=(P("section", "ctx", None), P("ctx", "section"), P("ctx", "section")),
        check_vma=False,
    )
```

```python
import functools

import jax
import jax.numpy as jnp
from jax import lax
from jax.experimental import pallas as pl
from jax.experimental.pallas import tpu as pltpu
from jax.sharding import PartitionSpec as P

DH = 128
DOC_SHARDS = 2
LOG2E = 1.4426950408889634
MESH = pl.DeviceIdType.MESH
VMEM_BYTES = 63 << 20
PIECES = 4


def shifted(shard, axis, by):
    size = lax.axis_size(axis)
    pairs = [(i, i + by) for i in range(size) if 0 <= i + by < size]
    return lax.ppermute(shard, axis, pairs)


def as_sent(shard):

    def short(part):
        return part.astype(jnp.bfloat16) if part.dtype == jnp.float32 else part

    return jax.tree.map(short, shard)


def by_group(rows, groups):
    count, width = rows.shape
    head_ratio = width // (groups * DH)
    return (
        rows.reshape(count, groups, head_ratio, DH)
        .transpose(1, 2, 0, 3)
        .reshape(groups, head_ratio * count, DH)
    )


def add_pair(first, second):
    return (first[0] + second[0], first[1] + second[1])


def on_device(queries, keys, values, cotangent, segment_ids):
    tok_rows = keys.shape[0]
    groups = keys.shape[1] // DH
    heads = queries.shape[2] // DH
    head_ratio = heads // groups
    score_scale = DH ** (-0.5)
    cycle_size = lax.axis_size("ctx")
    my_index = lax.axis_index("ctx")
    query_rows = by_group(queries[0], groups)
    grad_rows = by_group(cotangent[0], groups)
    row_pos = my_index * tok_rows + jnp.tile(jnp.arange(tok_rows, dtype=jnp.int32), head_ratio)
    row_seg = jnp.tile(segment_ids, head_ratio)
    blocks = []
    current = (keys, values, segment_ids)
    for shard_step in range(DOC_SHARDS + 1):
        if shard_step > 0:
            current = shifted((current[0], current[1], current[2]), "ctx", 1)
        key_block, value_block, key_seg = current
        key_rows = key_block.reshape(tok_rows, groups, DH).transpose(1, 0, 2)
        value_rows = value_block.reshape(tok_rows, groups, DH).transpose(1, 0, 2)
        key_pos = (my_index - shard_step) % cycle_size * tok_rows + jnp.arange(
            tok_rows, dtype=jnp.int32
        )
        allowed = (row_seg[:, None] == key_seg[None, :]) & (key_pos[None, :] <= row_pos[:, None])
        if shard_step == 0:
            is_live = jnp.array(True)
        else:
            is_live = (my_index >= shard_step) & (key_seg[-1] >= segment_ids[0])
        blocks.append((key_rows, value_rows, allowed, is_live))
    row_count = head_ratio * tok_rows
    row_max = jnp.full((groups, row_count, 1), -1e30, jnp.float32)
    row_sum = jnp.zeros((groups, row_count, 1), jnp.float32)
    kept_scores = []
    for key_rows, value_rows, allowed, is_live in blocks:

        def running_stats(key_rows=key_rows, allowed=allowed, row_max=row_max, row_sum=row_sum):
            scores = (
                jnp.einsum("grd,gkd->grk", query_rows, key_rows, preferred_element_type=jnp.float32)
                * score_scale
            )
            block_max = jnp.max(jnp.where(allowed, scores, -1e30), -1, keepdims=True)
            new_max = jnp.maximum(row_max, block_max)
            added = jnp.sum(jnp.where(allowed, jnp.exp(scores - new_max), 0.0), -1, keepdims=True)
            return (new_max, row_sum * jnp.exp(row_max - new_max) + added, scores)

        row_max, row_sum, scores = running_stats()
        kept_scores.append(scores)
    log_total = row_max + jnp.log(row_sum)

    def block_probs(scores, allowed):
        return jnp.where(allowed, jnp.exp(scores - log_total), 0.0)

    output_rows = jnp.zeros((groups, row_count, DH), jnp.float32)
    for (key_rows, value_rows, allowed, is_live), scores in zip(blocks, kept_scores):

        def output_part(scores=scores, value_rows=value_rows, allowed=allowed):
            probs_low = block_probs(scores, allowed).astype(jnp.bfloat16)
            return jnp.einsum(
                "grk,gkd->grd", probs_low, value_rows, preferred_element_type=jnp.float32
            )

        output_rows = output_rows + output_part()
    row_dot = jnp.sum(grad_rows.astype(jnp.float32) * output_rows, -1, keepdims=True)
    grad_query = jnp.zeros((groups, row_count, DH), jnp.float32)
    partials = []
    for (key_rows, value_rows, allowed, is_live), scores in zip(blocks, kept_scores):

        def backward_part(scores=scores, key_rows=key_rows, value_rows=value_rows, allowed=allowed):
            probs = block_probs(scores, allowed)
            probs_low = probs.astype(jnp.bfloat16)
            grad_probs = jnp.einsum(
                "grd,gkd->grk", grad_rows, value_rows, preferred_element_type=jnp.float32
            )
            scaled_low = (probs * (grad_probs - row_dot) * score_scale).astype(jnp.bfloat16)
            query_part = jnp.einsum(
                "grk,gkd->grd", scaled_low, key_rows, preferred_element_type=jnp.float32
            )
            key_part = jnp.einsum(
                "grk,grd->gkd", scaled_low, query_rows, preferred_element_type=jnp.float32
            )
            value_part = jnp.einsum(
                "grk,grd->gkd", probs_low, grad_rows, preferred_element_type=jnp.float32
            )
            key_flat = key_part.transpose(1, 0, 2).reshape(tok_rows, groups * DH)
            value_flat = value_part.transpose(1, 0, 2).reshape(tok_rows, groups * DH)
            return (query_part, key_flat, value_flat)

        query_part, key_flat, value_flat = backward_part()
        grad_query = grad_query + query_part
        partials.append((key_flat, value_flat))
    summed = partials[0]
    for shard_step in range(1, DOC_SHARDS + 1):
        arrived = shifted(as_sent(partials[shard_step]), "ctx", -shard_step)
        summed = add_pair(summed, arrived)
    summed = lax.psum_scatter(summed, "section", scatter_dimension=1, tiled=True)
    query_out = (
        grad_query.reshape(groups, head_ratio, tok_rows, DH)
        .transpose(2, 0, 1, 3)
        .reshape(1, tok_rows, heads * DH)
    )
    return (query_out.astype(jnp.bfloat16), summed[0], summed[1])


def dot(first, second, first_dim, second_dim):
    return lax.dot_general(
        first,
        second,
        (((first_dim,), (second_dim,)), ((), ())),
        preferred_element_type=jnp.float32,
    )


def kernel(
    cycle_size,
    q_hbm,
    k_hbm,
    v_hbm,
    g_hbm,
    seg_hbm,
    dq_hbm,
    dk_ref,
    dv_ref,
    q_buf,
    g_buf,
    k_buf,
    v_buf,
    seg_buf,
    bias,
    s_own,
    gp_own,
    s_buf,
    gp_buf,
    p_buf,
    ds_buf,
    dq_buf,
    part,
    got,
    local_sem,
    pair_send,
    pair_recv,
    seg_send,
    seg_recv,
    near_send,
    near_recv,
    part_send,
    part_recv,
):
    tok = k_hbm.shape[0]
    groups = k_buf.shape[0]
    share = q_buf.shape[3]
    ratio = share // DH
    rows = ratio * tok
    shards = DOC_SHARDS + 1
    scale = DH ** (-0.5)
    me = lax.axis_index("ctx")
    core = lax.axis_index("section")
    other = 1 - core
    steps = range(1, shards)

    def query_cols(owner, group):
        return pl.ds(pl.multiple_of((owner * groups + group) * share, DH), share)

    def key_cols(group):
        return pl.ds(pl.multiple_of((core * groups + group) * DH, DH), DH)

    def block(step):
        return slice((shards - 1 - step) * tok, (shards - step) * tok)

    def block_ds(step):
        return pl.ds((shards - 1 - step) * tok, tok)

    barrier = pltpu.get_barrier_semaphore()
    pl.semaphore_signal(barrier, inc=1, device_id={"section": other}, device_id_type=MESH)
    greeted = 1
    for step in steps:
        has_next = me + step < cycle_size
        has_prev = me >= step

        @pl.when(has_next)
        def _(step=step):
            pl.semaphore_signal(barrier, inc=1, device_id={"ctx": me + step}, device_id_type=MESH)

        @pl.when(has_prev)
        def _(step=step):
            pl.semaphore_signal(barrier, inc=1, device_id={"ctx": me - step}, device_id_type=MESH)

        greeted = greeted + has_next.astype(jnp.int32) + has_prev.astype(jnp.int32)

    def own_copies(group):
        pairs = (
            (k_hbm.at[:, key_cols(group)], k_buf.at[group, block_ds(0), :]),
            (q_hbm.at[0, :, query_cols(core, group)], q_buf.at[0, group]),
            (v_hbm.at[:, key_cols(group)], v_buf.at[group, block_ds(0), :]),
            (g_hbm.at[0, :, query_cols(core, group)], g_buf.at[0, group]),
        )
        return [
            pltpu.make_async_copy(source, target, local_sem.at[group, i])
            for i, (source, target) in enumerate(pairs)
        ]

    own = [own_copies(group) for group in range(groups)]
    own_seg = pltpu.make_async_copy(seg_hbm, seg_buf.at[0], local_sem.at[groups, 0])
    own_seg.start()
    for copies in own:
        for copy in copies:
            copy.start()
    for step in steps:

        @pl.when(me < step)
        def _(step=step):
            for group in range(groups):
                k_buf[group, block(step), :] = jnp.zeros((tok, DH), jnp.bfloat16)
                v_buf[group, block(step), :] = jnp.zeros((tok, DH), jnp.bfloat16)
            seg_buf[step] = jnp.full((1, tok), -1, jnp.int32)

    pl.semaphore_wait(barrier, greeted)

    def to_next(source, target, step, send, recv):
        return pltpu.make_async_remote_copy(
            src_ref=source,
            dst_ref=target,
            send_sem=send,
            recv_sem=recv,
            device_id={"ctx": me + step},
            device_id_type=MESH,
        )

    def near_copies(step, group):
        at = step - 1
        pairs = (
            (k_hbm.at[:, key_cols(group)], k_buf.at[group, block_ds(step), :]),
            (v_hbm.at[:, key_cols(group)], v_buf.at[group, block_ds(step), :]),
        )
        return [
            to_next(source, target, step, near_send.at[at, group, i], near_recv.at[at, group, i])
            for i, (source, target) in enumerate(pairs)
        ]

    near = {step: [near_copies(step, group) for group in range(groups)] for step in steps}
    near_seg = {
        step: to_next(
            seg_hbm, seg_buf.at[step], step, seg_send.at[step - 1], seg_recv.at[step - 1]
        )
        for step in steps
    }

    def pair_copy(source, target, group, at):
        return pltpu.make_async_remote_copy(
            src_ref=source,
            dst_ref=target,
            send_sem=pair_send.at[group, at],
            recv_sem=pair_recv.at[group, at],
            device_id={"section": other},
            device_id_type=MESH,
        )

    pair = [
        [
            pair_copy(q_hbm.at[0, :, query_cols(other, group)], q_buf.at[1, group], group, 0),
            pair_copy(g_hbm.at[0, :, query_cols(other, group)], g_buf.at[1, group], group, 1),
        ]
        for group in range(groups)
    ]
    def send_near(group):
        for step in reversed(steps):

            @pl.when(me + step < cycle_size)
            def _(step=step):
                if group == 0:
                    near_seg[step].start()
                for copy in near[step][group]:
                    copy.start()

    def near_sent(group):
        for step in steps:

            @pl.when(me + step < cycle_size)
            def _(step=step):
                if group == 0:
                    near_seg[step].wait_send()
                for copy in near[step][group]:
                    copy.wait_send()

    send_near(0)
    for group in range(groups):
        for copy in pair[group]:
            copy.start()

    def head_cols(head):
        return slice(head * DH, (head + 1) * DH)

    def stacked(buf, slot, group):
        return jnp.concatenate([buf[slot, group, :, head_cols(h)] for h in range(ratio)], 0)

    def all_rows(buf, group):
        return jnp.concatenate([stacked(buf, 0, group), stacked(buf, 1, group)], 0)

    def own_products(slot, group):
        at = slice(slot * rows, (slot + 1) * rows)
        s_own[group, :, at] = dot(k_buf[group, block(0), :], stacked(q_buf, slot, group), 1, 1)
        gp_own[group, :, at] = dot(v_buf[group, block(0), :], stacked(g_buf, slot, group), 1, 1)

    key_at = lax.broadcasted_iota(jnp.int32, (tok, tok), 0)
    row_at = lax.broadcasted_iota(jnp.int32, (tok, tok), 1)
    is_own = key_at <= row_at

    def key_segments(step):
        return jnp.broadcast_to(seg_buf[step].astype(jnp.float32), (tok, tok)).T

    def fill_bias():
        last = shards - 1
        row_seg = seg_buf[0].astype(jnp.float32)
        edge = jnp.where(is_own, key_segments(0), key_segments(last))
        bias[last * tok :, :] = jnp.where(edge == row_seg, 0.0, -1e30)
        for step in range(1, last):
            bias[block(step), :] = jnp.where(key_segments(step) == row_seg, 0.0, -1e30)

    inner = slice(tok, None)

    def probabilities(group):
        span = 2 * rows
        for start in range(0, span, tok):
            cols = slice(start, start + tok)
            edge_s = jnp.where(is_own, s_own[group, :, cols], s_buf[group, :tok, cols])
            edge_gp = jnp.where(is_own, gp_own[group, :, cols], gp_buf[group, :tok, cols])
            grad_probs = jnp.concatenate([gp_buf[group, inner, cols], edge_gp], 0)
            scores = jnp.concatenate([s_buf[group, inner, cols], edge_s], 0)
            scores = scores * (scale * LOG2E) + bias[inner, :]
            exps = jnp.exp2(scores - jnp.max(scores, 0, keepdims=True))
            total = jnp.sum(exps, 0, keepdims=True)
            row_dot = jnp.sum(exps * grad_probs, 0, keepdims=True) / total
            probs = exps * (1.0 / total)
            scaled = probs * (grad_probs - row_dot)
            for target, value in ((p_buf, probs), (ds_buf, scaled)):
                edge = value[-tok:]
                target[group, inner, cols] = jnp.concatenate(
                    [value[:-tok], jnp.where(is_own, edge, 0.0)], 0
                ).astype(jnp.bfloat16)
                target[group, :tok, cols] = jnp.where(is_own, 0.0, edge).astype(jnp.bfloat16)

    def key_value_grads(at, group):
        return (
            dot(ds_buf[group, at, :], all_rows(q_buf, group), 1, 0) * scale,
            dot(p_buf[group, at, :], all_rows(g_buf, group), 1, 0),
        )

    def query_grads(group, slot):
        flipped = dot(k_buf[group], ds_buf[group, :, slot * rows : (slot + 1) * rows], 0, 0)
        for head in range(ratio):
            dq_buf[slot, group, :, head_cols(head)] = (
                flipped[:, head * tok : (head + 1) * tok].T * scale
            ).astype(jnp.bfloat16)

    def part_copy(step, group):
        return pltpu.make_async_remote_copy(
            src_ref=part.at[group, step - 1],
            dst_ref=got.at[group, step - 1],
            send_sem=part_send.at[group, step - 1],
            recv_sem=part_recv.at[group, step - 1],
            device_id={"ctx": me - step},
            device_id_type=MESH,
        )

    parts = [{step: part_copy(step, group) for step in steps} for group in range(groups)]
    query_send = [
        pair_copy(dq_buf.at[1, group], dq_hbm.at[0, :, query_cols(core, group)], group, 2)
        for group in range(groups)
    ]
    query_keep = [
        pltpu.make_async_copy(
            dq_buf.at[0, group], dq_hbm.at[0, :, query_cols(core, group)], local_sem.at[group, 4]
        )
        for group in range(groups)
    ]

    own_seg.wait()
    for group in range(groups):
        for copy in own[group]:
            copy.wait()
        if group > 0:
            near_sent(group - 1)
            send_near(group)
        own_products(0, group)
    for group in range(groups):
        for copy in pair[group]:
            copy.wait_recv()
        own_products(1, group)
    far = slice(0, DOC_SHARDS * tok)
    for group in range(groups):
        for step in steps:

            @pl.when(me >= step)
            def _(step=step, group=group):
                if group == 0:
                    near_seg[step].wait_recv()
                for copy in near[step][group]:
                    copy.wait_recv()

        if group == 0:
            fill_bias()
        s_buf[group] = dot(k_buf[group, far, :], all_rows(q_buf, group), 1, 1)
        gp_buf[group] = dot(v_buf[group, far, :], all_rows(g_buf, group), 1, 1)
        probabilities(group)
        grad_key, grad_value = key_value_grads(far, group)
        for step in steps:
            part[group, step - 1, 0] = grad_key[block(step)].astype(jnp.bfloat16)
            part[group, step - 1, 1] = grad_value[block(step)].astype(jnp.bfloat16)
        for step in reversed(steps):

            @pl.when(me >= step)
            def _(step=step, group=group):
                parts[group][step].start()

    for group in range(groups):
        query_grads(group, 1)
        query_send[group].start()
    for group in range(groups):
        query_grads(group, 0)
        query_keep[group].start()
    for group in range(groups):
        grad_key, grad_value = key_value_grads(block(0), group)
        dk_ref[:, head_cols(group)] = grad_key
        dv_ref[:, head_cols(group)] = grad_value
    for group in range(groups):
        for step in steps:

            @pl.when(me + step < cycle_size)
            def _(step=step, group=group):
                parts[group][step].wait_recv()
                dk_ref[:, head_cols(group)] += got[group, step - 1, 0].astype(jnp.float32)
                dv_ref[:, head_cols(group)] += got[group, step - 1, 1].astype(jnp.float32)

    for group in range(groups):
        query_keep[group].wait()
        query_send[group].wait()
        for copy in pair[group]:
            copy.wait_send()
        for step in steps:

            @pl.when(me >= step)
            def _(step=step, group=group):
                parts[group][step].wait_send()

    near_sent(groups - 1)


def hand_over(dq_in, dk_in, dv_in, dq_out, dk_out, dv_out, dq_buf, dk_buf, dv_buf, sem):
    piece = dq_in.shape[1] // PIECES
    cuts = [pl.ds(i * piece, piece) for i in range(PIECES)]
    ways = [(dq_in.at[:, cut], dq_buf.at[:, cut], dq_out.at[:, cut]) for cut in cuts]
    ways += [(dk_in, dk_buf, dk_out), (dv_in, dv_buf, dv_out)]
    copies = [
        (
            pltpu.make_async_copy(source, held, sem.at[0, i]),
            pltpu.make_async_copy(held, target, sem.at[1, i]),
        )
        for i, (source, held, target) in enumerate(ways)
    ]
    for first, _ in copies:
        first.start()
    for first, second in copies:
        first.wait()
        second.start()
    for _, second in copies:
        second.wait()


def by_heads(cycle_size, queries, keys, values, cotangent, segment_ids):
    tok = keys.shape[0]
    half = queries.shape[2] // 2
    width = keys.shape[1] // 2
    groups = width // DH
    rows = half // groups
    rows = rows // DH * tok
    window = (DOC_SHARDS + 1) * tok
    bf16, f32 = jnp.bfloat16, jnp.float32
    anywhere = pl.BlockSpec(memory_space=pl.ANY)
    in_hbm = pl.BlockSpec(memory_space=pltpu.HBM)
    in_vmem = pl.BlockSpec(memory_space=pltpu.VMEM)
    dma = pltpu.SemaphoreType.DMA
    shapes = (
        jax.ShapeDtypeStruct(queries.shape, bf16),
        jax.ShapeDtypeStruct((tok, width), f32),
        jax.ShapeDtypeStruct((tok, width), f32),
    )
    grads = pl.pallas_call(
        functools.partial(kernel, cycle_size),
        out_shape=shapes,
        in_specs=[in_hbm] * 5,
        out_specs=(anywhere, in_vmem, in_vmem),
        scratch_shapes=[
            pltpu.VMEM((2, groups, tok, half // groups), bf16),
            pltpu.VMEM((2, groups, tok, half // groups), bf16),
            pltpu.VMEM((groups, window, DH), bf16),
            pltpu.VMEM((groups, window, DH), bf16),
            pltpu.VMEM((DOC_SHARDS + 1, 1, tok), jnp.int32),
            pltpu.VMEM((window, tok), f32),
            pltpu.VMEM((groups, tok, 2 * rows), f32),
            pltpu.VMEM((groups, tok, 2 * rows), f32),
            pltpu.VMEM((groups, window - tok, 2 * rows), f32),
            pltpu.VMEM((groups, window - tok, 2 * rows), f32),
            pltpu.VMEM((groups, window, 2 * rows), bf16),
            pltpu.VMEM((groups, window, 2 * rows), bf16),
            pltpu.VMEM((2, groups, tok, half // groups), bf16),
            pltpu.VMEM((groups, DOC_SHARDS, 2, tok, DH), bf16),
            pltpu.VMEM((groups, DOC_SHARDS, 2, tok, DH), bf16),
            dma((groups + 1, 5)),
            dma((groups, 3)),
            dma((groups, 3)),
            dma((DOC_SHARDS,)),
            dma((DOC_SHARDS,)),
            dma((DOC_SHARDS, groups, 2)),
            dma((DOC_SHARDS, groups, 2)),
            dma((groups, DOC_SHARDS)),
            dma((groups, DOC_SHARDS)),
        ],
        compiler_params=pltpu.CompilerParams(
            collective_id=0, has_side_effects=True, vmem_limit_bytes=VMEM_BYTES
        ),
    )(queries, keys, values, cotangent, segment_ids.reshape(1, tok))
    return pl.pallas_call(
        hand_over,
        out_shape=shapes,
        in_specs=[in_hbm] * 3,
        out_specs=(in_hbm,) * 3,
        scratch_shapes=[pltpu.VMEM(shape.shape, shape.dtype) for shape in shapes]
        + [dma((2, PIECES + 2))],
        compiler_params=pltpu.CompilerParams(vmem_limit_bytes=VMEM_BYTES),
    )(*grads)


def solution(mesh):
    placed = (
        P("section", "ctx", None),
        P("ctx", None),
        P("ctx", None),
        P("section", "ctx", None),
        P("ctx"),
    )
    cycle_size = mesh.shape["ctx"]
    pairs = mesh.shape["section"] == 2

    def step(queries, keys, values, cotangent, segment_ids):
        tok, width = keys.shape
        halves = pairs and queries.shape[0] == 1 and tok % DH == 0 and width % (2 * DH) == 0
        if halves:
            return by_heads(cycle_size, queries, keys, values, cotangent, segment_ids)
        return on_device(queries, keys, values, cotangent, segment_ids)

    return jax.shard_map(
        step,
        mesh=mesh,
        in_specs=placed,
        out_specs=(P("section", "ctx", None), P("ctx", "section"), P("ctx", "section")),
        check_vma=False,
    )
```

```python
import functools

import jax
import jax.numpy as jnp
from jax import lax
from jax.experimental import pallas as pl
from jax.experimental.pallas import tpu as pltpu
from jax.sharding import PartitionSpec as P

DH = 128
DOC_SHARDS = 2
LOG2E = 1.4426950408889634
MESH = pl.DeviceIdType.MESH
VMEM_BYTES = 63 << 20
PIECES = 4


def shifted(shard, axis, by):
    size = lax.axis_size(axis)
    pairs = [(i, i + by) for i in range(size) if 0 <= i + by < size]
    return lax.ppermute(shard, axis, pairs)


def as_sent(shard):

    def short(part):
        return part.astype(jnp.bfloat16) if part.dtype == jnp.float32 else part

    return jax.tree.map(short, shard)


def by_group(rows, groups):
    count, width = rows.shape
    head_ratio = width // (groups * DH)
    return (
        rows.reshape(count, groups, head_ratio, DH)
        .transpose(1, 2, 0, 3)
        .reshape(groups, head_ratio * count, DH)
    )


def add_pair(first, second):
    return (first[0] + second[0], first[1] + second[1])


def on_device(queries, keys, values, cotangent, segment_ids):
    tok_rows = keys.shape[0]
    groups = keys.shape[1] // DH
    heads = queries.shape[2] // DH
    head_ratio = heads // groups
    score_scale = DH ** (-0.5)
    cycle_size = lax.axis_size("ctx")
    my_index = lax.axis_index("ctx")
    query_rows = by_group(queries[0], groups)
    grad_rows = by_group(cotangent[0], groups)
    row_pos = my_index * tok_rows + jnp.tile(jnp.arange(tok_rows, dtype=jnp.int32), head_ratio)
    row_seg = jnp.tile(segment_ids, head_ratio)
    blocks = []
    current = (keys, values, segment_ids)
    for shard_step in range(DOC_SHARDS + 1):
        if shard_step > 0:
            current = shifted((current[0], current[1], current[2]), "ctx", 1)
        key_block, value_block, key_seg = current
        key_rows = key_block.reshape(tok_rows, groups, DH).transpose(1, 0, 2)
        value_rows = value_block.reshape(tok_rows, groups, DH).transpose(1, 0, 2)
        key_pos = (my_index - shard_step) % cycle_size * tok_rows + jnp.arange(
            tok_rows, dtype=jnp.int32
        )
        allowed = (row_seg[:, None] == key_seg[None, :]) & (key_pos[None, :] <= row_pos[:, None])
        if shard_step == 0:
            is_live = jnp.array(True)
        else:
            is_live = (my_index >= shard_step) & (key_seg[-1] >= segment_ids[0])
        blocks.append((key_rows, value_rows, allowed, is_live))
    row_count = head_ratio * tok_rows
    row_max = jnp.full((groups, row_count, 1), -1e30, jnp.float32)
    row_sum = jnp.zeros((groups, row_count, 1), jnp.float32)
    kept_scores = []
    for key_rows, value_rows, allowed, is_live in blocks:

        def running_stats(key_rows=key_rows, allowed=allowed, row_max=row_max, row_sum=row_sum):
            scores = (
                jnp.einsum("grd,gkd->grk", query_rows, key_rows, preferred_element_type=jnp.float32)
                * score_scale
            )
            block_max = jnp.max(jnp.where(allowed, scores, -1e30), -1, keepdims=True)
            new_max = jnp.maximum(row_max, block_max)
            added = jnp.sum(jnp.where(allowed, jnp.exp(scores - new_max), 0.0), -1, keepdims=True)
            return (new_max, row_sum * jnp.exp(row_max - new_max) + added, scores)

        row_max, row_sum, scores = running_stats()
        kept_scores.append(scores)
    log_total = row_max + jnp.log(row_sum)

    def block_probs(scores, allowed):
        return jnp.where(allowed, jnp.exp(scores - log_total), 0.0)

    output_rows = jnp.zeros((groups, row_count, DH), jnp.float32)
    for (key_rows, value_rows, allowed, is_live), scores in zip(blocks, kept_scores):

        def output_part(scores=scores, value_rows=value_rows, allowed=allowed):
            probs_low = block_probs(scores, allowed).astype(jnp.bfloat16)
            return jnp.einsum(
                "grk,gkd->grd", probs_low, value_rows, preferred_element_type=jnp.float32
            )

        output_rows = output_rows + output_part()
    row_dot = jnp.sum(grad_rows.astype(jnp.float32) * output_rows, -1, keepdims=True)
    grad_query = jnp.zeros((groups, row_count, DH), jnp.float32)
    partials = []
    for (key_rows, value_rows, allowed, is_live), scores in zip(blocks, kept_scores):

        def backward_part(scores=scores, key_rows=key_rows, value_rows=value_rows, allowed=allowed):
            probs = block_probs(scores, allowed)
            probs_low = probs.astype(jnp.bfloat16)
            grad_probs = jnp.einsum(
                "grd,gkd->grk", grad_rows, value_rows, preferred_element_type=jnp.float32
            )
            scaled_low = (probs * (grad_probs - row_dot) * score_scale).astype(jnp.bfloat16)
            query_part = jnp.einsum(
                "grk,gkd->grd", scaled_low, key_rows, preferred_element_type=jnp.float32
            )
            key_part = jnp.einsum(
                "grk,grd->gkd", scaled_low, query_rows, preferred_element_type=jnp.float32
            )
            value_part = jnp.einsum(
                "grk,grd->gkd", probs_low, grad_rows, preferred_element_type=jnp.float32
            )
            key_flat = key_part.transpose(1, 0, 2).reshape(tok_rows, groups * DH)
            value_flat = value_part.transpose(1, 0, 2).reshape(tok_rows, groups * DH)
            return (query_part, key_flat, value_flat)

        query_part, key_flat, value_flat = backward_part()
        grad_query = grad_query + query_part
        partials.append((key_flat, value_flat))
    summed = partials[0]
    for shard_step in range(1, DOC_SHARDS + 1):
        arrived = shifted(as_sent(partials[shard_step]), "ctx", -shard_step)
        summed = add_pair(summed, arrived)
    summed = lax.psum_scatter(summed, "section", scatter_dimension=1, tiled=True)
    query_out = (
        grad_query.reshape(groups, head_ratio, tok_rows, DH)
        .transpose(2, 0, 1, 3)
        .reshape(1, tok_rows, heads * DH)
    )
    return (query_out.astype(jnp.bfloat16), summed[0], summed[1])


def dot(first, second, first_dim, second_dim):
    return lax.dot_general(
        first,
        second,
        (((first_dim,), (second_dim,)), ((), ())),
        preferred_element_type=jnp.float32,
    )


def kernel(
    cycle_size,
    q_hbm,
    k_hbm,
    v_hbm,
    g_hbm,
    seg_hbm,
    dq_ref,
    dk_ref,
    dv_ref,
    q_buf,
    g_buf,
    k_buf,
    v_buf,
    seg_buf,
    bias,
    s_own,
    gp_own,
    s_buf,
    gp_buf,
    p_buf,
    ds_buf,
    dq_buf,
    part,
    got,
    local_sem,
    pair_send,
    pair_recv,
    seg_send,
    seg_recv,
    near_send,
    near_recv,
    part_send,
    part_recv,
):
    tok = k_hbm.shape[0]
    groups = k_buf.shape[0]
    share = q_buf.shape[3]
    ratio = share // DH
    rows = ratio * tok
    shards = DOC_SHARDS + 1
    scale = DH ** (-0.5)
    me = lax.axis_index("ctx")
    core = lax.axis_index("section")
    other = 1 - core
    steps = range(1, shards)

    def query_cols(owner, group):
        return pl.ds(pl.multiple_of((owner * groups + group) * share, DH), share)

    def key_cols(group):
        return pl.ds(pl.multiple_of((core * groups + group) * DH, DH), DH)

    def block(step):
        return slice((shards - 1 - step) * tok, (shards - step) * tok)

    def block_ds(step):
        return pl.ds((shards - 1 - step) * tok, tok)

    barrier = pltpu.get_barrier_semaphore()
    pl.semaphore_signal(barrier, inc=1, device_id={"section": other}, device_id_type=MESH)
    greeted = 1
    for step in steps:
        has_next = me + step < cycle_size
        has_prev = me >= step

        @pl.when(has_next)
        def _(step=step):
            pl.semaphore_signal(barrier, inc=1, device_id={"ctx": me + step}, device_id_type=MESH)

        @pl.when(has_prev)
        def _(step=step):
            pl.semaphore_signal(barrier, inc=1, device_id={"ctx": me - step}, device_id_type=MESH)

        greeted = greeted + has_next.astype(jnp.int32) + has_prev.astype(jnp.int32)

    def own_copies(group):
        pairs = (
            (k_hbm.at[:, key_cols(group)], k_buf.at[group, block_ds(0), :]),
            (q_hbm.at[0, :, query_cols(core, group)], q_buf.at[0, group]),
            (v_hbm.at[:, key_cols(group)], v_buf.at[group, block_ds(0), :]),
            (g_hbm.at[0, :, query_cols(core, group)], g_buf.at[0, group]),
        )
        return [
            pltpu.make_async_copy(source, target, local_sem.at[group, i])
            for i, (source, target) in enumerate(pairs)
        ]

    own = [own_copies(group) for group in range(groups)]
    own_seg = pltpu.make_async_copy(seg_hbm, seg_buf.at[0], local_sem.at[groups, 0])
    own_seg.start()
    for copies in own:
        for copy in copies:
            copy.start()
    for step in steps:

        @pl.when(me < step)
        def _(step=step):
            for group in range(groups):
                k_buf[group, block(step), :] = jnp.zeros((tok, DH), jnp.bfloat16)
                v_buf[group, block(step), :] = jnp.zeros((tok, DH), jnp.bfloat16)
            seg_buf[step] = jnp.full((1, tok), -1, jnp.int32)

    pl.semaphore_wait(barrier, greeted)

    def to_next(source, target, step, send, recv):
        return pltpu.make_async_remote_copy(
            src_ref=source,
            dst_ref=target,
            send_sem=send,
            recv_sem=recv,
            device_id={"ctx": me + step},
            device_id_type=MESH,
        )

    def near_copies(step, group):
        at = step - 1
        pairs = (
            (k_hbm.at[:, key_cols(group)], k_buf.at[group, block_ds(step), :]),
            (v_hbm.at[:, key_cols(group)], v_buf.at[group, block_ds(step), :]),
        )
        return [
            to_next(source, target, step, near_send.at[at, group, i], near_recv.at[at, group, i])
            for i, (source, target) in enumerate(pairs)
        ]

    near = {step: [near_copies(step, group) for group in range(groups)] for step in steps}
    near_seg = {
        step: to_next(
            seg_hbm, seg_buf.at[step], step, seg_send.at[step - 1], seg_recv.at[step - 1]
        )
        for step in steps
    }

    def pair_copy(source, target, group, at):
        return pltpu.make_async_remote_copy(
            src_ref=source,
            dst_ref=target,
            send_sem=pair_send.at[group, at],
            recv_sem=pair_recv.at[group, at],
            device_id={"section": other},
            device_id_type=MESH,
        )

    pair = [
        [
            pair_copy(q_hbm.at[0, :, query_cols(other, group)], q_buf.at[1, group], group, 0),
            pair_copy(g_hbm.at[0, :, query_cols(other, group)], g_buf.at[1, group], group, 1),
        ]
        for group in range(groups)
    ]
    def send_near(group):
        for step in reversed(steps):

            @pl.when(me + step < cycle_size)
            def _(step=step):
                if group == 0:
                    near_seg[step].start()
                for copy in near[step][group]:
                    copy.start()

    def near_sent(group):
        for step in steps:

            @pl.when(me + step < cycle_size)
            def _(step=step):
                if group == 0:
                    near_seg[step].wait_send()
                for copy in near[step][group]:
                    copy.wait_send()

    send_near(0)
    for group in range(groups):
        for copy in pair[group]:
            copy.start()

    def head_cols(head):
        return slice(head * DH, (head + 1) * DH)

    def stacked(buf, slot, group):
        return jnp.concatenate([buf[slot, group, :, head_cols(h)] for h in range(ratio)], 0)

    def all_rows(buf, group):
        return jnp.concatenate([stacked(buf, 0, group), stacked(buf, 1, group)], 0)

    def own_products(slot, group):
        at = slice(slot * rows, (slot + 1) * rows)
        s_own[group, :, at] = dot(k_buf[group, block(0), :], stacked(q_buf, slot, group), 1, 1)
        gp_own[group, :, at] = dot(v_buf[group, block(0), :], stacked(g_buf, slot, group), 1, 1)

    key_at = lax.broadcasted_iota(jnp.int32, (tok, tok), 0)
    row_at = lax.broadcasted_iota(jnp.int32, (tok, tok), 1)
    is_own = key_at <= row_at

    def key_segments(step):
        return jnp.broadcast_to(seg_buf[step].astype(jnp.float32), (tok, tok)).T

    def fill_bias():
        last = shards - 1
        row_seg = seg_buf[0].astype(jnp.float32)
        edge = jnp.where(is_own, key_segments(0), key_segments(last))
        bias[last * tok :, :] = jnp.where(edge == row_seg, 0.0, -1e30)
        for step in range(1, last):
            bias[block(step), :] = jnp.where(key_segments(step) == row_seg, 0.0, -1e30)

    inner = slice(tok, None)

    def probabilities(group):
        span = 2 * rows
        for start in range(0, span, tok):
            cols = slice(start, start + tok)
            edge_s = jnp.where(is_own, s_own[group, :, cols], s_buf[group, :tok, cols])
            edge_gp = jnp.where(is_own, gp_own[group, :, cols], gp_buf[group, :tok, cols])
            grad_probs = jnp.concatenate([gp_buf[group, inner, cols], edge_gp], 0)
            scores = jnp.concatenate([s_buf[group, inner, cols], edge_s], 0)
            scores = scores * (scale * LOG2E) + bias[inner, :]
            exps = jnp.exp2(scores - jnp.max(scores, 0, keepdims=True))
            total = jnp.sum(exps, 0, keepdims=True)
            row_dot = jnp.sum(exps * grad_probs, 0, keepdims=True) / total
            probs = exps * (1.0 / total)
            scaled = probs * (grad_probs - row_dot)
            for target, value in ((p_buf, probs), (ds_buf, scaled)):
                edge = value[-tok:]
                target[group, inner, cols] = jnp.concatenate(
                    [value[:-tok], jnp.where(is_own, edge, 0.0)], 0
                ).astype(jnp.bfloat16)
                target[group, :tok, cols] = jnp.where(is_own, 0.0, edge).astype(jnp.bfloat16)

    def key_value_grads(at, group):
        return (
            dot(ds_buf[group, at, :], all_rows(q_buf, group), 1, 0) * scale,
            dot(p_buf[group, at, :], all_rows(g_buf, group), 1, 0),
        )

    def query_grads(group, slot):
        flipped = dot(k_buf[group], ds_buf[group, :, slot * rows : (slot + 1) * rows], 0, 0)
        for head in range(ratio):
            grad_query = flipped[:, head * tok : (head + 1) * tok].T * scale
            grad_query = grad_query.astype(jnp.bfloat16)
            if slot == 0:
                start = (core * groups + group) * share + head * DH
                dq_ref[0, :, pl.ds(pl.multiple_of(start, DH), DH)] = grad_query
            else:
                dq_buf[group, :, head_cols(head)] = grad_query

    def part_copy(step, group):
        return pltpu.make_async_remote_copy(
            src_ref=part.at[group, step - 1],
            dst_ref=got.at[group, step - 1],
            send_sem=part_send.at[group, step - 1],
            recv_sem=part_recv.at[group, step - 1],
            device_id={"ctx": me - step},
            device_id_type=MESH,
        )

    parts = [{step: part_copy(step, group) for step in steps} for group in range(groups)]
    query_send = [
        pair_copy(dq_buf.at[group], dq_ref.at[0, :, query_cols(core, group)], group, 2)
        for group in range(groups)
    ]
    own_seg.wait()
    for group in range(groups):
        for copy in own[group]:
            copy.wait()
        if group > 0:
            near_sent(group - 1)
            send_near(group)
        own_products(0, group)
    for group in range(groups):
        for copy in pair[group]:
            copy.wait_recv()
        own_products(1, group)
    far = slice(0, DOC_SHARDS * tok)
    for group in range(groups):
        for step in steps:

            @pl.when(me >= step)
            def _(step=step, group=group):
                if group == 0:
                    near_seg[step].wait_recv()
                for copy in near[step][group]:
                    copy.wait_recv()

        if group == 0:
            fill_bias()
        s_buf[group] = dot(k_buf[group, far, :], all_rows(q_buf, group), 1, 1)
        gp_buf[group] = dot(v_buf[group, far, :], all_rows(g_buf, group), 1, 1)
        probabilities(group)
        grad_key, grad_value = key_value_grads(far, group)
        for step in steps:
            part[group, step - 1, 0] = grad_key[block(step)].astype(jnp.bfloat16)
            part[group, step - 1, 1] = grad_value[block(step)].astype(jnp.bfloat16)
        for step in reversed(steps):

            @pl.when(me >= step)
            def _(step=step, group=group):
                parts[group][step].start()

    for group in range(groups):
        query_grads(group, 1)
        query_send[group].start()
    for group in range(groups):
        query_grads(group, 0)
    for group in range(groups):
        grad_key, grad_value = key_value_grads(block(0), group)
        dk_ref[:, head_cols(group)] = grad_key
        dv_ref[:, head_cols(group)] = grad_value
    for group in range(groups):
        for step in steps:

            @pl.when(me + step < cycle_size)
            def _(step=step, group=group):
                parts[group][step].wait_recv()
                dk_ref[:, head_cols(group)] += got[group, step - 1, 0].astype(jnp.float32)
                dv_ref[:, head_cols(group)] += got[group, step - 1, 1].astype(jnp.float32)

    for group in range(groups):
        query_send[group].wait()
        for copy in pair[group]:
            copy.wait_send()
        for step in steps:

            @pl.when(me >= step)
            def _(step=step, group=group):
                parts[group][step].wait_send()

    near_sent(groups - 1)


def hand_over(dq_in, dk_in, dv_in, dq_out, dk_out, dv_out, sem):
    piece = dq_in.shape[1] // PIECES
    cuts = [pl.ds(i * piece, piece) for i in range(PIECES)]
    pairs = [(dq_in.at[:, cut], dq_out.at[:, cut]) for cut in cuts]
    pairs += [(dk_in, dk_out), (dv_in, dv_out)]
    copies = [pltpu.make_async_copy(*pair, sem.at[i]) for i, pair in enumerate(pairs)]
    for copy in copies:
        copy.start()
    for copy in copies:
        copy.wait()


def by_heads(cycle_size, queries, keys, values, cotangent, segment_ids):
    tok = keys.shape[0]
    half = queries.shape[2] // 2
    width = keys.shape[1] // 2
    groups = width // DH
    rows = half // groups
    rows = rows // DH * tok
    window = (DOC_SHARDS + 1) * tok
    bf16, f32 = jnp.bfloat16, jnp.float32
    anywhere = pl.BlockSpec(memory_space=pl.ANY)
    in_hbm = pl.BlockSpec(memory_space=pltpu.HBM)
    in_vmem = pl.BlockSpec(memory_space=pltpu.VMEM)
    dma = pltpu.SemaphoreType.DMA
    shapes = (
        jax.ShapeDtypeStruct(queries.shape, bf16),
        jax.ShapeDtypeStruct((tok, width), f32),
        jax.ShapeDtypeStruct((tok, width), f32),
    )
    grads = pl.pallas_call(
        functools.partial(kernel, cycle_size),
        out_shape=tuple(pltpu.VMEM(shape.shape, shape.dtype) for shape in shapes),
        in_specs=[in_hbm] * 5,
        out_specs=(in_vmem,) * 3,
        scratch_shapes=[
            pltpu.VMEM((2, groups, tok, half // groups), bf16),
            pltpu.VMEM((2, groups, tok, half // groups), bf16),
            pltpu.VMEM((groups, window, DH), bf16),
            pltpu.VMEM((groups, window, DH), bf16),
            pltpu.VMEM((DOC_SHARDS + 1, 1, tok), jnp.int32),
            pltpu.VMEM((window, tok), f32),
            pltpu.VMEM((groups, tok, 2 * rows), f32),
            pltpu.VMEM((groups, tok, 2 * rows), f32),
            pltpu.VMEM((groups, window - tok, 2 * rows), f32),
            pltpu.VMEM((groups, window - tok, 2 * rows), f32),
            pltpu.VMEM((groups, window, 2 * rows), bf16),
            pltpu.VMEM((groups, window, 2 * rows), bf16),
            pltpu.VMEM((groups, tok, half // groups), bf16),
            pltpu.VMEM((groups, DOC_SHARDS, 2, tok, DH), bf16),
            pltpu.VMEM((groups, DOC_SHARDS, 2, tok, DH), bf16),
            dma((groups + 1, 5)),
            dma((groups, 3)),
            dma((groups, 3)),
            dma((DOC_SHARDS,)),
            dma((DOC_SHARDS,)),
            dma((DOC_SHARDS, groups, 2)),
            dma((DOC_SHARDS, groups, 2)),
            dma((groups, DOC_SHARDS)),
            dma((groups, DOC_SHARDS)),
        ],
        compiler_params=pltpu.CompilerParams(
            collective_id=0, has_side_effects=True, vmem_limit_bytes=VMEM_BYTES
        ),
    )(queries, keys, values, cotangent, segment_ids.reshape(1, tok))
    return pl.pallas_call(
        hand_over,
        out_shape=shapes,
        in_specs=[in_vmem] * 3,
        out_specs=(in_hbm,) * 3,
        scratch_shapes=[dma((PIECES + 2,))],
        compiler_params=pltpu.CompilerParams(vmem_limit_bytes=8 << 20),
    )(*grads)


def solution(mesh):
    placed = (
        P("section", "ctx", None),
        P("ctx", None),
        P("ctx", None),
        P("section", "ctx", None),
        P("ctx"),
    )
    cycle_size = mesh.shape["ctx"]
    pairs = mesh.shape["section"] == 2

    def step(queries, keys, values, cotangent, segment_ids):
        tok, width = keys.shape
        halves = pairs and queries.shape[0] == 1 and tok % DH == 0 and width % (2 * DH) == 0
        if halves:
            return by_heads(cycle_size, queries, keys, values, cotangent, segment_ids)
        return on_device(queries, keys, values, cotangent, segment_ids)

    return jax.shard_map(
        step,
        mesh=mesh,
        in_specs=placed,
        out_specs=(P("section", "ctx", None), P("ctx", "section"), P("ctx", "section")),
        check_vma=False,
    )
```

```python
import functools

import jax
import jax.numpy as jnp
from jax import lax
from jax.experimental import pallas as pl
from jax.experimental.pallas import tpu as pltpu
from jax.sharding import PartitionSpec as P

DH = 128
DOC_SHARDS = 2
LOG2E = 1.4426950408889634
MESH = pl.DeviceIdType.MESH
VMEM_BYTES = 63 << 20
PIECES = 4


def shifted(shard, axis, by):
    size = lax.axis_size(axis)
    pairs = [(i, i + by) for i in range(size) if 0 <= i + by < size]
    return lax.ppermute(shard, axis, pairs)


def as_sent(shard):

    def short(part):
        return part.astype(jnp.bfloat16) if part.dtype == jnp.float32 else part

    return jax.tree.map(short, shard)


def by_group(rows, groups):
    count, width = rows.shape
    head_ratio = width // (groups * DH)
    return (
        rows.reshape(count, groups, head_ratio, DH)
        .transpose(1, 2, 0, 3)
        .reshape(groups, head_ratio * count, DH)
    )


def add_pair(first, second):
    return (first[0] + second[0], first[1] + second[1])


def on_device(queries, keys, values, cotangent, segment_ids):
    tok_rows = keys.shape[0]
    groups = keys.shape[1] // DH
    heads = queries.shape[2] // DH
    head_ratio = heads // groups
    score_scale = DH ** (-0.5)
    cycle_size = lax.axis_size("ctx")
    my_index = lax.axis_index("ctx")
    query_rows = by_group(queries[0], groups)
    grad_rows = by_group(cotangent[0], groups)
    row_pos = my_index * tok_rows + jnp.tile(jnp.arange(tok_rows, dtype=jnp.int32), head_ratio)
    row_seg = jnp.tile(segment_ids, head_ratio)
    blocks = []
    current = (keys, values, segment_ids)
    for shard_step in range(DOC_SHARDS + 1):
        if shard_step > 0:
            current = shifted((current[0], current[1], current[2]), "ctx", 1)
        key_block, value_block, key_seg = current
        key_rows = key_block.reshape(tok_rows, groups, DH).transpose(1, 0, 2)
        value_rows = value_block.reshape(tok_rows, groups, DH).transpose(1, 0, 2)
        key_pos = (my_index - shard_step) % cycle_size * tok_rows + jnp.arange(
            tok_rows, dtype=jnp.int32
        )
        allowed = (row_seg[:, None] == key_seg[None, :]) & (key_pos[None, :] <= row_pos[:, None])
        if shard_step == 0:
            is_live = jnp.array(True)
        else:
            is_live = (my_index >= shard_step) & (key_seg[-1] >= segment_ids[0])
        blocks.append((key_rows, value_rows, allowed, is_live))
    row_count = head_ratio * tok_rows
    row_max = jnp.full((groups, row_count, 1), -1e30, jnp.float32)
    row_sum = jnp.zeros((groups, row_count, 1), jnp.float32)
    kept_scores = []
    for key_rows, value_rows, allowed, is_live in blocks:

        def running_stats(key_rows=key_rows, allowed=allowed, row_max=row_max, row_sum=row_sum):
            scores = (
                jnp.einsum("grd,gkd->grk", query_rows, key_rows, preferred_element_type=jnp.float32)
                * score_scale
            )
            block_max = jnp.max(jnp.where(allowed, scores, -1e30), -1, keepdims=True)
            new_max = jnp.maximum(row_max, block_max)
            added = jnp.sum(jnp.where(allowed, jnp.exp(scores - new_max), 0.0), -1, keepdims=True)
            return (new_max, row_sum * jnp.exp(row_max - new_max) + added, scores)

        row_max, row_sum, scores = running_stats()
        kept_scores.append(scores)
    log_total = row_max + jnp.log(row_sum)

    def block_probs(scores, allowed):
        return jnp.where(allowed, jnp.exp(scores - log_total), 0.0)

    output_rows = jnp.zeros((groups, row_count, DH), jnp.float32)
    for (key_rows, value_rows, allowed, is_live), scores in zip(blocks, kept_scores):

        def output_part(scores=scores, value_rows=value_rows, allowed=allowed):
            probs_low = block_probs(scores, allowed).astype(jnp.bfloat16)
            return jnp.einsum(
                "grk,gkd->grd", probs_low, value_rows, preferred_element_type=jnp.float32
            )

        output_rows = output_rows + output_part()
    row_dot = jnp.sum(grad_rows.astype(jnp.float32) * output_rows, -1, keepdims=True)
    grad_query = jnp.zeros((groups, row_count, DH), jnp.float32)
    partials = []
    for (key_rows, value_rows, allowed, is_live), scores in zip(blocks, kept_scores):

        def backward_part(scores=scores, key_rows=key_rows, value_rows=value_rows, allowed=allowed):
            probs = block_probs(scores, allowed)
            probs_low = probs.astype(jnp.bfloat16)
            grad_probs = jnp.einsum(
                "grd,gkd->grk", grad_rows, value_rows, preferred_element_type=jnp.float32
            )
            scaled_low = (probs * (grad_probs - row_dot) * score_scale).astype(jnp.bfloat16)
            query_part = jnp.einsum(
                "grk,gkd->grd", scaled_low, key_rows, preferred_element_type=jnp.float32
            )
            key_part = jnp.einsum(
                "grk,grd->gkd", scaled_low, query_rows, preferred_element_type=jnp.float32
            )
            value_part = jnp.einsum(
                "grk,grd->gkd", probs_low, grad_rows, preferred_element_type=jnp.float32
            )
            key_flat = key_part.transpose(1, 0, 2).reshape(tok_rows, groups * DH)
            value_flat = value_part.transpose(1, 0, 2).reshape(tok_rows, groups * DH)
            return (query_part, key_flat, value_flat)

        query_part, key_flat, value_flat = backward_part()
        grad_query = grad_query + query_part
        partials.append((key_flat, value_flat))
    summed = partials[0]
    for shard_step in range(1, DOC_SHARDS + 1):
        arrived = shifted(as_sent(partials[shard_step]), "ctx", -shard_step)
        summed = add_pair(summed, arrived)
    summed = lax.psum_scatter(summed, "section", scatter_dimension=1, tiled=True)
    query_out = (
        grad_query.reshape(groups, head_ratio, tok_rows, DH)
        .transpose(2, 0, 1, 3)
        .reshape(1, tok_rows, heads * DH)
    )
    return (query_out.astype(jnp.bfloat16), summed[0], summed[1])


def dot(first, second, first_dim, second_dim):
    return lax.dot_general(
        first,
        second,
        (((first_dim,), (second_dim,)), ((), ())),
        preferred_element_type=jnp.float32,
    )


def kernel(
    cycle_size,
    q_hbm,
    k_hbm,
    v_hbm,
    g_hbm,
    seg_hbm,
    dq_ref,
    dk_ref,
    dv_ref,
    q_buf,
    g_buf,
    k_buf,
    v_buf,
    seg_buf,
    bias,
    s_own,
    gp_own,
    s_buf,
    gp_buf,
    p_buf,
    ds_buf,
    dq_buf,
    part,
    got,
    local_sem,
    pair_send,
    pair_recv,
    seg_send,
    seg_recv,
    near_send,
    near_recv,
    part_send,
    part_recv,
):
    tok = k_hbm.shape[0]
    groups = k_buf.shape[0]
    share = q_buf.shape[3]
    ratio = share // DH
    rows = ratio * tok
    shards = DOC_SHARDS + 1
    scale = DH ** (-0.5)
    me = lax.axis_index("ctx")
    core = lax.axis_index("section")
    other = 1 - core
    steps = range(1, shards)

    def query_cols(owner, group):
        return pl.ds(pl.multiple_of((owner * groups + group) * share, DH), share)

    def key_cols(group):
        return pl.ds(pl.multiple_of((core * groups + group) * DH, DH), DH)

    def block(step):
        return slice((shards - 1 - step) * tok, (shards - step) * tok)

    def block_ds(step):
        return pl.ds((shards - 1 - step) * tok, tok)

    barrier = pltpu.get_barrier_semaphore()
    pl.semaphore_signal(barrier, inc=1, device_id={"section": other}, device_id_type=MESH)
    greeted = 1
    for step in steps:
        has_next = me + step < cycle_size
        has_prev = me >= step

        @pl.when(has_next)
        def _(step=step):
            pl.semaphore_signal(barrier, inc=1, device_id={"ctx": me + step}, device_id_type=MESH)

        @pl.when(has_prev)
        def _(step=step):
            pl.semaphore_signal(barrier, inc=1, device_id={"ctx": me - step}, device_id_type=MESH)

        greeted = greeted + has_next.astype(jnp.int32) + has_prev.astype(jnp.int32)

    def own_copies(group):
        pairs = (
            (k_hbm.at[:, key_cols(group)], k_buf.at[group, block_ds(0), :]),
            (q_hbm.at[0, :, query_cols(core, group)], q_buf.at[0, group]),
            (v_hbm.at[:, key_cols(group)], v_buf.at[group, block_ds(0), :]),
            (g_hbm.at[0, :, query_cols(core, group)], g_buf.at[0, group]),
        )
        return [
            pltpu.make_async_copy(source, target, local_sem.at[group, i])
            for i, (source, target) in enumerate(pairs)
        ]

    own = [own_copies(group) for group in range(groups)]
    own_seg = pltpu.make_async_copy(seg_hbm, seg_buf.at[0], local_sem.at[groups, 0])
    own_seg.start()
    for copies in own:
        for copy in copies:
            copy.start()
    for step in steps:

        @pl.when(me < step)
        def _(step=step):
            for group in range(groups):
                k_buf[group, block(step), :] = jnp.zeros((tok, DH), jnp.bfloat16)
                v_buf[group, block(step), :] = jnp.zeros((tok, DH), jnp.bfloat16)
            seg_buf[step] = jnp.full((1, tok), -1, jnp.int32)

    pl.semaphore_wait(barrier, greeted)

    def to_next(source, target, step, send, recv):
        return pltpu.make_async_remote_copy(
            src_ref=source,
            dst_ref=target,
            send_sem=send,
            recv_sem=recv,
            device_id={"ctx": me + step},
            device_id_type=MESH,
        )

    def near_copies(step, group):
        at = step - 1
        pairs = (
            (k_hbm.at[:, key_cols(group)], k_buf.at[group, block_ds(step), :]),
            (v_hbm.at[:, key_cols(group)], v_buf.at[group, block_ds(step), :]),
        )
        return [
            to_next(source, target, step, near_send.at[at, group, i], near_recv.at[at, group, i])
            for i, (source, target) in enumerate(pairs)
        ]

    near = {step: [near_copies(step, group) for group in range(groups)] for step in steps}
    near_seg = {
        step: to_next(
            seg_hbm, seg_buf.at[step], step, seg_send.at[step - 1], seg_recv.at[step - 1]
        )
        for step in steps
    }

    def pair_copy(source, target, group, at):
        return pltpu.make_async_remote_copy(
            src_ref=source,
            dst_ref=target,
            send_sem=pair_send.at[group, at],
            recv_sem=pair_recv.at[group, at],
            device_id={"section": other},
            device_id_type=MESH,
        )

    pair = [
        [
            pair_copy(q_hbm.at[0, :, query_cols(other, group)], q_buf.at[1, group], group, 0),
            pair_copy(g_hbm.at[0, :, query_cols(other, group)], g_buf.at[1, group], group, 1),
        ]
        for group in range(groups)
    ]
    def send_near(group):
        for which in range(2):
            for step in reversed(steps):

                @pl.when(me + step < cycle_size)
                def _(step=step, which=which):
                    if group == 0 and which == 0:
                        near_seg[step].start()
                    near[step][group][which].start()

    def near_sent(group):
        for step in steps:

            @pl.when(me + step < cycle_size)
            def _(step=step):
                if group == 0:
                    near_seg[step].wait_send()
                for copy in near[step][group]:
                    copy.wait_send()

    send_near(0)
    for group in range(groups):
        for copy in pair[group]:
            copy.start()

    def head_cols(head):
        return slice(head * DH, (head + 1) * DH)

    def stacked(buf, slot, group):
        return jnp.concatenate([buf[slot, group, :, head_cols(h)] for h in range(ratio)], 0)

    def all_rows(buf, group):
        return jnp.concatenate([stacked(buf, 0, group), stacked(buf, 1, group)], 0)

    def own_products(slot, group):
        at = slice(slot * rows, (slot + 1) * rows)
        s_own[group, :, at] = dot(k_buf[group, block(0), :], stacked(q_buf, slot, group), 1, 1)
        gp_own[group, :, at] = dot(v_buf[group, block(0), :], stacked(g_buf, slot, group), 1, 1)

    key_at = lax.broadcasted_iota(jnp.int32, (tok, tok), 0)
    row_at = lax.broadcasted_iota(jnp.int32, (tok, tok), 1)
    is_own = key_at <= row_at

    def key_segments(step):
        return jnp.broadcast_to(seg_buf[step].astype(jnp.float32), (tok, tok)).T

    def fill_bias():
        last = shards - 1
        row_seg = seg_buf[0].astype(jnp.float32)
        edge = jnp.where(is_own, key_segments(0), key_segments(last))
        bias[last * tok :, :] = jnp.where(edge == row_seg, 0.0, -1e30)
        for step in range(1, last):
            bias[block(step), :] = jnp.where(key_segments(step) == row_seg, 0.0, -1e30)

    inner = slice(tok, None)

    def store_tiles(target, group, cols, value):
        edge = value[-tok:]
        target[group, inner, cols] = jnp.concatenate(
            [value[:-tok], jnp.where(is_own, edge, 0.0)], 0
        ).astype(jnp.bfloat16)
        target[group, :tok, cols] = jnp.where(is_own, 0.0, edge).astype(jnp.bfloat16)

    def probabilities(group):
        for start in range(0, 2 * rows, tok):
            cols = slice(start, start + tok)
            edge = jnp.where(is_own, s_own[group, :, cols], s_buf[group, :tok, cols])
            scores = jnp.concatenate([s_buf[group, inner, cols], edge], 0)
            scores = scores * (scale * LOG2E) + bias[inner, :]
            exps = jnp.exp2(scores - jnp.max(scores, 0, keepdims=True))
            probs = exps * (1.0 / jnp.sum(exps, 0, keepdims=True))
            s_buf[group, :, cols] = probs
            store_tiles(p_buf, group, cols, probs)

    def score_grads(group):
        for start in range(0, 2 * rows, tok):
            cols = slice(start, start + tok)
            edge = jnp.where(is_own, gp_own[group, :, cols], gp_buf[group, :tok, cols])
            grad_probs = jnp.concatenate([gp_buf[group, inner, cols], edge], 0)
            probs = s_buf[group, :, cols]
            row_dot = jnp.sum(probs * grad_probs, 0, keepdims=True)
            store_tiles(ds_buf, group, cols, probs * (grad_probs - row_dot))

    def key_grads(at, group):
        return dot(ds_buf[group, at, :], all_rows(q_buf, group), 1, 0) * scale

    def value_grads(at, group):
        return dot(p_buf[group, at, :], all_rows(g_buf, group), 1, 0)

    def query_grads(group, slot):
        flipped = dot(k_buf[group], ds_buf[group, :, slot * rows : (slot + 1) * rows], 0, 0)
        for head in range(ratio):
            grad_query = flipped[:, head * tok : (head + 1) * tok].T * scale
            grad_query = grad_query.astype(jnp.bfloat16)
            if slot == 0:
                start = (core * groups + group) * share + head * DH
                dq_ref[0, :, pl.ds(pl.multiple_of(start, DH), DH)] = grad_query
            else:
                dq_buf[group, :, head_cols(head)] = grad_query

    def part_copy(step, group, which):
        return pltpu.make_async_remote_copy(
            src_ref=part.at[group, step - 1, which],
            dst_ref=got.at[group, step - 1, which],
            send_sem=part_send.at[group, step - 1, which],
            recv_sem=part_recv.at[group, step - 1, which],
            device_id={"ctx": me - step},
            device_id_type=MESH,
        )

    parts = [
        {step: [part_copy(step, group, which) for which in range(2)] for step in steps}
        for group in range(groups)
    ]

    def send_part(group, which, grad):
        for step in steps:
            part[group, step - 1, which] = grad[block(step)].astype(jnp.bfloat16)
        for step in reversed(steps):

            @pl.when(me >= step)
            def _(step=step):
                parts[group][step][which].start()

    def near_arrived(group, which):
        for step in steps:

            @pl.when(me >= step)
            def _(step=step):
                if group == 0 and which == 0:
                    near_seg[step].wait_recv()
                near[step][group][which].wait_recv()

    query_send = [
        pair_copy(dq_buf.at[group], dq_ref.at[0, :, query_cols(core, group)], group, 2)
        for group in range(groups)
    ]
    own_seg.wait()
    for group in range(groups):
        for copy in own[group]:
            copy.wait()
        if group > 0:
            near_sent(group - 1)
            send_near(group)
        own_products(0, group)
    for group in range(groups):
        for copy in pair[group]:
            copy.wait_recv()
        own_products(1, group)
    far = slice(0, DOC_SHARDS * tok)
    for group in range(groups):
        near_arrived(group, 0)
        if group == 0:
            fill_bias()
        s_buf[group] = dot(k_buf[group, far, :], all_rows(q_buf, group), 1, 1)
        probabilities(group)
        send_part(group, 1, value_grads(far, group))
        near_arrived(group, 1)
        gp_buf[group] = dot(v_buf[group, far, :], all_rows(g_buf, group), 1, 1)
        score_grads(group)
        send_part(group, 0, key_grads(far, group))
    for group in range(groups):
        query_grads(group, 1)
        query_send[group].start()
    for group in range(groups):
        query_grads(group, 0)
        dk_ref[:, head_cols(group)] = key_grads(block(0), group)
        dv_ref[:, head_cols(group)] = value_grads(block(0), group)
    for group in range(groups):
        for which, target in ((1, dv_ref), (0, dk_ref)):
            for step in steps:

                @pl.when(me + step < cycle_size)
                def _(step=step, group=group, which=which, target=target):
                    parts[group][step][which].wait_recv()
                    more = got[group, step - 1, which].astype(jnp.float32)
                    target[:, head_cols(group)] += more

    for group in range(groups):
        query_send[group].wait()
        for copy in pair[group]:
            copy.wait_send()
        for step in steps:

            @pl.when(me >= step)
            def _(step=step, group=group):
                for copy in parts[group][step]:
                    copy.wait_send()

    near_sent(groups - 1)


def hand_over(dq_in, dk_in, dv_in, dq_out, dk_out, dv_out, sem):
    piece = dq_in.shape[1] // PIECES
    cuts = [pl.ds(i * piece, piece) for i in range(PIECES)]
    pairs = [(dq_in.at[:, cut], dq_out.at[:, cut]) for cut in cuts]
    pairs += [(dk_in, dk_out), (dv_in, dv_out)]
    copies = [pltpu.make_async_copy(*pair, sem.at[i]) for i, pair in enumerate(pairs)]
    for copy in copies:
        copy.start()
    for copy in copies:
        copy.wait()


def by_heads(cycle_size, queries, keys, values, cotangent, segment_ids):
    tok = keys.shape[0]
    half = queries.shape[2] // 2
    width = keys.shape[1] // 2
    groups = width // DH
    rows = half // groups
    rows = rows // DH * tok
    window = (DOC_SHARDS + 1) * tok
    bf16, f32 = jnp.bfloat16, jnp.float32
    anywhere = pl.BlockSpec(memory_space=pl.ANY)
    in_hbm = pl.BlockSpec(memory_space=pltpu.HBM)
    in_vmem = pl.BlockSpec(memory_space=pltpu.VMEM)
    dma = pltpu.SemaphoreType.DMA
    shapes = (
        jax.ShapeDtypeStruct(queries.shape, bf16),
        jax.ShapeDtypeStruct((tok, width), f32),
        jax.ShapeDtypeStruct((tok, width), f32),
    )
    grads = pl.pallas_call(
        functools.partial(kernel, cycle_size),
        out_shape=tuple(pltpu.VMEM(shape.shape, shape.dtype) for shape in shapes),
        in_specs=[in_hbm] * 5,
        out_specs=(in_vmem,) * 3,
        scratch_shapes=[
            pltpu.VMEM((2, groups, tok, half // groups), bf16),
            pltpu.VMEM((2, groups, tok, half // groups), bf16),
            pltpu.VMEM((groups, window, DH), bf16),
            pltpu.VMEM((groups, window, DH), bf16),
            pltpu.VMEM((DOC_SHARDS + 1, 1, tok), jnp.int32),
            pltpu.VMEM((window, tok), f32),
            pltpu.VMEM((groups, tok, 2 * rows), f32),
            pltpu.VMEM((groups, tok, 2 * rows), f32),
            pltpu.VMEM((groups, window - tok, 2 * rows), f32),
            pltpu.VMEM((groups, window - tok, 2 * rows), f32),
            pltpu.VMEM((groups, window, 2 * rows), bf16),
            pltpu.VMEM((groups, window, 2 * rows), bf16),
            pltpu.VMEM((groups, tok, half // groups), bf16),
            pltpu.VMEM((groups, DOC_SHARDS, 2, tok, DH), bf16),
            pltpu.VMEM((groups, DOC_SHARDS, 2, tok, DH), bf16),
            dma((groups + 1, 5)),
            dma((groups, 3)),
            dma((groups, 3)),
            dma((DOC_SHARDS,)),
            dma((DOC_SHARDS,)),
            dma((DOC_SHARDS, groups, 2)),
            dma((DOC_SHARDS, groups, 2)),
            dma((groups, DOC_SHARDS, 2)),
            dma((groups, DOC_SHARDS, 2)),
        ],
        compiler_params=pltpu.CompilerParams(
            collective_id=0, has_side_effects=True, vmem_limit_bytes=VMEM_BYTES
        ),
    )(queries, keys, values, cotangent, segment_ids.reshape(1, tok))
    return pl.pallas_call(
        hand_over,
        out_shape=shapes,
        in_specs=[in_vmem] * 3,
        out_specs=(in_hbm,) * 3,
        scratch_shapes=[dma((PIECES + 2,))],
        compiler_params=pltpu.CompilerParams(vmem_limit_bytes=8 << 20),
    )(*grads)


def solution(mesh):
    placed = (
        P("section", "ctx", None),
        P("ctx", None),
        P("ctx", None),
        P("section", "ctx", None),
        P("ctx"),
    )
    cycle_size = mesh.shape["ctx"]
    pairs = mesh.shape["section"] == 2

    def step(queries, keys, values, cotangent, segment_ids):
        tok, width = keys.shape
        halves = pairs and queries.shape[0] == 1 and tok % DH == 0 and width % (2 * DH) == 0
        if halves:
            return by_heads(cycle_size, queries, keys, values, cotangent, segment_ids)
        return on_device(queries, keys, values, cotangent, segment_ids)

    return jax.shard_map(
        step,
        mesh=mesh,
        in_specs=placed,
        out_specs=(P("section", "ctx", None), P("ctx", "section"), P("ctx", "section")),
        check_vma=False,
    )
```

```python
import functools

import jax
import jax.numpy as jnp
from jax import lax
from jax.experimental import pallas as pl
from jax.experimental.pallas import tpu as pltpu
from jax.sharding import PartitionSpec as P

DH = 128
DOC_SHARDS = 2
LOG2E = 1.4426950408889634
MESH = pl.DeviceIdType.MESH
VMEM_BYTES = 63 << 20
PIECES = 4


def shifted(shard, axis, by):
    size = lax.axis_size(axis)
    pairs = [(i, i + by) for i in range(size) if 0 <= i + by < size]
    return lax.ppermute(shard, axis, pairs)


def as_sent(shard):

    def short(part):
        return part.astype(jnp.bfloat16) if part.dtype == jnp.float32 else part

    return jax.tree.map(short, shard)


def by_group(rows, groups):
    count, width = rows.shape
    head_ratio = width // (groups * DH)
    return (
        rows.reshape(count, groups, head_ratio, DH)
        .transpose(1, 2, 0, 3)
        .reshape(groups, head_ratio * count, DH)
    )


def add_pair(first, second):
    return (first[0] + second[0], first[1] + second[1])


def on_device(queries, keys, values, cotangent, segment_ids):
    tok_rows = keys.shape[0]
    groups = keys.shape[1] // DH
    heads = queries.shape[2] // DH
    head_ratio = heads // groups
    score_scale = DH ** (-0.5)
    cycle_size = lax.axis_size("ctx")
    my_index = lax.axis_index("ctx")
    query_rows = by_group(queries[0], groups)
    grad_rows = by_group(cotangent[0], groups)
    row_pos = my_index * tok_rows + jnp.tile(jnp.arange(tok_rows, dtype=jnp.int32), head_ratio)
    row_seg = jnp.tile(segment_ids, head_ratio)
    blocks = []
    current = (keys, values, segment_ids)
    for shard_step in range(DOC_SHARDS + 1):
        if shard_step > 0:
            current = shifted((current[0], current[1], current[2]), "ctx", 1)
        key_block, value_block, key_seg = current
        key_rows = key_block.reshape(tok_rows, groups, DH).transpose(1, 0, 2)
        value_rows = value_block.reshape(tok_rows, groups, DH).transpose(1, 0, 2)
        key_pos = (my_index - shard_step) % cycle_size * tok_rows + jnp.arange(
            tok_rows, dtype=jnp.int32
        )
        allowed = (row_seg[:, None] == key_seg[None, :]) & (key_pos[None, :] <= row_pos[:, None])
        if shard_step == 0:
            is_live = jnp.array(True)
        else:
            is_live = (my_index >= shard_step) & (key_seg[-1] >= segment_ids[0])
        blocks.append((key_rows, value_rows, allowed, is_live))
    row_count = head_ratio * tok_rows
    row_max = jnp.full((groups, row_count, 1), -1e30, jnp.float32)
    row_sum = jnp.zeros((groups, row_count, 1), jnp.float32)
    kept_scores = []
    for key_rows, value_rows, allowed, is_live in blocks:

        def running_stats(key_rows=key_rows, allowed=allowed, row_max=row_max, row_sum=row_sum):
            scores = (
                jnp.einsum("grd,gkd->grk", query_rows, key_rows, preferred_element_type=jnp.float32)
                * score_scale
            )
            block_max = jnp.max(jnp.where(allowed, scores, -1e30), -1, keepdims=True)
            new_max = jnp.maximum(row_max, block_max)
            added = jnp.sum(jnp.where(allowed, jnp.exp(scores - new_max), 0.0), -1, keepdims=True)
            return (new_max, row_sum * jnp.exp(row_max - new_max) + added, scores)

        row_max, row_sum, scores = running_stats()
        kept_scores.append(scores)
    log_total = row_max + jnp.log(row_sum)

    def block_probs(scores, allowed):
        return jnp.where(allowed, jnp.exp(scores - log_total), 0.0)

    output_rows = jnp.zeros((groups, row_count, DH), jnp.float32)
    for (key_rows, value_rows, allowed, is_live), scores in zip(blocks, kept_scores):

        def output_part(scores=scores, value_rows=value_rows, allowed=allowed):
            probs_low = block_probs(scores, allowed).astype(jnp.bfloat16)
            return jnp.einsum(
                "grk,gkd->grd", probs_low, value_rows, preferred_element_type=jnp.float32
            )

        output_rows = output_rows + output_part()
    row_dot = jnp.sum(grad_rows.astype(jnp.float32) * output_rows, -1, keepdims=True)
    grad_query = jnp.zeros((groups, row_count, DH), jnp.float32)
    partials = []
    for (key_rows, value_rows, allowed, is_live), scores in zip(blocks, kept_scores):

        def backward_part(scores=scores, key_rows=key_rows, value_rows=value_rows, allowed=allowed):
            probs = block_probs(scores, allowed)
            probs_low = probs.astype(jnp.bfloat16)
            grad_probs = jnp.einsum(
                "grd,gkd->grk", grad_rows, value_rows, preferred_element_type=jnp.float32
            )
            scaled_low = (probs * (grad_probs - row_dot) * score_scale).astype(jnp.bfloat16)
            query_part = jnp.einsum(
                "grk,gkd->grd", scaled_low, key_rows, preferred_element_type=jnp.float32
            )
            key_part = jnp.einsum(
                "grk,grd->gkd", scaled_low, query_rows, preferred_element_type=jnp.float32
            )
            value_part = jnp.einsum(
                "grk,grd->gkd", probs_low, grad_rows, preferred_element_type=jnp.float32
            )
            key_flat = key_part.transpose(1, 0, 2).reshape(tok_rows, groups * DH)
            value_flat = value_part.transpose(1, 0, 2).reshape(tok_rows, groups * DH)
            return (query_part, key_flat, value_flat)

        query_part, key_flat, value_flat = backward_part()
        grad_query = grad_query + query_part
        partials.append((key_flat, value_flat))
    summed = partials[0]
    for shard_step in range(1, DOC_SHARDS + 1):
        arrived = shifted(as_sent(partials[shard_step]), "ctx", -shard_step)
        summed = add_pair(summed, arrived)
    summed = lax.psum_scatter(summed, "section", scatter_dimension=1, tiled=True)
    query_out = (
        grad_query.reshape(groups, head_ratio, tok_rows, DH)
        .transpose(2, 0, 1, 3)
        .reshape(1, tok_rows, heads * DH)
    )
    return (query_out.astype(jnp.bfloat16), summed[0], summed[1])


def dot(first, second, first_dim, second_dim):
    return lax.dot_general(
        first,
        second,
        (((first_dim,), (second_dim,)), ((), ())),
        preferred_element_type=jnp.float32,
    )


def kernel(
    cycle_size,
    q_hbm,
    k_hbm,
    v_hbm,
    g_hbm,
    seg_hbm,
    dq_ref,
    dk_ref,
    dv_ref,
    q_buf,
    g_buf,
    k_buf,
    v_buf,
    seg_buf,
    bias,
    s_own,
    gp_own,
    s_buf,
    gp_buf,
    p_buf,
    ds_buf,
    dq_buf,
    part,
    got,
    local_sem,
    pair_send,
    pair_recv,
    seg_send,
    seg_recv,
    near_send,
    near_recv,
    part_send,
    part_recv,
):
    tok = k_hbm.shape[0]
    groups = k_buf.shape[0]
    share = q_buf.shape[3]
    ratio = share // DH
    rows = ratio * tok
    shards = DOC_SHARDS + 1
    scale = DH ** (-0.5)
    me = lax.axis_index("ctx")
    core = lax.axis_index("section")
    other = 1 - core
    steps = range(1, shards)

    def query_cols(owner, group):
        return pl.ds(pl.multiple_of((owner * groups + group) * share, DH), share)

    def key_cols(group):
        return pl.ds(pl.multiple_of((core * groups + group) * DH, DH), DH)

    def block(step):
        return slice((shards - 1 - step) * tok, (shards - step) * tok)

    def block_ds(step):
        return pl.ds((shards - 1 - step) * tok, tok)

    barrier = pltpu.get_barrier_semaphore()
    pl.semaphore_signal(barrier, inc=1, device_id={"section": other}, device_id_type=MESH)
    greeted = 1
    for step in steps:
        has_next = me + step < cycle_size
        has_prev = me >= step

        @pl.when(has_next)
        def _(step=step):
            pl.semaphore_signal(barrier, inc=1, device_id={"ctx": me + step}, device_id_type=MESH)

        @pl.when(has_prev)
        def _(step=step):
            pl.semaphore_signal(barrier, inc=1, device_id={"ctx": me - step}, device_id_type=MESH)

        greeted = greeted + has_next.astype(jnp.int32) + has_prev.astype(jnp.int32)

    def own_copies(group):
        pairs = (
            (k_hbm.at[:, key_cols(group)], k_buf.at[group, block_ds(0), :]),
            (q_hbm.at[0, :, query_cols(core, group)], q_buf.at[0, group]),
            (v_hbm.at[:, key_cols(group)], v_buf.at[group, block_ds(0), :]),
            (g_hbm.at[0, :, query_cols(core, group)], g_buf.at[0, group]),
        )
        return [
            pltpu.make_async_copy(source, target, local_sem.at[group, i])
            for i, (source, target) in enumerate(pairs)
        ]

    own = [own_copies(group) for group in range(groups)]
    own_seg = pltpu.make_async_copy(seg_hbm, seg_buf.at[0], local_sem.at[groups, 0])
    own_seg.start()
    for copies in own:
        for copy in copies:
            copy.start()
    for step in steps:

        @pl.when(me < step)
        def _(step=step):
            for group in range(groups):
                k_buf[group, block(step), :] = jnp.zeros((tok, DH), jnp.bfloat16)
                v_buf[group, block(step), :] = jnp.zeros((tok, DH), jnp.bfloat16)
            seg_buf[step] = jnp.full((1, tok), -1, jnp.int32)

    pl.semaphore_wait(barrier, greeted)

    def to_next(source, target, step, send, recv):
        return pltpu.make_async_remote_copy(
            src_ref=source,
            dst_ref=target,
            send_sem=send,
            recv_sem=recv,
            device_id={"ctx": me + step},
            device_id_type=MESH,
        )

    def near_copies(step, group):
        at = step - 1
        pairs = (
            (k_hbm.at[:, key_cols(group)], k_buf.at[group, block_ds(step), :]),
            (v_hbm.at[:, key_cols(group)], v_buf.at[group, block_ds(step), :]),
        )
        return [
            to_next(source, target, step, near_send.at[at, group, i], near_recv.at[at, group, i])
            for i, (source, target) in enumerate(pairs)
        ]

    near = {step: [near_copies(step, group) for group in range(groups)] for step in steps}
    near_seg = {
        step: to_next(
            seg_hbm, seg_buf.at[step], step, seg_send.at[step - 1], seg_recv.at[step - 1]
        )
        for step in steps
    }

    def pair_copy(source, target, group, at):
        return pltpu.make_async_remote_copy(
            src_ref=source,
            dst_ref=target,
            send_sem=pair_send.at[group, at],
            recv_sem=pair_recv.at[group, at],
            device_id={"section": other},
            device_id_type=MESH,
        )

    pair = [
        [
            pair_copy(q_hbm.at[0, :, query_cols(other, group)], q_buf.at[1, group], group, 0),
            pair_copy(g_hbm.at[0, :, query_cols(other, group)], g_buf.at[1, group], group, 1),
        ]
        for group in range(groups)
    ]
    def send_near(group):
        for which in range(2):
            for step in reversed(steps):

                @pl.when(me + step < cycle_size)
                def _(step=step, which=which):
                    if group == 0 and which == 0:
                        near_seg[step].start()
                    near[step][group][which].start()

    def near_sent(group):
        for step in steps:

            @pl.when(me + step < cycle_size)
            def _(step=step):
                if group == 0:
                    near_seg[step].wait_send()
                for copy in near[step][group]:
                    copy.wait_send()

    for group in range(groups):
        send_near(group)
        for copy in pair[group]:
            copy.start()

    def head_cols(head):
        return slice(head * DH, (head + 1) * DH)

    def stacked(buf, slot, group):
        return jnp.concatenate([buf[slot, group, :, head_cols(h)] for h in range(ratio)], 0)

    def all_rows(buf, group):
        return jnp.concatenate([stacked(buf, 0, group), stacked(buf, 1, group)], 0)

    def own_products(slot, group):
        at = slice(slot * rows, (slot + 1) * rows)
        s_own[group, :, at] = dot(k_buf[group, block(0), :], stacked(q_buf, slot, group), 1, 1)
        gp_own[group, :, at] = dot(v_buf[group, block(0), :], stacked(g_buf, slot, group), 1, 1)

    key_at = lax.broadcasted_iota(jnp.int32, (tok, tok), 0)
    row_at = lax.broadcasted_iota(jnp.int32, (tok, tok), 1)
    is_own = key_at <= row_at

    def key_segments(step):
        return jnp.broadcast_to(seg_buf[step].astype(jnp.float32), (tok, tok)).T

    def fill_bias():
        last = shards - 1
        row_seg = seg_buf[0].astype(jnp.float32)
        edge = jnp.where(is_own, key_segments(0), key_segments(last))
        bias[last * tok :, :] = jnp.where(edge == row_seg, 0.0, -1e30)
        for step in range(1, last):
            bias[block(step), :] = jnp.where(key_segments(step) == row_seg, 0.0, -1e30)

    inner = slice(tok, None)

    def store_tiles(target, group, cols, value):
        edge = value[-tok:]
        target[group, inner, cols] = jnp.concatenate(
            [value[:-tok], jnp.where(is_own, edge, 0.0)], 0
        ).astype(jnp.bfloat16)
        target[group, :tok, cols] = jnp.where(is_own, 0.0, edge).astype(jnp.bfloat16)

    def probabilities(group):
        for start in range(0, 2 * rows, tok):
            cols = slice(start, start + tok)
            edge = jnp.where(is_own, s_own[group, :, cols], s_buf[group, :tok, cols])
            scores = jnp.concatenate([s_buf[group, inner, cols], edge], 0)
            scores = scores * (scale * LOG2E) + bias[inner, :]
            exps = jnp.exp2(scores - jnp.max(scores, 0, keepdims=True))
            probs = exps * (1.0 / jnp.sum(exps, 0, keepdims=True))
            s_buf[group, :, cols] = probs
            store_tiles(p_buf, group, cols, probs)

    def score_grads(group):
        for start in range(0, 2 * rows, tok):
            cols = slice(start, start + tok)
            edge = jnp.where(is_own, gp_own[group, :, cols], gp_buf[group, :tok, cols])
            grad_probs = jnp.concatenate([gp_buf[group, inner, cols], edge], 0)
            probs = s_buf[group, :, cols]
            row_dot = jnp.sum(probs * grad_probs, 0, keepdims=True)
            store_tiles(ds_buf, group, cols, probs * (grad_probs - row_dot))

    def key_grads(at, group):
        return dot(ds_buf[group, at, :], all_rows(q_buf, group), 1, 0) * scale

    def value_grads(at, group):
        return dot(p_buf[group, at, :], all_rows(g_buf, group), 1, 0)

    def query_grads(group, slot):
        flipped = dot(k_buf[group], ds_buf[group, :, slot * rows : (slot + 1) * rows], 0, 0)
        for head in range(ratio):
            grad_query = flipped[:, head * tok : (head + 1) * tok].T * scale
            grad_query = grad_query.astype(jnp.bfloat16)
            if slot == 0:
                start = (core * groups + group) * share + head * DH
                dq_ref[0, :, pl.ds(pl.multiple_of(start, DH), DH)] = grad_query
            else:
                dq_buf[group, :, head_cols(head)] = grad_query

    def part_copy(step, group, which):
        return pltpu.make_async_remote_copy(
            src_ref=part.at[group, step - 1, which],
            dst_ref=got.at[group, step - 1, which],
            send_sem=part_send.at[group, step - 1, which],
            recv_sem=part_recv.at[group, step - 1, which],
            device_id={"ctx": me - step},
            device_id_type=MESH,
        )

    parts = [
        {step: [part_copy(step, group, which) for which in range(2)] for step in steps}
        for group in range(groups)
    ]

    def send_part(group, which, grad):
        for step in steps:
            part[group, step - 1, which] = grad[block(step)].astype(jnp.bfloat16)
        for step in reversed(steps):

            @pl.when(me >= step)
            def _(step=step):
                parts[group][step][which].start()

    def near_arrived(group, which):
        for step in steps:

            @pl.when(me >= step)
            def _(step=step):
                if group == 0 and which == 0:
                    near_seg[step].wait_recv()
                near[step][group][which].wait_recv()

    query_send = [
        pair_copy(dq_buf.at[group], dq_ref.at[0, :, query_cols(core, group)], group, 2)
        for group in range(groups)
    ]
    own_seg.wait()
    for group in range(groups):
        for copy in own[group]:
            copy.wait()
        own_products(0, group)
    for group in range(groups):
        for copy in pair[group]:
            copy.wait_recv()
        own_products(1, group)
    far = slice(0, DOC_SHARDS * tok)
    for group in range(groups):
        near_arrived(group, 0)
        if group == 0:
            fill_bias()
        s_buf[group] = dot(k_buf[group, far, :], all_rows(q_buf, group), 1, 1)
        probabilities(group)
        send_part(group, 1, value_grads(far, group))
        near_arrived(group, 1)
        gp_buf[group] = dot(v_buf[group, far, :], all_rows(g_buf, group), 1, 1)
        score_grads(group)
        send_part(group, 0, key_grads(far, group))
    for group in range(groups):
        query_grads(group, 1)
        query_send[group].start()
    for group in range(groups):
        query_grads(group, 0)
        dk_ref[:, head_cols(group)] = key_grads(block(0), group)
        dv_ref[:, head_cols(group)] = value_grads(block(0), group)
    for group in range(groups):
        for which, target in ((1, dv_ref), (0, dk_ref)):
            for step in steps:

                @pl.when(me + step < cycle_size)
                def _(step=step, group=group, which=which, target=target):
                    parts[group][step][which].wait_recv()
                    more = got[group, step - 1, which].astype(jnp.float32)
                    target[:, head_cols(group)] += more

    for group in range(groups):
        query_send[group].wait()
        for copy in pair[group]:
            copy.wait_send()
        for step in steps:

            @pl.when(me >= step)
            def _(step=step, group=group):
                for copy in parts[group][step]:
                    copy.wait_send()

    for group in range(groups):
        near_sent(group)


def hand_over(dq_in, dk_in, dv_in, dq_out, dk_out, dv_out, sem):
    piece = dq_in.shape[1] // PIECES
    cuts = [pl.ds(i * piece, piece) for i in range(PIECES)]
    pairs = [(dq_in.at[:, cut], dq_out.at[:, cut]) for cut in cuts]
    pairs += [(dk_in, dk_out), (dv_in, dv_out)]
    copies = [pltpu.make_async_copy(*pair, sem.at[i]) for i, pair in enumerate(pairs)]
    for copy in copies:
        copy.start()
    for copy in copies:
        copy.wait()


def by_heads(cycle_size, queries, keys, values, cotangent, segment_ids):
    tok = keys.shape[0]
    half = queries.shape[2] // 2
    width = keys.shape[1] // 2
    groups = width // DH
    rows = half // groups
    rows = rows // DH * tok
    window = (DOC_SHARDS + 1) * tok
    bf16, f32 = jnp.bfloat16, jnp.float32
    anywhere = pl.BlockSpec(memory_space=pl.ANY)
    in_hbm = pl.BlockSpec(memory_space=pltpu.HBM)
    in_vmem = pl.BlockSpec(memory_space=pltpu.VMEM)
    dma = pltpu.SemaphoreType.DMA
    shapes = (
        jax.ShapeDtypeStruct(queries.shape, bf16),
        jax.ShapeDtypeStruct((tok, width), f32),
        jax.ShapeDtypeStruct((tok, width), f32),
    )
    grads = pl.pallas_call(
        functools.partial(kernel, cycle_size),
        out_shape=tuple(pltpu.VMEM(shape.shape, shape.dtype) for shape in shapes),
        in_specs=[in_hbm] * 5,
        out_specs=(in_vmem,) * 3,
        scratch_shapes=[
            pltpu.VMEM((2, groups, tok, half // groups), bf16),
            pltpu.VMEM((2, groups, tok, half // groups), bf16),
            pltpu.VMEM((groups, window, DH), bf16),
            pltpu.VMEM((groups, window, DH), bf16),
            pltpu.VMEM((DOC_SHARDS + 1, 1, tok), jnp.int32),
            pltpu.VMEM((window, tok), f32),
            pltpu.VMEM((groups, tok, 2 * rows), f32),
            pltpu.VMEM((groups, tok, 2 * rows), f32),
            pltpu.VMEM((groups, window - tok, 2 * rows), f32),
            pltpu.VMEM((groups, window - tok, 2 * rows), f32),
            pltpu.VMEM((groups, window, 2 * rows), bf16),
            pltpu.VMEM((groups, window, 2 * rows), bf16),
            pltpu.VMEM((groups, tok, half // groups), bf16),
            pltpu.VMEM((groups, DOC_SHARDS, 2, tok, DH), bf16),
            pltpu.VMEM((groups, DOC_SHARDS, 2, tok, DH), bf16),
            dma((groups + 1, 5)),
            dma((groups, 3)),
            dma((groups, 3)),
            dma((DOC_SHARDS,)),
            dma((DOC_SHARDS,)),
            dma((DOC_SHARDS, groups, 2)),
            dma((DOC_SHARDS, groups, 2)),
            dma((groups, DOC_SHARDS, 2)),
            dma((groups, DOC_SHARDS, 2)),
        ],
        compiler_params=pltpu.CompilerParams(
            collective_id=0, has_side_effects=True, vmem_limit_bytes=VMEM_BYTES
        ),
    )(queries, keys, values, cotangent, segment_ids.reshape(1, tok))
    return pl.pallas_call(
        hand_over,
        out_shape=shapes,
        in_specs=[in_vmem] * 3,
        out_specs=(in_hbm,) * 3,
        scratch_shapes=[dma((PIECES + 2,))],
        compiler_params=pltpu.CompilerParams(vmem_limit_bytes=8 << 20),
    )(*grads)


def solution(mesh):
    placed = (
        P("section", "ctx", None),
        P("ctx", None),
        P("ctx", None),
        P("section", "ctx", None),
        P("ctx"),
    )
    cycle_size = mesh.shape["ctx"]
    pairs = mesh.shape["section"] == 2

    def step(queries, keys, values, cotangent, segment_ids):
        tok, width = keys.shape
        halves = pairs and queries.shape[0] == 1 and tok % DH == 0 and width % (2 * DH) == 0
        if halves:
            return by_heads(cycle_size, queries, keys, values, cotangent, segment_ids)
        return on_device(queries, keys, values, cotangent, segment_ids)

    return jax.shard_map(
        step,
        mesh=mesh,
        in_specs=placed,
        out_specs=(P("section", "ctx", None), P("ctx", "section"), P("ctx", "section")),
        check_vma=False,
    )
```

```python
import functools

import jax
import jax.numpy as jnp
from jax import lax
from jax.experimental import pallas as pl
from jax.experimental.pallas import tpu as pltpu
from jax.sharding import PartitionSpec as P

DH = 128
DOC_SHARDS = 2
LOG2E = 1.4426950408889634
MESH = pl.DeviceIdType.MESH
VMEM_BYTES = 63 << 20
PIECES = 4


def shifted(shard, axis, by):
    size = lax.axis_size(axis)
    pairs = [(i, i + by) for i in range(size) if 0 <= i + by < size]
    return lax.ppermute(shard, axis, pairs)


def as_sent(shard):

    def short(part):
        return part.astype(jnp.bfloat16) if part.dtype == jnp.float32 else part

    return jax.tree.map(short, shard)


def by_group(rows, groups):
    count, width = rows.shape
    head_ratio = width // (groups * DH)
    return (
        rows.reshape(count, groups, head_ratio, DH)
        .transpose(1, 2, 0, 3)
        .reshape(groups, head_ratio * count, DH)
    )


def add_pair(first, second):
    return (first[0] + second[0], first[1] + second[1])


def on_device(queries, keys, values, cotangent, segment_ids):
    tok_rows = keys.shape[0]
    groups = keys.shape[1] // DH
    heads = queries.shape[2] // DH
    head_ratio = heads // groups
    score_scale = DH ** (-0.5)
    cycle_size = lax.axis_size("ctx")
    my_index = lax.axis_index("ctx")
    query_rows = by_group(queries[0], groups)
    grad_rows = by_group(cotangent[0], groups)
    row_pos = my_index * tok_rows + jnp.tile(jnp.arange(tok_rows, dtype=jnp.int32), head_ratio)
    row_seg = jnp.tile(segment_ids, head_ratio)
    blocks = []
    current = (keys, values, segment_ids)
    for shard_step in range(DOC_SHARDS + 1):
        if shard_step > 0:
            current = shifted((current[0], current[1], current[2]), "ctx", 1)
        key_block, value_block, key_seg = current
        key_rows = key_block.reshape(tok_rows, groups, DH).transpose(1, 0, 2)
        value_rows = value_block.reshape(tok_rows, groups, DH).transpose(1, 0, 2)
        key_pos = (my_index - shard_step) % cycle_size * tok_rows + jnp.arange(
            tok_rows, dtype=jnp.int32
        )
        allowed = (row_seg[:, None] == key_seg[None, :]) & (key_pos[None, :] <= row_pos[:, None])
        if shard_step == 0:
            is_live = jnp.array(True)
        else:
            is_live = (my_index >= shard_step) & (key_seg[-1] >= segment_ids[0])
        blocks.append((key_rows, value_rows, allowed, is_live))
    row_count = head_ratio * tok_rows
    row_max = jnp.full((groups, row_count, 1), -1e30, jnp.float32)
    row_sum = jnp.zeros((groups, row_count, 1), jnp.float32)
    kept_scores = []
    for key_rows, value_rows, allowed, is_live in blocks:

        def running_stats(key_rows=key_rows, allowed=allowed, row_max=row_max, row_sum=row_sum):
            scores = (
                jnp.einsum("grd,gkd->grk", query_rows, key_rows, preferred_element_type=jnp.float32)
                * score_scale
            )
            block_max = jnp.max(jnp.where(allowed, scores, -1e30), -1, keepdims=True)
            new_max = jnp.maximum(row_max, block_max)
            added = jnp.sum(jnp.where(allowed, jnp.exp(scores - new_max), 0.0), -1, keepdims=True)
            return (new_max, row_sum * jnp.exp(row_max - new_max) + added, scores)

        row_max, row_sum, scores = running_stats()
        kept_scores.append(scores)
    log_total = row_max + jnp.log(row_sum)

    def block_probs(scores, allowed):
        return jnp.where(allowed, jnp.exp(scores - log_total), 0.0)

    output_rows = jnp.zeros((groups, row_count, DH), jnp.float32)
    for (key_rows, value_rows, allowed, is_live), scores in zip(blocks, kept_scores):

        def output_part(scores=scores, value_rows=value_rows, allowed=allowed):
            probs_low = block_probs(scores, allowed).astype(jnp.bfloat16)
            return jnp.einsum(
                "grk,gkd->grd", probs_low, value_rows, preferred_element_type=jnp.float32
            )

        output_rows = output_rows + output_part()
    row_dot = jnp.sum(grad_rows.astype(jnp.float32) * output_rows, -1, keepdims=True)
    grad_query = jnp.zeros((groups, row_count, DH), jnp.float32)
    partials = []
    for (key_rows, value_rows, allowed, is_live), scores in zip(blocks, kept_scores):

        def backward_part(scores=scores, key_rows=key_rows, value_rows=value_rows, allowed=allowed):
            probs = block_probs(scores, allowed)
            probs_low = probs.astype(jnp.bfloat16)
            grad_probs = jnp.einsum(
                "grd,gkd->grk", grad_rows, value_rows, preferred_element_type=jnp.float32
            )
            scaled_low = (probs * (grad_probs - row_dot) * score_scale).astype(jnp.bfloat16)
            query_part = jnp.einsum(
                "grk,gkd->grd", scaled_low, key_rows, preferred_element_type=jnp.float32
            )
            key_part = jnp.einsum(
                "grk,grd->gkd", scaled_low, query_rows, preferred_element_type=jnp.float32
            )
            value_part = jnp.einsum(
                "grk,grd->gkd", probs_low, grad_rows, preferred_element_type=jnp.float32
            )
            key_flat = key_part.transpose(1, 0, 2).reshape(tok_rows, groups * DH)
            value_flat = value_part.transpose(1, 0, 2).reshape(tok_rows, groups * DH)
            return (query_part, key_flat, value_flat)

        query_part, key_flat, value_flat = backward_part()
        grad_query = grad_query + query_part
        partials.append((key_flat, value_flat))
    summed = partials[0]
    for shard_step in range(1, DOC_SHARDS + 1):
        arrived = shifted(as_sent(partials[shard_step]), "ctx", -shard_step)
        summed = add_pair(summed, arrived)
    summed = lax.psum_scatter(summed, "section", scatter_dimension=1, tiled=True)
    query_out = (
        grad_query.reshape(groups, head_ratio, tok_rows, DH)
        .transpose(2, 0, 1, 3)
        .reshape(1, tok_rows, heads * DH)
    )
    return (query_out.astype(jnp.bfloat16), summed[0], summed[1])


def dot(first, second, first_dim, second_dim):
    return lax.dot_general(
        first,
        second,
        (((first_dim,), (second_dim,)), ((), ())),
        preferred_element_type=jnp.float32,
    )


def kernel(
    cycle_size,
    q_hbm,
    k_hbm,
    v_hbm,
    g_hbm,
    seg_hbm,
    dq_ref,
    dk_ref,
    dv_ref,
    q_buf,
    g_buf,
    k_buf,
    v_buf,
    seg_buf,
    bias,
    s_own,
    gp_own,
    s_buf,
    gp_buf,
    p_buf,
    ds_buf,
    dq_buf,
    part,
    got,
    local_sem,
    pair_send,
    pair_recv,
    seg_send,
    seg_recv,
    near_send,
    near_recv,
    part_send,
    part_recv,
):
    tok = k_hbm.shape[0]
    groups = k_buf.shape[0]
    share = q_buf.shape[3]
    ratio = share // DH
    rows = ratio * tok
    shards = DOC_SHARDS + 1
    scale = DH ** (-0.5)
    me = lax.axis_index("ctx")
    core = lax.axis_index("section")
    other = 1 - core
    steps = range(1, shards)

    def query_cols(owner, group):
        return pl.ds(pl.multiple_of((owner * groups + group) * share, DH), share)

    def key_cols(group):
        return pl.ds(pl.multiple_of((core * groups + group) * DH, DH), DH)

    def block(step):
        return slice((shards - 1 - step) * tok, (shards - step) * tok)

    def block_ds(step):
        return pl.ds((shards - 1 - step) * tok, tok)

    barrier = pltpu.get_barrier_semaphore()
    pl.semaphore_signal(barrier, inc=1, device_id={"section": other}, device_id_type=MESH)
    greeted = 1
    for step in steps:
        has_next = me + step < cycle_size
        has_prev = me >= step

        @pl.when(has_next)
        def _(step=step):
            pl.semaphore_signal(barrier, inc=1, device_id={"ctx": me + step}, device_id_type=MESH)

        @pl.when(has_prev)
        def _(step=step):
            pl.semaphore_signal(barrier, inc=1, device_id={"ctx": me - step}, device_id_type=MESH)

        greeted = greeted + has_next.astype(jnp.int32) + has_prev.astype(jnp.int32)

    def own_copies(group):
        pairs = (
            (k_hbm.at[:, key_cols(group)], k_buf.at[group, block_ds(0), :]),
            (q_hbm.at[0, :, query_cols(core, group)], q_buf.at[0, group]),
            (v_hbm.at[:, key_cols(group)], v_buf.at[group, block_ds(0), :]),
            (g_hbm.at[0, :, query_cols(core, group)], g_buf.at[0, group]),
        )
        return [
            pltpu.make_async_copy(source, target, local_sem.at[group, i])
            for i, (source, target) in enumerate(pairs)
        ]

    own = [own_copies(group) for group in range(groups)]
    own_seg = pltpu.make_async_copy(seg_hbm, seg_buf.at[0], local_sem.at[groups, 0])
    own_seg.start()
    for copies in own:
        for copy in copies:
            copy.start()
    for step in steps:

        @pl.when(me < step)
        def _(step=step):
            for group in range(groups):
                k_buf[group, block(step), :] = jnp.zeros((tok, DH), jnp.bfloat16)
                v_buf[group, block(step), :] = jnp.zeros((tok, DH), jnp.bfloat16)
            seg_buf[step] = jnp.full((1, tok), -1, jnp.int32)

    pl.semaphore_wait(barrier, greeted)

    def to_next(source, target, step, send, recv):
        return pltpu.make_async_remote_copy(
            src_ref=source,
            dst_ref=target,
            send_sem=send,
            recv_sem=recv,
            device_id={"ctx": me + step},
            device_id_type=MESH,
        )

    def near_copies(step, group):
        at = step - 1
        pairs = (
            (k_hbm.at[:, key_cols(group)], k_buf.at[group, block_ds(step), :]),
            (v_hbm.at[:, key_cols(group)], v_buf.at[group, block_ds(step), :]),
        )
        return [
            to_next(source, target, step, near_send.at[at, group, i], near_recv.at[at, group, i])
            for i, (source, target) in enumerate(pairs)
        ]

    near = {step: [near_copies(step, group) for group in range(groups)] for step in steps}
    near_seg = {
        step: to_next(
            seg_hbm, seg_buf.at[step], step, seg_send.at[step - 1], seg_recv.at[step - 1]
        )
        for step in steps
    }

    def pair_copy(source, target, group, at):
        return pltpu.make_async_remote_copy(
            src_ref=source,
            dst_ref=target,
            send_sem=pair_send.at[group, at],
            recv_sem=pair_recv.at[group, at],
            device_id={"section": other},
            device_id_type=MESH,
        )

    pair = [
        [
            pair_copy(q_hbm.at[0, :, query_cols(other, group)], q_buf.at[1, group], group, 0),
            pair_copy(g_hbm.at[0, :, query_cols(other, group)], g_buf.at[1, group], group, 1),
        ]
        for group in range(groups)
    ]
    def send_near(group):
        for which in range(2):
            for step in reversed(steps):

                @pl.when(me + step < cycle_size)
                def _(step=step, which=which):
                    if group == 0 and which == 0:
                        near_seg[step].start()
                    near[step][group][which].start()

    def near_sent(group):
        for step in steps:

            @pl.when(me + step < cycle_size)
            def _(step=step):
                if group == 0:
                    near_seg[step].wait_send()
                for copy in near[step][group]:
                    copy.wait_send()

    for group in range(groups):
        send_near(group)
        for copy in pair[group]:
            copy.start()

    def head_cols(head):
        return slice(head * DH, (head + 1) * DH)

    def stacked(buf, slot, group):
        return jnp.concatenate([buf[slot, group, :, head_cols(h)] for h in range(ratio)], 0)

    def all_rows(buf, group):
        return jnp.concatenate([stacked(buf, 0, group), stacked(buf, 1, group)], 0)

    def own_products(slot, group):
        at = slice(slot * rows, (slot + 1) * rows)
        s_own[group, :, at] = dot(k_buf[group, block(0), :], stacked(q_buf, slot, group), 1, 1)
        gp_own[group, :, at] = dot(v_buf[group, block(0), :], stacked(g_buf, slot, group), 1, 1)

    key_at = lax.broadcasted_iota(jnp.int32, (tok, tok), 0)
    row_at = lax.broadcasted_iota(jnp.int32, (tok, tok), 1)
    is_own = key_at <= row_at

    def key_segments(step):
        return jnp.broadcast_to(seg_buf[step].astype(jnp.float32), (tok, tok)).T

    def fill_bias():
        last = shards - 1
        row_seg = seg_buf[0].astype(jnp.float32)
        edge = jnp.where(is_own, key_segments(0), key_segments(last))
        bias[last * tok :, :] = jnp.where(edge == row_seg, 0.0, -1e30)
        for step in range(1, last):
            bias[block(step), :] = jnp.where(key_segments(step) == row_seg, 0.0, -1e30)

    inner = slice(tok, None)

    def store_tiles(target, group, cols, value):
        edge = value[-tok:]
        target[group, inner, cols] = jnp.concatenate(
            [value[:-tok], jnp.where(is_own, edge, 0.0)], 0
        ).astype(jnp.bfloat16)
        target[group, :tok, cols] = jnp.where(is_own, 0.0, edge).astype(jnp.bfloat16)

    def probabilities(group):
        for start in range(0, 2 * rows, tok):
            cols = slice(start, start + tok)
            edge = jnp.where(is_own, s_own[group, :, cols], s_buf[group, :tok, cols])
            scores = jnp.concatenate([s_buf[group, inner, cols], edge], 0)
            scores = scores * (scale * LOG2E) + bias[inner, :]
            exps = jnp.exp2(scores - jnp.max(scores, 0, keepdims=True))
            probs = exps * (1.0 / jnp.sum(exps, 0, keepdims=True))
            s_buf[group, :, cols] = probs
            store_tiles(p_buf, group, cols, probs)

    def score_grads(group):
        for start in range(0, 2 * rows, tok):
            cols = slice(start, start + tok)
            edge = jnp.where(is_own, gp_own[group, :, cols], gp_buf[group, :tok, cols])
            grad_probs = jnp.concatenate([gp_buf[group, inner, cols], edge], 0)
            probs = s_buf[group, :, cols]
            row_dot = jnp.sum(probs * grad_probs, 0, keepdims=True)
            store_tiles(ds_buf, group, cols, probs * (grad_probs - row_dot))

    def key_grads(at, group):
        return dot(ds_buf[group, at, :], all_rows(q_buf, group), 1, 0) * scale

    def value_grads(at, group):
        return dot(p_buf[group, at, :], all_rows(g_buf, group), 1, 0)

    def query_grads(group, slot):
        flipped = dot(k_buf[group], ds_buf[group, :, slot * rows : (slot + 1) * rows], 0, 0)
        for head in range(ratio):
            grad_query = flipped[:, head * tok : (head + 1) * tok].T * scale
            grad_query = grad_query.astype(jnp.bfloat16)
            if slot == 0:
                start = (core * groups + group) * share + head * DH
                dq_ref[0, :, pl.ds(pl.multiple_of(start, DH), DH)] = grad_query
            else:
                dq_buf[group, :, head_cols(head)] = grad_query

    def part_copy(step, group, which):
        return pltpu.make_async_remote_copy(
            src_ref=part.at[group, step - 1, which],
            dst_ref=got.at[group, step - 1, which],
            send_sem=part_send.at[group, step - 1, which],
            recv_sem=part_recv.at[group, step - 1, which],
            device_id={"ctx": me - step},
            device_id_type=MESH,
        )

    parts = [
        {step: [part_copy(step, group, which) for which in range(2)] for step in steps}
        for group in range(groups)
    ]

    def send_part(group, which, grad):
        for step in steps:
            part[group, step - 1, which] = grad[block(step)].astype(jnp.bfloat16)
        for step in reversed(steps):

            @pl.when(me >= step)
            def _(step=step):
                parts[group][step][which].start()

    def near_arrived(group, which):
        for step in steps:

            @pl.when(me >= step)
            def _(step=step):
                near[step][group][which].wait_recv()

    query_send = [
        pair_copy(dq_buf.at[group], dq_ref.at[0, :, query_cols(core, group)], group, 2)
        for group in range(groups)
    ]
    own_seg.wait()
    for group in range(groups):
        for copy in own[group]:
            copy.wait()
        own_products(0, group)
    for group in range(groups):
        for copy in pair[group]:
            copy.wait_recv()
        own_products(1, group)
    far = slice(0, DOC_SHARDS * tok)
    for step in steps:

        @pl.when(me >= step)
        def _(step=step):
            near_seg[step].wait_recv()

    fill_bias()
    for group in range(groups):
        near_arrived(group, 0)
        s_buf[group] = dot(k_buf[group, far, :], all_rows(q_buf, group), 1, 1)
        probabilities(group)
        send_part(group, 1, value_grads(far, group))
        near_arrived(group, 1)
        gp_buf[group] = dot(v_buf[group, far, :], all_rows(g_buf, group), 1, 1)
        score_grads(group)
        send_part(group, 0, key_grads(far, group))
    for group in range(groups):
        query_grads(group, 1)
        query_send[group].start()
    for group in range(groups):
        query_grads(group, 0)
        dk_ref[:, head_cols(group)] = key_grads(block(0), group)
        dv_ref[:, head_cols(group)] = value_grads(block(0), group)
    for group in range(groups):
        for which, target in ((1, dv_ref), (0, dk_ref)):
            for step in steps:

                @pl.when(me + step < cycle_size)
                def _(step=step, group=group, which=which, target=target):
                    parts[group][step][which].wait_recv()
                    more = got[group, step - 1, which].astype(jnp.float32)
                    target[:, head_cols(group)] += more

    for group in range(groups):
        query_send[group].wait()
        for copy in pair[group]:
            copy.wait_send()
        for step in steps:

            @pl.when(me >= step)
            def _(step=step, group=group):
                for copy in parts[group][step]:
                    copy.wait_send()

    for group in range(groups):
        near_sent(group)


def hand_over(dq_in, dk_in, dv_in, dq_out, dk_out, dv_out, sem):
    piece = dq_in.shape[1] // PIECES
    cuts = [pl.ds(i * piece, piece) for i in range(PIECES)]
    pairs = [(dq_in.at[:, cut], dq_out.at[:, cut]) for cut in cuts]
    pairs += [(dk_in, dk_out), (dv_in, dv_out)]
    copies = [pltpu.make_async_copy(*pair, sem.at[i]) for i, pair in enumerate(pairs)]
    for copy in copies:
        copy.start()
    for copy in copies:
        copy.wait()


def by_heads(cycle_size, queries, keys, values, cotangent, segment_ids):
    tok = keys.shape[0]
    half = queries.shape[2] // 2
    width = keys.shape[1] // 2
    groups = width // DH
    rows = half // groups
    rows = rows // DH * tok
    window = (DOC_SHARDS + 1) * tok
    bf16, f32 = jnp.bfloat16, jnp.float32
    anywhere = pl.BlockSpec(memory_space=pl.ANY)
    in_hbm = pl.BlockSpec(memory_space=pltpu.HBM)
    in_vmem = pl.BlockSpec(memory_space=pltpu.VMEM)
    dma = pltpu.SemaphoreType.DMA
    shapes = (
        jax.ShapeDtypeStruct(queries.shape, bf16),
        jax.ShapeDtypeStruct((tok, width), f32),
        jax.ShapeDtypeStruct((tok, width), f32),
    )
    grads = pl.pallas_call(
        functools.partial(kernel, cycle_size),
        out_shape=tuple(pltpu.VMEM(shape.shape, shape.dtype) for shape in shapes),
        in_specs=[in_hbm] * 5,
        out_specs=(in_vmem,) * 3,
        scratch_shapes=[
            pltpu.VMEM((2, groups, tok, half // groups), bf16),
            pltpu.VMEM((2, groups, tok, half // groups), bf16),
            pltpu.VMEM((groups, window, DH), bf16),
            pltpu.VMEM((groups, window, DH), bf16),
            pltpu.VMEM((DOC_SHARDS + 1, 1, tok), jnp.int32),
            pltpu.VMEM((window, tok), f32),
            pltpu.VMEM((groups, tok, 2 * rows), f32),
            pltpu.VMEM((groups, tok, 2 * rows), f32),
            pltpu.VMEM((groups, window - tok, 2 * rows), f32),
            pltpu.VMEM((groups, window - tok, 2 * rows), f32),
            pltpu.VMEM((groups, window, 2 * rows), bf16),
            pltpu.VMEM((groups, window, 2 * rows), bf16),
            pltpu.VMEM((groups, tok, half // groups), bf16),
            pltpu.VMEM((groups, DOC_SHARDS, 2, tok, DH), bf16),
            pltpu.VMEM((groups, DOC_SHARDS, 2, tok, DH), bf16),
            dma((groups + 1, 5)),
            dma((groups, 3)),
            dma((groups, 3)),
            dma((DOC_SHARDS,)),
            dma((DOC_SHARDS,)),
            dma((DOC_SHARDS, groups, 2)),
            dma((DOC_SHARDS, groups, 2)),
            dma((groups, DOC_SHARDS, 2)),
            dma((groups, DOC_SHARDS, 2)),
        ],
        compiler_params=pltpu.CompilerParams(
            collective_id=0, has_side_effects=True, vmem_limit_bytes=VMEM_BYTES
        ),
    )(queries, keys, values, cotangent, segment_ids.reshape(1, tok))
    return pl.pallas_call(
        hand_over,
        out_shape=shapes,
        in_specs=[in_vmem] * 3,
        out_specs=(in_hbm,) * 3,
        scratch_shapes=[dma((PIECES + 2,))],
        compiler_params=pltpu.CompilerParams(vmem_limit_bytes=8 << 20),
    )(*grads)


def solution(mesh):
    placed = (
        P("section", "ctx", None),
        P("ctx", None),
        P("ctx", None),
        P("section", "ctx", None),
        P("ctx"),
    )
    cycle_size = mesh.shape["ctx"]
    pairs = mesh.shape["section"] == 2

    def step(queries, keys, values, cotangent, segment_ids):
        tok, width = keys.shape
        halves = pairs and queries.shape[0] == 1 and tok % DH == 0 and width % (2 * DH) == 0
        if halves:
            return by_heads(cycle_size, queries, keys, values, cotangent, segment_ids)
        return on_device(queries, keys, values, cotangent, segment_ids)

    return jax.shard_map(
        step,
        mesh=mesh,
        in_specs=placed,
        out_specs=(P("section", "ctx", None), P("ctx", "section"), P("ctx", "section")),
        check_vma=False,
    )
```
